512 devices in a mesh: face: 8 (over z_lo, core), tile: 64 (over x, z_hi, y).
Axes of the slice: x: 4, y: 8, z: 8 (z_hi: 2, z_lo: 4; z = z_hi * 4 + z_lo), core: 2. Of those that a mesh axis runs over, the one named last changes fastest.
Arguments:
- state_field: float32 [8, 64, 16, 16, 256], P('face', 'tile'), may hold values from -6 to 6
- out_grad: float32 [8, 64, 16, 16, 256], P('face', 'tile'), may hold values from -6 to 6
- depth_kernel: float32 [9, 256], P(None, 'tile'), may hold values from -2 to 2
- norm_gain: float32 [256], P('tile'), may hold values from 0.5 to 1.5
- up_weight: float32 [256, 1024], P('tile'), may hold values from -0.375 to 0.375
- down_weight: float32 [1024, 256], P('tile'), may hold values from -0.1875 to 0.1875
- seam_code: int32 [8, 64, 4], P('face', 'tile'), may hold values from 0 to 1, as said below
Outputs:
- new_field: float32 [8, 64, 16, 16, 256], P('face', 'tile')
- field_grad: float32 [8, 64, 16, 16, 256], P('face', 'tile')
- kernel_grad: float32 [9, 256], P(None, 'tile')
- gain_grad: float32 [256], P('tile')
- up_grad: float32 [256, 1024], P('tile')
- down_grad: float32 [1024, 256], P('tile')
The draws below stay inside these ranges and needn't reach their ends.
Inputs may be any that keep to these rules, and one draw needn't show every extreme that they name: `seam_code`: 1 where the strip across a seam runs in reverse order; the same value on both sides of a seam; 0 on edges that do not lie on the face border.
All inputs are finite; a program needn't handle non-finite values.
Results may differ from the reference program's by a relative error of at most 0.00027.
Values sent between devices are 32-bit elements; how exact they have to be, the bound alone decides.
A program may use at most 64 MiB of HBM per device.

```python
import math
import jax
import jax.numpy as jnp
from jax import lax

CH = 256
HID = 1024
CELL = 16
FACES = 8
TILES = 64
N_FACE = 8
N_TILE = 64


def draw_seam_code(key, part):
    key = jax.random.fold_in(key, 5)
    face_count = N_FACE
    tile_count = N_TILE
    grid_side = math.isqrt(N_TILE)
    face_ids = jnp.arange(face_count, dtype=jnp.int32)
    north_face = (face_ids + face_count // 2) % face_count
    south_face = face_count - 1 - face_ids
    west_face = jnp.where(face_ids % 2 == 0, (face_ids - 1) % face_count, (face_ids + 1) % face_count)
    east_face = face_ids ^ 1
    across = jnp.stack([north_face, south_face, west_face, east_face], axis=1).astype(jnp.int32)
    tile_ids = jnp.arange(tile_count, dtype=jnp.int32)
    tile_row = tile_ids // grid_side
    tile_col = tile_ids % grid_side
    border = jnp.stack([tile_row == 0, tile_row == grid_side - 1, tile_col == 0, tile_col == grid_side - 1], axis=1)
    coin_flips = jax.random.randint(key, (face_count, tile_count, 4), 0, 2, dtype=jnp.int32)
    lower_face = jnp.broadcast_to(jnp.minimum(face_ids[:, None], across)[:, None, :], (face_count, tile_count, 4))
    edge_ids = jnp.arange(4, dtype=jnp.int32)
    edge_codes = coin_flips[lower_face, tile_ids[None, :, None], edge_ids[None, None, :]]
    return jnp.where(border[None, :, :], edge_codes, 0).astype(jnp.int32)


def block_scale(rng, extent, shards, least, top_value):
    level, own = 1.0, jax.random.fold_in(rng, 6)
    for dim, parts in shards:
        heights = jnp.exp(jax.random.uniform(jax.random.fold_in(own, dim), (parts,), jnp.float32, least / len(shards), top_value / len(shards)))
        level = level * jnp.repeat(heights, extent[dim] // parts).reshape([-1 if axis == dim else 1 for axis in range(len(extent))])
    return level


def noise(own_key, dims, width, reach, pieces=(), kind=jnp.bfloat16):
    entries = width * jax.random.normal(own_key, dims, jnp.float32)
    if pieces:
        entries = entries * block_scale(own_key, dims, pieces, -0.22, 0.18)
    return jnp.clip(entries, -reach, reach).astype(kind)


def setup_inputs(seed: int = 0) -> dict:
    seeds = jax.random.split(jax.random.key(seed), 8)
    state_field = noise(seeds[0], (FACES, TILES, CELL, CELL, CH), 1.0, 6.0, ((0, 8), (1, 64)), jnp.float32)
    out_grad = noise(seeds[1], (FACES, TILES, CELL, CELL, CH), 1.0, 6.0, ((0, 8), (1, 64)), jnp.float32)
    depth_kernel = noise(seeds[2], (9, CH), 9 ** -0.5, 2.0, ((1, 64),), jnp.float32)
    norm_gain = jnp.clip(1.0 + 0.1 * jax.random.normal(seeds[3], (CH,), jnp.float32), 0.5, 1.5)
    up_weight = noise(seeds[4], (CH, HID), CH ** -0.5, 0.375, ((0, 64),), jnp.float32)
    down_weight = noise(seeds[5], (HID, CH), HID ** -0.5, 0.1875, ((0, 64),), jnp.float32)
    seam_code = draw_seam_code(jax.random.fold_in(seeds[7], 71), 0)
    return {"state_field": state_field, "out_grad": out_grad, "depth_kernel": depth_kernel, "norm_gain": norm_gain, "up_weight": up_weight, "down_weight": down_weight, "seam_code": seam_code}


EPSILON = 1e-06
PRECISE = lax.Precision.HIGHEST

def face_partners(face_count):
    face_ids = jnp.arange(face_count, dtype=jnp.int32)
    north_face = (face_ids + face_count // 2) % face_count
    south_face = face_count - 1 - face_ids
    west_face = jnp.where(face_ids % 2 == 0, (face_ids - 1) % face_count, (face_ids + 1) % face_count)
    east_face = face_ids ^ 1
    return jnp.stack([north_face, south_face, west_face, east_face], axis=1).astype(jnp.int32)

def convnext_block(padded, kernel, gain_full, up_full, down_full):
    size_cells = padded.shape[-2] - 2
    depthwise = jnp.zeros_like(padded[..., 1:-1, 1:-1, :])
    for offset_row in range(3):
        for offset_col in range(3):
            depthwise = depthwise + kernel[3 * offset_row + offset_col] * padded[..., offset_row:offset_row + size_cells, offset_col:offset_col + size_cells, :]
    centre_mean = lax.optimization_barrier(jnp.mean(depthwise, axis=-1, keepdims=True))
    centred = depthwise - centre_mean
    spread = lax.optimization_barrier(jnp.mean(centred * centred, axis=-1, keepdims=True))
    normed = centred * lax.rsqrt(spread + EPSILON) * gain_full
    flattened = normed.reshape(-1, normed.shape[-1])
    hidden = jax.nn.gelu(jnp.dot(flattened, up_full, precision=PRECISE, preferred_element_type=jnp.float32))
    branch_out = jnp.dot(hidden, down_full, precision=PRECISE, preferred_element_type=jnp.float32)
    return padded[..., 1:-1, 1:-1, :] + branch_out.reshape(depthwise.shape)

def across_seams(strips, partners, seam_code, edge):
    partner = partners[:, edge]
    tile_ids = jnp.arange(strips.shape[1], dtype=jnp.int32)
    fetched = strips[partner[:, None], tile_ids[None, :]]
    return jnp.where((seam_code[:, :, edge] == 1)[:, :, None, None], fetched[:, :, ::-1], fetched)

def rim_pair(low_strip, high_strip, partners, seam_code, stride, low_edge, high_edge, low_border, high_border):
    zero_rows = jnp.zeros_like(low_strip[:, :stride])
    from_low = jnp.concatenate([zero_rows, high_strip[:, :-stride]], axis=1)
    from_high = jnp.concatenate([low_strip[:, stride:], zero_rows], axis=1)
    seam_low = across_seams(low_strip, partners, seam_code, low_edge)
    seam_high = across_seams(high_strip, partners, seam_code, high_edge)
    got_low = jnp.where(low_border[None, :, None, None], seam_low, from_low)
    got_high = jnp.where(high_border[None, :, None, None], seam_high, from_high)
    return (got_low, got_high)

def pad_field(state_field, seam_code):
    partners = face_partners(state_field.shape[0])
    grid_side = math.isqrt(state_field.shape[1])
    tile_ids = jnp.arange(state_field.shape[1], dtype=jnp.int32)
    tile_row = tile_ids // grid_side
    tile_col = tile_ids % grid_side
    west_rim, east_rim = rim_pair(state_field[:, :, :, 0], state_field[:, :, :, -1], partners, seam_code, 1, 2, 3, tile_col == 0, tile_col == grid_side - 1)
    widened = jnp.concatenate([west_rim[:, :, :, None], state_field, east_rim[:, :, :, None]], axis=3)
    north_rim, south_rim = rim_pair(widened[:, :, 0], widened[:, :, -1], partners, seam_code, grid_side, 0, 1, tile_row == 0, tile_row == grid_side - 1)
    return jnp.concatenate([north_rim[:, :, None], widened, south_rim[:, :, None]], axis=2)

def reference(state_field, out_grad, depth_kernel, norm_gain, up_weight, down_weight, seam_code):
    padded, pad_back = jax.vjp(lambda values: pad_field(values, seam_code), state_field)

    def per_face(pair_in):
        face_pad, face_cot = pair_in
        result, pull_back = jax.vjp(convnext_block, face_pad, depth_kernel, norm_gain, up_weight, down_weight)
        return (result, pull_back(face_cot))
    new_field, gradients = lax.map(per_face, (padded, out_grad))
    field_grad, = pad_back(gradients[0])
    kernel_grad = lax.optimization_barrier(jnp.sum(gradients[1], axis=0))
    gain_grad = lax.optimization_barrier(jnp.sum(gradients[2], axis=0))
    up_grad = lax.optimization_barrier(jnp.sum(gradients[3], axis=0))
    down_grad = lax.optimization_barrier(jnp.sum(gradients[4], axis=0))
    return (new_field, field_grad, kernel_grad, gain_grad, up_grad, down_grad)
```

```python
import functools
import math

import jax
import jax.numpy as jnp
from jax import lax
from jax.experimental import pallas as pl
from jax.experimental.pallas import tpu as pltpu
from jax.sharding import PartitionSpec as P

EPSILON = 1e-06
NX, NH, NY, NL, NC = 4, 2, 8, 4, 2
MESH = pl.DeviceIdType.MESH
F32, BF16 = jnp.float32, jnp.bfloat16
ROOT = math.sqrt(2.0 / math.pi)
NN = (((1,), (0,)), ((), ()))
NT = (((1,), (1,)), ((), ()))


class Slots:
    def __init__(self):
        self.used = 0

    def take(self, count):
        first = self.used
        self.used += count
        return first


SLOTS = Slots()
S_XH = SLOTS.take(8)
S_RING = SLOTS.take(32)
S_X = SLOTS.take(24)
S_SIB = SLOTS.take(8)
S_KG1 = SLOTS.take(8)
S_KG2 = SLOTS.take(8)
S_HALO = SLOTS.take(4)
R_SIB = SLOTS.take(8)
R_RING = SLOTS.take(32)
R_X = SLOTS.take(24)
R_Z = SLOTS.take(8)
R_F = SLOTS.take(8)
R_KY = SLOTS.take(8)
R_KX = SLOTS.take(4)
R_KZ = SLOTS.take(16)
R_HALO = SLOTS.take(4)
N_SLOTS = SLOTS.used

SIGNS = ((0, 1), (0, -1))


def split(value):
    high = value.astype(BF16)
    return high, (value - high.astype(F32)).astype(BF16)


def dot3(a, b, dims):
    def one(p, q):
        return lax.dot_general(p, q, dims, preferred_element_type=F32)

    return one(a[0], b[0]) + (one(a[0], b[1]) + one(a[1], b[0]))


def device(x, h, y, l, c):
    return (l * NC + c, (x * NH + h) * NY + y)


def kernel(
    state, cot, up, down, kg, code,
    out_new, out_field, out_up, out_down, out_kg,
    w, g, padded, pgrad, zpad, ns_send, ns_recv, we_send, we_recv, bns_send, bns_recv, bwe_send, bwe_recv,
    kg_own, kg_xh, kg_all, kgr_own, kgr_y, kgr_x, kgr_z,
    u_hi, u_lo, d_hi, d_lo, xhat, rstd, n_hi, n_lo, nt_hi, nt_lo, g_hi, g_lo, branch, dnorm, ugrad, ddw, krows,
    s_recv, ring_recv0, ring_recv1, x_recv0, x_recv1, z_recv, final,
    ssem, rsem,
):
    face, tile = lax.axis_index("face"), lax.axis_index("tile")
    l, c = face // 2, face % 2
    x, h, y = tile // 16, (tile // 8) % 2, tile % 8
    xh = x * 2 + h
    z = h * 4 + l

    def copy(src, dst, slot, to):
        return pltpu.make_async_remote_copy(
            src_ref=src, dst_ref=dst, send_sem=ssem.at[slot], recv_sem=rsem.at[slot],
            device_id=to, device_id_type=MESH,
        )

    def arrived(dst, slot):
        copy(dst, dst, slot, device(x, h, y, l, 1 - c)).wait_recv()

    barrier = pltpu.get_barrier_semaphore()
    peers = []
    for k in range(1, 16):
        peers.append(device(x, (h + k // 8) % 2, y, (l + (k // 2) % 4) % 4, (c + k % 2) % 2))
    for k in range(1, NY):
        peers.append(device(x, h, (y + k) % NY, l, c))
    for dx in range(1, NX):
        for dh in range(NH):
            peers.append(device((x + dx) % NX, (h + dh) % NH, y, l, c))
    for peer in peers:
        pl.semaphore_signal(barrier, inc=1, device_id=peer, device_id_type=MESH)

    sub8 = lax.broadcasted_iota(jnp.int32, (8, 128), 0)

    def own_blocks(core):
        for q in range(2):
            lanes = slice(256 * core + 128 * q, 256 * core + 128 * q + 128)
            lanes2 = slice(512 + 256 * core + 128 * q, 512 + 256 * core + 128 * q + 128)
            w[core, y, xh * 4 + q] = jnp.concatenate([up[:, lanes], up[:, lanes2]], axis=0)
            w[core, y, xh * 4 + 2 + q] = down[8 * core : 8 * core + 8, 128 * q : 128 * q + 128]

    for core in range(2):
        pl.when(c == core)(functools.partial(own_blocks, core))
    kg_tile = jnp.where(sub8 == xh, jnp.broadcast_to(kg[...], (8, 128)), 0.0)
    kg_own[...] = kg_tile
    kg_xh[0] = kg_tile

    flips = [code[0, e].astype(F32) for e in range(4)]

    def mixed(flip, a, b):
        return a * (1.0 - flip) + b * flip

    for i in range(16):
        padded[1 + i, 8:24, :] = state[i]
        we_send[0, i : i + 1, :] = mixed(flips[2], state[i, 0:1, :], state[15 - i, 0:1, :])
        we_send[1, i : i + 1, :] = mixed(flips[3], state[i, 15:16, :], state[15 - i, 15:16, :])

    row, col = xh, y
    inner_n, inner_s = (row + 7) // 8, (14 - row) // 8
    inner_w, inner_e = (col + 7) // 8, (14 - col) // 8
    across = (
        (face + 4) % 8,
        7 - face,
        (face + 7 + 2 * (face % 2)) % 8,
        face + 1 - 2 * (face % 2),
    )

    def rim_copies(send, recv, base, stride, low_edge, high_edge, inner_low, inner_high):
        low_to = (
            inner_low * face + (1 - inner_low) * across[low_edge],
            tile - stride * inner_low,
        )
        high_to = (
            inner_high * face + (1 - inner_high) * across[high_edge],
            tile + stride * inner_high,
        )
        low = pltpu.make_async_remote_copy(
            src_ref=send.at[0], dst_ref=recv.at[inner_low], send_sem=ssem.at[base],
            recv_sem=rsem.at[base + inner_low], device_id=low_to, device_id_type=MESH,
        )
        high = pltpu.make_async_remote_copy(
            src_ref=send.at[1], dst_ref=recv.at[1 - inner_high], send_sem=ssem.at[base + 1],
            recv_sem=rsem.at[base + 1 - inner_high], device_id=high_to, device_id_type=MESH,
        )
        return low, high

    pl.semaphore_wait(barrier, len(peers))

    we = rim_copies(we_send, we_recv, S_HALO, 1, 2, 3, inner_w, inner_e)
    for each in we:
        each.start()
    kg1 = []
    for k in range(1, 8):
        dx, dh = k // 2, k % 2
        kg1.append(
            copy(kg_own, kg_xh.at[k], S_KG1 + k, device((x + dx) % NX, (h + dh) % NH, y, l, c))
        )

    def own_chunk(core, xs, hs):
        return w.at[core, y, pl.ds((xs * 2 + hs) * 4, 4)]

    def first_leg_0():
        mine = own_chunk(0, x, h)
        for k in (1, 2, 6, 3, 7, 4, 5):
            dx, dh = k // 2, k % 2
            copy(mine, mine, S_XH + k, device((x + dx) % NX, (h + dh) % NH, y, l, c)).start()

    def first_leg_1():
        mine = own_chunk(1, x, h)
        copy(mine, mine, S_XH + 1, device(x, 1 - h, y, l, c)).start()

    pl.when(c == 0)(first_leg_0)
    pl.when(c == 1)(first_leg_1)
    for each in kg1:
        each.start()

    for k in range(2):
        arrived(we_recv.at[k], S_HALO + k)
    for i in range(16):
        padded[1 + i, 7:8, :] = we_recv[0, i : i + 1, :]
        padded[1 + i, 24:25, :] = we_recv[1, i : i + 1, :]
    for i in range(18):
        ns_send[0, i : i + 1, :] = mixed(flips[0], padded[1, 7 + i : 8 + i, :], padded[1, 24 - i : 25 - i, :])
        ns_send[1, i : i + 1, :] = mixed(flips[1], padded[16, 7 + i : 8 + i, :], padded[16, 24 - i : 25 - i, :])
    ns = rim_copies(ns_send, ns_recv, S_HALO + 2, 8, 0, 1, inner_n, inner_s)
    for each in ns:
        each.start()
    for k in range(1, 8):
        arrived(kg_xh.at[k], S_KG1 + k)
    total = kg_xh[0]
    for k in range(1, 8):
        total = total + kg_xh[k]
    kg_all[y] = total
    kg2 = []
    for k in range(1, NY):
        mine = kg_all.at[y]
        each = copy(mine, mine, S_KG2 + k, device(x, h, (y + k) % NY, l, c))
        each.start()
        kg2.append(each)

    sibling = device(x, h, y, l, 1 - c)
    near = [0, -1, 1, -2, 2, -3, 3, 4]

    def ring_to(sign):
        return device(x, h, (y + sign + NY) % NY, l, c)

    def gather_0():
        sends = []

        def sub(yy, dx):
            return w.at[0, yy, pl.ds(((x - dx + NX) % NX) * 8, 8)]

        def hop(way, step, dx):
            sign = 1 if way == 0 else -1
            ref = sub((y - sign * step + NY) % NY, dx)
            each = copy(ref, ref, S_RING + way * 16 + step * 4 + dx, ring_to(sign))
            each.start()
            sends.append(each)

        for dx in range(NX):
            for dh in range(NH):
                if dx or dh:
                    arrived(own_chunk(0, (x - dx + NX) % NX, (h - dh + NH) % NH), S_XH + dx * 2 + dh)
            hop(0, 0, dx)
            hop(1, 0, dx)
        sib = copy(w.at[0, y], w.at[0, y], S_SIB, sibling)
        sib.start()
        sends.append(sib)
        for step in range(1, 5):
            for dx in range(NX):
                for way in range(2):
                    if step == 4 and (dx // 2) != way:
                        continue
                    sign = 1 if way == 0 else -1
                    arrived(sub((y - sign * step + NY) % NY, dx), S_RING + way * 16 + (step - 1) * 4 + dx)
                    if step < 3 or (step == 3 and (dx // 2) == way):
                        hop(way, step, dx)
            for offset in (-step, step) if step < 4 else (4,):
                ref = w.at[0, (y + offset + NY) % NY]
                sib = copy(ref, ref, S_SIB + near.index(offset), sibling)
                sib.start()
                sends.append(sib)
        mine = own_chunk(0, x, h)
        for k in range(1, 8):
            sends.append(copy(mine, mine, S_XH + k, sibling))
        for each in sends:
            each.wait_send()

    def gather_1():
        sends = []

        def sub(yy, hs):
            return w.at[1, yy, pl.ds(x * 8 + hs * 4, 4)]

        def hop(way, step, hs):
            sign = 1 if way == 0 else -1
            ref = sub((y - sign * step + NY) % NY, hs)
            each = copy(ref, ref, S_RING + way * 16 + step * 4 + hs, ring_to(sign))
            each.start()
            sends.append(each)

        def spread(offset):
            ref = w.at[1, (y + offset + NY) % NY, pl.ds(x * 8, 8)]
            for dx in (2, 1, 3):
                each = copy(
                    ref, ref, S_X + (dx - 1) * 8 + near.index(offset), device((x + dx) % NX, h, y, l, c)
                )
                each.start()
                sends.append(each)

        arrived(own_chunk(1, x, 1 - h), S_XH + 1)
        for hs in range(2):
            hop(0, 0, hs)
            hop(1, 0, hs)
        spread(0)
        for step in range(1, 5):
            for hs in range(2):
                for way in range(2):
                    if step == 4 and hs != way:
                        continue
                    sign = 1 if way == 0 else -1
                    arrived(sub((y - sign * step + NY) % NY, hs), S_RING + way * 16 + (step - 1) * 4 + hs)
                    if step < 3 or (step == 3 and hs == way):
                        hop(way, step, hs)
            for offset in (-step, step) if step < 4 else (4,):
                spread(offset)
        for offset in near:
            yy = (y + offset + NY) % NY
            for dx in range(1, NX):
                arrived(w.at[1, yy, pl.ds(((x - dx + NX) % NX) * 8, 8)], S_X + (dx - 1) * 8 + near.index(offset))
            sib = copy(w.at[1, yy], w.at[1, yy], S_SIB + near.index(offset), sibling)
            sib.start()
            sends.append(sib)
        mine = own_chunk(1, x, h)
        sends.append(copy(mine, mine, S_XH + 1, sibling))
        for each in sends:
            each.wait_send()

    pl.when(c == 0)(gather_0)
    pl.when(c == 1)(gather_1)

    for k in range(1, NY):
        ref = kg_all.at[(y - k + NY) % NY]
        arrived(ref, S_KG2 + k)
    rows64 = lax.broadcasted_iota(jnp.int32, (64, 256), 0)
    chan = lax.broadcasted_iota(jnp.int32, (64, 256), 1)
    owner = (chan // 4) == ((rows64 % 8) * 8 + rows64 // 8)
    lane = lax.broadcasted_iota(jnp.int32, (64, 128), 1)
    same4 = (
        lax.broadcasted_iota(jnp.int32, (128, 256), 0) % 4
        == lax.broadcasted_iota(jnp.int32, (128, 256), 1) % 4
    )
    spread4 = jnp.where(same4, 1.0, 0.0).astype(BF16)
    tiles = kg_all[...].reshape(64, 128)
    grouped = jnp.concatenate(
        [jnp.where(lane // 4 == k, tiles, 0.0) for k in range(10)], axis=0
    )
    first, second = split(grouped)
    spread_rows = lax.dot_general(first, spread4, NN, preferred_element_type=F32) + lax.dot_general(
        second, spread4, NN, preferred_element_type=F32
    )
    for k in range(10):
        krows[k : k + 1, :] = jnp.sum(
            jnp.where(owner, spread_rows[64 * k : 64 * k + 64], 0.0), axis=0, keepdims=True
        )

    for k in range(2):
        arrived(ns_recv.at[k], S_HALO + 2 + k)
    padded[0, 7:25, :] = ns_recv[0]
    padded[17, 7:25, :] = ns_recv[1]

    gain = krows[9:10, :]

    def conv_row(r, carry):
        acc = jnp.zeros((16, 256), F32)
        for i in range(3):
            for j in range(3):
                acc = acc + krows[3 * i + j : 3 * i + j + 1, :] * padded[r + i, 7 + j : 23 + j, :]
        mean = jnp.mean(acc, axis=-1, keepdims=True)
        centred = acc - mean
        var = jnp.mean(centred * centred, axis=-1, keepdims=True)
        inv = lax.rsqrt(var + EPSILON)
        hat = centred * inv
        at = pl.ds(pl.multiple_of(r * 16, 16), 16)
        xhat[at, :] = hat
        rstd[at, :] = jnp.broadcast_to(inv, (16, 128))
        high, low = split(hat * gain)
        n_hi[at, :] = high
        n_lo[at, :] = low
        high, low = split(cot[r])
        g_hi[at, :] = high
        g_lo[at, :] = low
        return carry

    lax.fori_loop(0, 16, conv_row, 0)
    high, low = split(jnp.transpose(xhat[...] * gain))
    nt_hi[...] = high
    nt_lo[...] = low

    for k, offset in enumerate(near):
        arrived(w.at[1 - c, (y + offset + NY) % NY], S_SIB + k)

    lows = lax.broadcasted_iota(jnp.int32, (4, 8, 128), 1) < 4

    def unpack(xs, carry):
        for hs in range(NH):
            for q in range(2):
                ref = pl.ds(xs * 8 + hs * 4 + q, 1)
                for cc in range(2):
                    v = w[cc, :, ref].reshape(4, 2, 8, 128)
                    a, b = v[:, 0], v[:, 1]
                    at = pl.ds(pl.multiple_of(xs * 64 + hs * 32, 32), 32)
                    for half, value in (
                        (0, jnp.where(lows, a, pltpu.roll(b, 4, 1))),
                        (1, jnp.where(lows, pltpu.roll(a, 4, 1), b)),
                    ):
                        high, low = split(value.reshape(32, 128))
                        u_hi[2 * half + cc, at, 128 * q : 128 * q + 128] = high
                        u_lo[2 * half + cc, at, 128 * q : 128 * q + 128] = low
                ref = pl.ds(xs * 8 + hs * 4 + 2 + q, 1)
                both = jnp.concatenate(
                    [w[0, :, ref].reshape(8, 8, 128), w[1, :, ref].reshape(8, 8, 128)], axis=1
                ).reshape(128, 128)
                high, low = split(both)
                d_hi[xs, 128 * hs : 128 * hs + 128, 128 * q : 128 * q + 128] = high
                d_lo[xs, 128 * hs : 128 * hs + 128, 128 * q : 128 * q + 128] = low
        return carry

    lax.fori_loop(0, NX, unpack, 0)

    branch[...] = jnp.zeros_like(branch)
    dnorm[...] = jnp.zeros_like(dnorm)

    def chunk(j, carry):
        normed = (n_hi[...], n_lo[...])
        grads = (g_hi[...], g_lo[...])
        ups = (u_hi[j], u_lo[j])
        downs = (d_hi[j], d_lo[j])
        pre = dot3(normed, ups, NN)
        back = dot3(grads, downs, NT)
        square = pre * pre
        t = jnp.tanh(ROOT * (pre + 0.044715 * (square * pre)))
        half = 0.5 * (1.0 + t)
        hidden = pre * half
        slope = half + 0.5 * pre * (1.0 - t * t) * (ROOT * (1.0 + 3 * 0.044715 * square))
        dpre = back * slope
        branch[...] += dot3(split(hidden), downs, NN)
        dp = split(dpre)
        dnorm[...] += dot3(dp, ups, NT)
        ugrad[j] = dot3((nt_hi[...], nt_lo[...]), dp, NN)
        dg = dot3(split(jnp.transpose(hidden)), grads, NN)
        for hs in range(NH):
            for q in range(2):
                v = dg[128 * hs : 128 * hs + 128, 128 * q : 128 * q + 128].reshape(8, 2, 8, 128)
                for cc in range(2):
                    g[cc, :, pl.ds(j * 8 + hs * 4 + 2 + q, 1)] = v[:, cc].reshape(8, 1, 8, 128)
        return carry

    lax.fori_loop(0, 4, chunk, 0)

    def pack(xs, carry):
        for hs in range(NH):
            for q in range(2):
                for cc in range(2):
                    at = pl.ds(pl.multiple_of(xs * 64 + hs * 32, 32), 32)
                    v0 = ugrad[cc, at, 128 * q : 128 * q + 128].reshape(4, 8, 128)
                    v1 = ugrad[2 + cc, at, 128 * q : 128 * q + 128].reshape(4, 8, 128)
                    even = jnp.where(lows, v0, pltpu.roll(v1, 4, 1))
                    odd = jnp.where(lows, pltpu.roll(v0, 4, 1), v1)
                    both = jnp.concatenate([even[:, None], odd[:, None]], axis=1)
                    g[cc, :, pl.ds(xs * 8 + hs * 4 + q, 1)] = both.reshape(8, 1, 8, 128)
        return carry

    lax.fori_loop(0, NX, pack, 0)

    far = [4, 3, -3, 2, -2, 1, -1, 0]
    swaps = []
    for k, offset in enumerate(far):
        yy = (y + offset + NY) % NY
        each = copy(g.at[1 - c, yy], s_recv.at[yy], R_SIB + k, sibling)
        each.start()
        swaps.append(each)

    for r in range(16):
        out_new[r] = state[r] + branch[16 * r : 16 * r + 16, :]

    krows[9:10, :] = jnp.sum(dnorm[...] * xhat[...], axis=0, keepdims=True)
    zpad[...] = jnp.zeros_like(zpad)

    def norm_row(r, sums):
        at = pl.ds(pl.multiple_of(r * 16, 16), 16)
        hat = xhat[at, :]
        inv = rstd[at, :][:, 0:1]
        dhat = dnorm[at, :] * gain
        mean = jnp.mean(dhat, axis=-1, keepdims=True)
        cross = jnp.mean(dhat * hat, axis=-1, keepdims=True)
        dd = inv * (dhat - mean - hat * cross)
        zpad[r + 2, 8:24, :] = dd
        fresh = []
        for i in range(3):
            for j in range(3):
                v = dd * padded[r + i, 7 + j : 23 + j, :]
                fresh.append(sums[3 * i + j] + v[0:8] + v[8:16])
        return tuple(fresh)

    gain_saved = gain
    sums = lax.fori_loop(0, 16, norm_row, tuple(jnp.zeros((8, 256), F32) for _ in range(9)))
    kernel_rows = [krows[k : k + 1, :] for k in range(9)]

    def back_row(r, carry):
        acc = jnp.zeros((18, 256), F32)
        for i in range(3):
            for j in range(3):
                acc = acc + krows[3 * i + j : 3 * i + j + 1, :] * zpad[r + 2 - i, 8 - j : 26 - j, :]
        pgrad[r, 7:25, :] = acc
        return carry

    lax.fori_loop(0, 18, back_row, 0)
    for i in range(18):
        bns_send[0, i : i + 1, :] = mixed(flips[0], pgrad[0, 7 + i : 8 + i, :], pgrad[0, 24 - i : 25 - i, :])
        bns_send[1, i : i + 1, :] = mixed(flips[1], pgrad[17, 7 + i : 8 + i, :], pgrad[17, 24 - i : 25 - i, :])
    bns = rim_copies(bns_send, bns_recv, R_HALO, 8, 0, 1, inner_n, inner_s)
    for each in bns:
        each.start()

    grad_rows = [jnp.sum(sums[k], axis=0, keepdims=True) for k in range(9)] + [krows[9:10, :]]
    grouped = jnp.concatenate([jnp.where(owner, jnp.broadcast_to(v, (64, 256)), 0.0) for v in grad_rows], axis=0)
    first, second = split(grouped)
    fold = lax.dot_general(first, spread4, NT, preferred_element_type=F32) + lax.dot_general(
        second, spread4, NT, preferred_element_type=F32
    )
    folded = jnp.zeros((64, 128), F32)
    for k in range(10):
        folded = folded + jnp.where(lane // 4 == k, fold[64 * k : 64 * k + 64], 0.0)
    kgr_own[...] = folded.reshape(8, 8, 128)
    kgs = []
    for k in range(1, NY):
        yy = (y + k) % NY
        each = copy(kgr_own.at[yy], kgr_y.at[k], R_KY + k, device(x, h, yy, l, c))
        each.start()
        kgs.append(each)

    def add(dst, src):
        dst[...] = dst[...] + src[...]

    def swapped(offset):
        yy = (y + offset + NY) % NY
        arrived(s_recv.at[yy], R_SIB + far.index(offset))
        return yy

    def reduce_0():
        sends = []

        def sub(offset, xs):
            return g.at[0, (y + offset + NY) % NY, pl.ds(xs * 8, 8)]

        def hop(way, step, xs):
            sign = 1 if way == 0 else -1
            each = copy(
                sub(sign * (4 - step), xs), ring_recv0.at[way, step, xs],
                R_RING + way * 16 + step * 4 + xs, ring_to(sign),
            )
            each.start()
            sends.append(each)

        for step in range(4):
            for offset in (4,) if step == 0 else (4 - step, step - 4):
                yy = swapped(offset)
                add(g.at[0, yy], s_recv.at[yy])
            for xs in range(NX):
                for way in range(2):
                    sign = 1 if way == 0 else -1
                    started = (xs // 2) == way
                    if step == 0 and not started:
                        continue
                    if step > 1 or (step == 1 and started):
                        arrived(ring_recv0.at[way, step - 1, xs], R_RING + way * 16 + (step - 1) * 4 + xs)
                        add(sub(sign * (4 - step), xs), ring_recv0.at[way, step - 1, xs])
                    hop(way, step, xs)
        yy = swapped(0)
        add(g.at[0, yy], s_recv.at[yy])
        for way in range(2):
            for xs in range(NX):
                arrived(ring_recv0.at[way, 3, xs], R_RING + way * 16 + 12 + xs)
                add(sub(0, xs), ring_recv0.at[way, 3, xs])
        for dx in (2, 1, 3):
            to = (x + dx) % NX
            each = copy(sub(0, to), x_recv0.at[dx - 1], R_X + dx - 1, device(to, h, y, l, c))
            each.start()
            sends.append(each)
        for dx in (1, 3, 2):
            arrived(x_recv0.at[dx - 1], R_X + dx - 1)
            add(sub(0, x), x_recv0.at[dx - 1])
        for each in sends:
            each.wait_send()

    def reduce_1():
        sends = []

        def block(offset, xs):
            return g.at[1, (y + offset + NY) % NY, pl.ds(xs * 8, 8)]

        def sub(offset, hs):
            return g.at[1, (y + offset + NY) % NY, pl.ds(x * 8 + hs * 4, 4)]

        for k, offset in enumerate(far):
            yy = swapped(offset)
            add(g.at[1, yy], s_recv.at[yy])
            for dx in (2, 1, 3):
                to = (x + dx) % NX
                each = copy(
                    block(offset, to), x_recv1.at[k, dx - 1], R_X + (dx - 1) * 8 + k, device(to, h, y, l, c)
                )
                each.start()
                sends.append(each)

        def hop(way, step, hs):
            sign = 1 if way == 0 else -1
            each = copy(
                sub(sign * (4 - step), hs), ring_recv1.at[way, step, hs],
                R_RING + way * 16 + step * 4 + hs, ring_to(sign),
            )
            each.start()
            sends.append(each)

        def gathered(offset):
            k = far.index(offset)
            for dx in (1, 3, 2):
                arrived(x_recv1.at[k, dx - 1], R_X + (dx - 1) * 8 + k)
                add(block(offset, x), x_recv1.at[k, dx - 1])

        for step in range(4):
            for offset in (4,) if step == 0 else (4 - step, step - 4):
                gathered(offset)
            for hs in range(2):
                for way in range(2):
                    sign = 1 if way == 0 else -1
                    started = hs == way
                    if step == 0 and not started:
                        continue
                    if step > 1 or (step == 1 and started):
                        arrived(ring_recv1.at[way, step - 1, hs], R_RING + way * 16 + (step - 1) * 4 + hs)
                        add(sub(sign * (4 - step), hs), ring_recv1.at[way, step - 1, hs])
                    hop(way, step, hs)
        gathered(0)
        for way in range(2):
            for hs in range(2):
                arrived(ring_recv1.at[way, 3, hs], R_RING + way * 16 + 12 + hs)
                add(sub(0, hs), ring_recv1.at[way, 3, hs])
        for each in sends:
            each.wait_send()

    pl.when(c == 0)(reduce_0)
    pl.when(c == 1)(reduce_1)

    ends = []

    def piece(hs, ls):
        return g.at[c, y, x * 8 + hs * 4 + ls]

    for k in range(1, 8):
        zz = (z + k) % 8
        each = copy(piece(zz // 4, zz % 4), z_recv.at[k], R_Z + k, device(x, zz // 4, y, zz % 4, c))
        each.start()
        ends.append(each)

    for k in range(2):
        arrived(bns_recv.at[k], R_HALO + k)
    pgrad[1, 7:25, :] = pgrad[1, 7:25, :] + bns_recv[0]
    pgrad[16, 7:25, :] = pgrad[16, 7:25, :] + bns_recv[1]
    for i in range(16):
        bwe_send[0, i : i + 1, :] = mixed(flips[2], pgrad[1 + i, 7:8, :], pgrad[16 - i, 7:8, :])
        bwe_send[1, i : i + 1, :] = mixed(flips[3], pgrad[1 + i, 24:25, :], pgrad[16 - i, 24:25, :])
    bwe = rim_copies(bwe_send, bwe_recv, R_HALO + 2, 1, 2, 3, inner_w, inner_e)
    for each in bwe:
        each.start()

    for k in range(1, NY):
        arrived(kgr_y.at[k], R_KY + k)
    total = kgr_own[y]
    for k in range(1, NY):
        total = total + kgr_y[k]
    kgr_x[x] = total
    for k in range(1, NX):
        to = (x + k) % NX
        each = copy(kgr_x.at[x], kgr_x.at[x], R_KX + k, device(to, h, y, l, c))
        each.start()
        kgs.append(each)

    total = piece(h, l)[...]
    for k in range(1, 8):
        arrived(z_recv.at[k], R_Z + k)
        total = total + z_recv[k]
    final[c, l] = total
    for k in range(1, 8):
        ll, cc = (l + k // 2) % 4, (c + k % 2) % 2
        each = copy(final.at[c, l], final.at[c, l], R_F + k, device(x, h, y, ll, cc))
        each.start()
        ends.append(each)

    for k in range(1, NX):
        arrived(kgr_x.at[(x - k + NX) % NX], R_KX + k)
    total = kgr_x[0]
    for k in range(1, NX):
        total = total + kgr_x[k]
    zc = z * 2 + c
    kgr_z[zc] = total
    for k in range(1, 16):
        to = device(x, (h + k // 8) % 2, y, (l + (k // 2) % 4) % 4, (c + k % 2) % 2)
        each = copy(kgr_z.at[zc], kgr_z.at[zc], R_KZ + k, to)
        each.start()
        kgs.append(each)

    for k in range(2):
        arrived(bwe_recv.at[k], R_HALO + 2 + k)
    for i in range(16):
        pgrad[1 + i, 8:9, :] = pgrad[1 + i, 8:9, :] + bwe_recv[0, i : i + 1, :]
        pgrad[1 + i, 23:24, :] = pgrad[1 + i, 23:24, :] + bwe_recv[1, i : i + 1, :]
        out_field[i] = pgrad[1 + i, 8:24, :] + cot[i]

    for k in range(1, 8):
        ll, cc = (l - k // 2 + 4) % 4, (c + k % 2) % 2
        arrived(final.at[cc, ll], R_F + k)
    for cc in range(2):
        for q in range(2):
            v = final[cc, q]
            out_up[:, 256 * cc + 128 * q : 256 * cc + 128 * q + 128] = v[0:4]
            out_up[:, 512 + 256 * cc + 128 * q : 512 + 256 * cc + 128 * q + 128] = v[4:8]
            out_down[8 * cc : 8 * cc + 8, 128 * q : 128 * q + 128] = final[cc, 2 + q]

    for k in range(1, 16):
        hh, ll, cc = (h + k // 8) % 2, (l - (k // 2) % 4 + 4) % 4, (c + k % 2) % 2
        arrived(kgr_z.at[(hh * 4 + ll) * 2 + cc], R_KZ + k)
    total = kgr_z[0]
    for k in range(1, 16):
        total = total + kgr_z[k]
    out_kg[...] = jnp.sum(jnp.where(sub8 == xh, total, 0.0), axis=0, keepdims=True)

    for each in [*we, *kg1, *ns, *kg2, *swaps, *bns, *kgs, *bwe, *ends]:
        each.wait_send()


def shards(state_field, out_grad, depth_kernel, norm_gain, up_weight, down_weight, seam_code):
    kg = jnp.concatenate([depth_kernel.reshape(1, 36), norm_gain.reshape(1, 4), jnp.zeros((1, 88), F32)], axis=1)
    vmem = pl.BlockSpec(memory_space=pltpu.VMEM)

    def buf(*shape, dtype=F32):
        return pltpu.VMEM(shape, dtype)

    new, field, up, down, kgo = pl.pallas_call(
        kernel,
        out_shape=(
            jax.ShapeDtypeStruct((16, 16, 256), F32),
            jax.ShapeDtypeStruct((16, 16, 256), F32),
            jax.ShapeDtypeStruct((4, 1024), F32),
            jax.ShapeDtypeStruct((16, 256), F32),
            jax.ShapeDtypeStruct((1, 128), F32),
        ),
        in_specs=[vmem] * 5 + [pl.BlockSpec(memory_space=pltpu.SMEM)],
        out_specs=(vmem,) * 5,
        scratch_shapes=[
            buf(2, 8, 32, 8, 128),
            buf(2, 8, 32, 8, 128),
            buf(18, 32, 256),
            buf(18, 32, 256),
            buf(20, 32, 256),
            buf(2, 18, 256), buf(2, 18, 256), buf(2, 16, 256), buf(2, 16, 256),
            buf(2, 18, 256), buf(2, 18, 256), buf(2, 16, 256), buf(2, 16, 256),
            buf(8, 128), buf(8, 8, 128), buf(8, 8, 128),
            buf(8, 8, 128), buf(8, 8, 128), buf(4, 8, 128), buf(16, 8, 128),
            buf(4, 256, 256, dtype=BF16), buf(4, 256, 256, dtype=BF16),
            buf(4, 256, 256, dtype=BF16), buf(4, 256, 256, dtype=BF16),
            buf(256, 256), buf(256, 128),
            buf(256, 256, dtype=BF16), buf(256, 256, dtype=BF16),
            buf(256, 256, dtype=BF16), buf(256, 256, dtype=BF16),
            buf(256, 256, dtype=BF16), buf(256, 256, dtype=BF16),
            buf(256, 256), buf(256, 256), buf(4, 256, 256), buf(8, 128), buf(16, 256),
            buf(8, 32, 8, 128),
            buf(2, 4, 4, 8, 8, 128), buf(2, 4, 2, 4, 8, 128),
            buf(3, 8, 8, 128), buf(8, 3, 8, 8, 128),
            buf(8, 8, 128), buf(2, 4, 8, 128),
            pltpu.SemaphoreType.DMA((N_SLOTS,)),
            pltpu.SemaphoreType.DMA((N_SLOTS,)),
        ],
        compiler_params=pltpu.CompilerParams(
            collective_id=0, has_side_effects=True, vmem_limit_bytes=56 * 1024 * 1024
        ),
        name="block",
    )(state_field[0, 0], out_grad[0, 0], up_weight, down_weight, kg, seam_code[0])
    return (
        new[None, None],
        field[None, None],
        kgo[0, :36].reshape(9, 4),
        kgo[0, 36:40],
        up,
        down,
    )


def solution(mesh):
    placed = (
        P("face", "tile", None, None, None),
        P("face", "tile", None, None, None),
        P(None, "tile"),
        P("tile"),
        P("tile", None),
        P("tile", None),
        P("face", "tile", None),
    )
    return jax.shard_map(
        shards,
        mesh=mesh,
        in_specs=placed,
        out_specs=(
            P("face", "tile", None, None, None),
            P("face", "tile", None, None, None),
            P(None, "tile"),
            P("tile"),
            P("tile", None),
            P("tile", None),
        ),
        check_vma=False,
    )
```

```python
import functools
import math

import jax
import jax.numpy as jnp
from jax import lax
from jax.experimental import pallas as pl
from jax.experimental.pallas import tpu as pltpu
from jax.sharding import PartitionSpec as P

EPSILON = 1e-06
NX, NH, NY, NL, NC = 4, 2, 8, 4, 2
MESH = pl.DeviceIdType.MESH
F32, BF16 = jnp.float32, jnp.bfloat16
ROOT = math.sqrt(2.0 / math.pi)
NN = (((1,), (0,)), ((), ()))
NT = (((1,), (1,)), ((), ()))


class Slots:
    def __init__(self):
        self.used = 0

    def take(self, count):
        first = self.used
        self.used += count
        return first


SLOTS = Slots()
S_Y = SLOTS.take(8)
S_C = SLOTS.take(16)
S_X = SLOTS.take(48)
S_COT = SLOTS.take(1)
S_NORM = SLOTS.take(1)
S_KG1 = SLOTS.take(8)
S_KG2 = SLOTS.take(8)
S_HALO = SLOTS.take(4)
R_X = SLOTS.take(24)
R_Y = SLOTS.take(8)
R_Z = SLOTS.take(8)
R_F = SLOTS.take(2)
R_BR = SLOTS.take(2)
R_KY = SLOTS.take(8)
R_KX = SLOTS.take(4)
R_KZ = SLOTS.take(16)
R_HALO = SLOTS.take(4)
N_SLOTS = SLOTS.used

NEAR = (1, 7, 2, 6, 3, 5, 4)
FAR = (4, 3, 5, 2, 6, 1, 7, 0)


def split(value):
    high = value.astype(BF16)
    return high, (value - high.astype(F32)).astype(BF16)


def dot3(a, b, dims):
    def one(p, q):
        return lax.dot_general(p, q, dims, preferred_element_type=F32)

    return one(a[0], b[0]) + (one(a[0], b[1]) + one(a[1], b[0]))


def device(x, h, y, l, c):
    return (l * NC + c, (x * NH + h) * NY + y)


def kernel(
    state, cot, up, down, kt, gn, code,
    out_new, out_field, out_up, out_down, out_kg,
    w, g, west, middle, east, zpad, centre, wcol, ecol,
    ns_send, ns_recv, we_send, we_recv, bns_send, bns_recv, bwe_send, bwe_recv,
    kg_row, kg_own, kg_xh, kg_all, kgr_own, kgr_y, kgr_x, kgr_z,
    u_hi, u_lo, d_hi, d_lo, xhat, rstd, norm_own, norm_sib, cot_sib,
    n_hi, n_lo, nt_hi, nt_lo, g_hi, g_lo, branch, dnorm, br_recv, dn_recv, ugrad, dgrad, krows,
    x_recv, y_recv, z_recv, fin_up, fin_down,
    ssem, rsem,
):
    face, tile = lax.axis_index("face"), lax.axis_index("tile")
    l, c = face // 2, face % 2
    x, h, y = tile // 16, (tile // 8) % 2, tile % 8
    xh = x * 2 + h
    z = h * 4 + l
    same = (h + c) % 2
    ends = (l % 3 + 1) // 2

    def copy(src, dst, slot, to, send_slot=None):
        return pltpu.make_async_remote_copy(
            src_ref=src, dst_ref=dst,
            send_sem=ssem.at[slot if send_slot is None else send_slot], recv_sem=rsem.at[slot],
            device_id=to, device_id_type=MESH,
        )

    sibling = device(x, h, y, l, 1 - c)

    def arrived(dst, slot):
        copy(dst, dst, slot, sibling).wait_recv()

    def both(fn):
        pl.when(same == 0)(functools.partial(fn, True))
        pl.when(same == 1)(functools.partial(fn, False))

    barrier = pltpu.get_barrier_semaphore()
    peers = []
    for k in range(1, 16):
        peers.append(device(x, (h + k // 8) % 2, y, (l + (k // 2) % 4) % 4, (c + k % 2) % 2))
    for k in range(1, NY):
        peers.append(device(x, h, (y + k) % NY, l, c))
    for dx in range(1, NX):
        for dh in range(NH):
            peers.append(device((x + dx) % NX, (h + dh) % NH, y, l, c))
    mutual = len(peers)
    for k in range(NY):
        peers.append(device(x, 1 - h, (y + k) % NY, 3 * (1 - l // 2), c))
    for peer in peers:
        pl.semaphore_signal(barrier, inc=1, device_id=peer, device_id_type=MESH)

    def own_up(core, first):
        for e in range(2):
            low, high = (128 * (2 * (2 * e + bb) + core) for bb in range(2))
            w[y, x, first + e] = jnp.concatenate([up[:, low : low + 128], up[:, high : high + 128]], axis=0)

    def own_down():
        for rh in range(2):
            for q in range(2):
                w[y, x, 4 + 2 * rh + q] = down[8 * rh : 8 * rh + 8, 128 * q : 128 * q + 128]

    for core in range(2):
        for kind in range(2):

            def own(core=core, kind=kind):
                own_up(core, 2 if kind == 0 else 0)
                if kind == 0:
                    own_down()

            pl.when((c * 2 + same) == (core * 2 + kind))(own)

    sub8 = lax.broadcasted_iota(jnp.int32, (8, 128), 0)
    kg_row[...] = jnp.zeros_like(kg_row)
    for i in range(4):
        kg_row[i : i + 1, 0:9] = kt[i : i + 1, :]
        kg_row[i : i + 1, 9:10] = gn[0:1, i : i + 1]
    packed = kg_row[0:1, :]
    for i in range(1, 4):
        packed = packed + pltpu.roll(kg_row[i : i + 1, :], 32 * i, 1)
    kg_tile = jnp.where(sub8 == xh, jnp.broadcast_to(packed, (8, 128)), 0.0)
    kg_own[...] = kg_tile
    kg_xh[0] = kg_tile

    flips = [code[0, e].astype(F32) for e in range(4)]

    def mixed(flip, a, b):
        return a * (1.0 - flip) + b * flip

    for i in range(16):
        we_send[0, i : i + 1, :] = mixed(flips[2], state[i, 0:1, :], state[15 - i, 0:1, :])
        we_send[1, i : i + 1, :] = mixed(flips[3], state[i, 15:16, :], state[15 - i, 15:16, :])

    row, col = xh, y
    inner_n, inner_s = (row + 7) // 8, (14 - row) // 8
    inner_w, inner_e = (col + 7) // 8, (14 - col) // 8
    across = (
        (face + 4) % 8,
        7 - face,
        (face + 7 + 2 * (face % 2)) % 8,
        face + 1 - 2 * (face % 2),
    )

    def rim_copies(send, recv, base, stride, low_edge, high_edge, inner_low, inner_high):
        low_to = (
            inner_low * face + (1 - inner_low) * across[low_edge],
            tile - stride * inner_low,
        )
        high_to = (
            inner_high * face + (1 - inner_high) * across[high_edge],
            tile + stride * inner_high,
        )
        low = pltpu.make_async_remote_copy(
            src_ref=send.at[0], dst_ref=recv.at[inner_low], send_sem=ssem.at[base],
            recv_sem=rsem.at[base + inner_low], device_id=low_to, device_id_type=MESH,
        )
        high = pltpu.make_async_remote_copy(
            src_ref=send.at[1], dst_ref=recv.at[1 - inner_high], send_sem=ssem.at[base + 1],
            recv_sem=rsem.at[base + 1 - inner_high], device_id=high_to, device_id_type=MESH,
        )
        return low, high

    def prepare(r, carry):
        rows = state[pl.ds(r * 4, 4)]
        at = pl.ds(1 + r * 4, 4)
        middle[at] = rows
        west[at] = pltpu.roll(rows, 1, 1)
        east[at] = pltpu.roll(rows, 15, 1)
        high, low = split(cot[pl.ds(r * 4, 4)].reshape(64, 256))
        to = pl.ds(pl.multiple_of(r * 64, 64), 64)
        g_hi[0, to, :] = high
        g_lo[0, to, :] = low
        return carry

    lax.fori_loop(0, 4, prepare, 0)

    pl.semaphore_wait(barrier, mutual + 16 * (1 - ends))

    we = rim_copies(we_send, we_recv, S_HALO, 1, 2, 3, inner_w, inner_e)
    for each in we:
        each.start()

    def piece(yy, xx, whole):
        return w.at[yy, xx, 2:8] if whole else w.at[yy, xx, 0:2]

    def y_sends(whole):
        mine = piece(y, x, whole)
        return [copy(mine, mine, S_Y + k, device(x, h, (y + k) % NY, l, c)) for k in NEAR]

    def cross_sends(whole):
        mine = piece(y, x, whole)
        sends = []
        for k in (0, *NEAR):
            for m in range(2):
                ll = (3 - m) * (1 - l // 3) + m * (l // 3)
                to = device(x, 1 - h, (y + k) % NY, ll, c)
                sends.append(
                    pltpu.make_async_remote_copy(
                        src_ref=mine, dst_ref=mine, send_sem=ssem.at[S_C + 2 * k + m], recv_sem=rsem.at[S_C + k],
                        device_id=to, device_id_type=MESH,
                    )
                )
        return sends

    def x_sends(k, other, whole):
        ref = piece((y - k + NY) % NY, x, whole != other)
        return [
            copy(ref, ref, S_X + (2 * k + other) * 3 + dx - 1, device((x + dx) % NX, h, y, l, c))
            for dx in (2, 1, 3)
        ]

    def forward(k, other, whole):
        if k or other:
            arrived(piece((y - k + NY) % NY, x, whole != other), (S_C if other else S_Y) + k)
        for each in x_sends(k, other, whole):
            each.start()

    def first_leg(whole):
        for each in y_sends(whole):
            each.start()

        @pl.when(ends == 0)
        def _():
            for each in cross_sends(whole):
                each.start()

        forward(0, False, whole)

    both(first_leg)
    cot_copy = copy(cot, cot_sib, S_COT, sibling)
    cot_copy.start()
    kg1 = []
    for k in range(1, 8):
        dx, dh = k // 2, k % 2
        each = copy(kg_own, kg_xh.at[k], S_KG1 + k, device((x + dx) % NX, (h + dh) % NH, y, l, c))
        each.start()
        kg1.append(each)

    def second_leg(whole):
        forward(1, False, whole)
        forward(7, False, whole)

    both(second_leg)

    for k in range(2):
        arrived(we_recv.at[k], S_HALO + k)
    for i in range(16):
        west[1 + i, 0:1, :] = we_recv[0, i : i + 1, :]
        east[1 + i, 15:16, :] = we_recv[1, i : i + 1, :]
    for k, (edge, line) in enumerate(((0, 0), (1, 15))):
        first, last = we_recv[0, line : line + 1, :], we_recv[1, line : line + 1, :]
        ns_send[k, 0:1, :] = mixed(flips[edge], first, last)
        ns_send[k, 17:18, :] = mixed(flips[edge], last, first)
        for i in range(16):
            ns_send[k, 1 + i : 2 + i, :] = mixed(
                flips[edge], state[line, i : i + 1, :], state[line, 15 - i : 16 - i, :]
            )
    ns = rim_copies(ns_send, ns_recv, S_HALO + 2, 8, 0, 1, inner_n, inner_s)
    for each in ns:
        each.start()

    def third_leg(whole):
        for k, other in ((0, True), (2, False), (6, False), (1, True), (7, True), (3, False), (5, False)):
            forward(k, other, whole)

    both(third_leg)

    for k in range(1, 8):
        arrived(kg_xh.at[k], S_KG1 + k)
    total = kg_xh[0]
    for k in range(1, 8):
        total = total + kg_xh[k]
    kg_all[y] = total
    kg2 = []
    for k in range(1, NY):
        mine = kg_all.at[y]
        each = copy(mine, mine, S_KG2 + k, device(x, h, (y + k) % NY, l, c))
        each.start()
        kg2.append(each)

    def fourth_leg(whole):
        for k, other in ((2, True), (6, True), (4, False), (3, True), (5, True), (4, True)):
            forward(k, other, whole)

    both(fourth_leg)

    for k in range(1, NY):
        arrived(kg_all.at[(y - k + NY) % NY], S_KG2 + k)
    rows64 = lax.broadcasted_iota(jnp.int32, (64, 256), 0)
    chan = lax.broadcasted_iota(jnp.int32, (64, 256), 1)
    owner = (chan // 4) == ((rows64 % 8) * 8 + rows64 // 8)
    lane = lax.broadcasted_iota(jnp.int32, (64, 128), 1)
    same4 = (
        lax.broadcasted_iota(jnp.int32, (128, 256), 0) // 32
        == lax.broadcasted_iota(jnp.int32, (128, 256), 1) % 4
    )
    spread4 = jnp.where(same4, 1.0, 0.0).astype(BF16)
    tiles = kg_all[...].reshape(64, 128)
    grouped = jnp.concatenate([jnp.where(lane % 32 == k, tiles, 0.0) for k in range(10)], axis=0)
    first, second = split(grouped)
    spread_rows = lax.dot_general(first, spread4, NN, preferred_element_type=F32) + lax.dot_general(
        second, spread4, NN, preferred_element_type=F32
    )
    for k in range(10):
        krows[k : k + 1, :] = jnp.sum(
            jnp.where(owner, spread_rows[64 * k : 64 * k + 64], 0.0), axis=0, keepdims=True
        )

    for k in range(2):
        arrived(ns_recv.at[k], S_HALO + 2 + k)
        line = 17 * k
        west[line] = ns_recv[k, 0:16, :]
        middle[line] = ns_recv[k, 1:17, :]
        east[line] = ns_recv[k, 2:18, :]

    shifted = (west, middle, east)
    taps = [krows[k : k + 1, :] for k in range(9)]
    gain = krows[9:10, :]

    def conv_rows(r, carry):
        acc = jnp.zeros((4, 16, 256), F32)
        for i in range(3):
            for j in range(3):
                acc = acc + krows[3 * i + j : 3 * i + j + 1, :] * shifted[j][pl.ds(r * 4 + i, 4)]
        acc = acc.reshape(64, 256)
        mean = jnp.mean(acc, axis=-1, keepdims=True)
        centred = acc - mean
        var = jnp.mean(centred * centred, axis=-1, keepdims=True)
        inv = lax.rsqrt(var + EPSILON)
        hat = centred * inv
        at = pl.ds(pl.multiple_of(r * 64, 64), 64)
        xhat[at, :] = hat
        rstd[at, :] = jnp.broadcast_to(inv, (64, 128))
        normed = hat * krows[9:10, :]
        norm_own[at, :] = normed
        return carry

    lax.fori_loop(0, 4, conv_rows, 0)
    norm_copy = copy(norm_own, norm_sib, S_NORM, sibling)
    norm_copy.start()

    def prepare_tokens(m, source):
        def halves(r, carry):
            at = pl.ds(pl.multiple_of(r * 128, 128), 128)
            value = source[at, :]
            high, low = split(value)
            n_hi[m, at, :] = high
            n_lo[m, at, :] = low
            high, low = split(jnp.transpose(value))
            nt_hi[m, r] = high
            nt_lo[m, r] = low
            return carry

        lax.fori_loop(0, 2, halves, 0)

    prepare_tokens(0, norm_own)

    def x_arrivals(whole):
        for k in (0, *NEAR):
            for other in (False, True):
                for dx in (1, 3, 2):
                    ref = piece((y - k + NY) % NY, (x - dx + NX) % NX, whole != other)
                    arrived(ref, S_X + (2 * k + other) * 3 + dx - 1)

    both(x_arrivals)

    lows = lax.broadcasted_iota(jnp.int32, (4, 8, 128), 1) < 4

    def unpack(xs, carry):
        for r in range(2):
            hs = r * c + (1 - r) * (1 - c)
            at = pl.ds(pl.multiple_of(xs * 64 + hs * 32, 32), 32)
            for e in range(2):
                v = w[:, xs, 2 * r + e].reshape(4, 2, 8, 128)
                a, b = v[:, 0], v[:, 1]
                for bb, value in (
                    (0, jnp.where(lows, a, pltpu.roll(b, 4, 1))),
                    (1, jnp.where(lows, pltpu.roll(a, 4, 1), b)),
                ):
                    high, low = split(value.reshape(32, 128))
                    u_hi[e, at, 128 * bb : 128 * bb + 128] = high
                    u_lo[e, at, 128 * bb : 128 * bb + 128] = low
        at = pl.ds(pl.multiple_of((xs % 2) * 128, 128), 128)
        for q in range(2):
            value = jnp.concatenate([w[:, xs, 4 + q], w[:, xs, 6 + q]], axis=1).reshape(128, 128)
            high, low = split(value)
            d_hi[xs // 2, at, 128 * q : 128 * q + 128] = high
            d_lo[xs // 2, at, 128 * q : 128 * q + 128] = low
        return carry

    lax.fori_loop(0, NX, unpack, 0)

    arrived(cot_sib, S_COT)

    def prepare_cot(r, carry):
        high, low = split(cot_sib[pl.ds(r * 4, 4)].reshape(64, 256))
        to = pl.ds(pl.multiple_of(r * 64, 64), 64)
        g_hi[1, to, :] = high
        g_lo[1, to, :] = low
        return carry

    lax.fori_loop(0, 4, prepare_cot, 0)
    arrived(norm_sib, S_NORM)
    prepare_tokens(1, norm_sib)

    branch[...] = jnp.zeros_like(branch)
    dnorm[...] = jnp.zeros_like(dnorm)
    ugrad[...] = jnp.zeros_like(ugrad)
    dgrad[...] = jnp.zeros_like(dgrad)

    def chunk(step, carry):
        e, m = step // 2, step % 2
        normed = (n_hi[m], n_lo[m])
        grads = (g_hi[m], g_lo[m])
        ups = (u_hi[e], u_lo[e])
        downs = (d_hi[e], d_lo[e])
        pre = dot3(normed, ups, NN)
        back = dot3(grads, downs, NT)
        square = pre * pre
        t = jnp.tanh(ROOT * (pre + 0.044715 * (square * pre)))
        half = 0.5 * (1.0 + t)
        hidden = pre * half
        slope = half + 0.5 * pre * (1.0 - t * t) * (ROOT * (1.0 + 3 * 0.044715 * square))
        dpre = back * slope
        branch[m] += dot3(split(hidden), downs, NN)
        dp = split(dpre)
        dnorm[m] += dot3(dp, ups, NT)
        for r in range(2):
            part = tuple(v[128 * r : 128 * r + 128] for v in dp)
            ugrad[e] += dot3((nt_hi[m, r], nt_lo[m, r]), part, NN)
        dgrad[e] += dot3(split(jnp.transpose(hidden)), grads, NN)
        return carry

    lax.fori_loop(0, 4, chunk, 0)

    def pack(xs, carry):
        for r in range(2):
            hs = r * c + (1 - r) * (1 - c)
            at = pl.ds(pl.multiple_of(xs * 64 + hs * 32, 32), 32)
            for e in range(2):
                v0 = ugrad[e, at, 0:128].reshape(4, 8, 128)
                v1 = ugrad[e, at, 128:256].reshape(4, 8, 128)
                even = jnp.where(lows, v0, pltpu.roll(v1, 4, 1))
                odd = jnp.where(lows, pltpu.roll(v0, 4, 1), v1)
                g[:, xs, 2 * r + e] = jnp.concatenate([even[:, None], odd[:, None]], axis=1).reshape(8, 8, 128)
        at = pl.ds(pl.multiple_of((xs % 2) * 128, 128), 128)
        for q in range(2):
            v = dgrad[xs // 2, at, 128 * q : 128 * q + 128].reshape(8, 2, 8, 128)
            for rh in range(2):
                g[:, xs, 4 + 2 * rh + q] = v[:, rh]
        return carry

    lax.fori_loop(0, NX, pack, 0)

    swaps = [copy(dnorm.at[1], dn_recv, R_BR, sibling), copy(branch.at[1], br_recv, R_BR + 1, sibling)]
    swaps[0].start()
    reduces = []
    for k, offset in enumerate(FAR):
        yy = (y + offset) % NY
        for dx in (2, 1, 3):
            to = (x + dx) % NX
            each = copy(g.at[yy, to], x_recv.at[k, dx - 1], R_X + 3 * k + dx - 1, device(to, h, y, l, c))
            each.start()
            reduces.append(each)
    swaps[1].start()

    zpad[0:2] = jnp.zeros((2, 16, 256), F32)
    zpad[18:20] = jnp.zeros((2, 16, 256), F32)
    arrived(dn_recv, R_BR)

    def norm_rows(r, sums):
        at = pl.ds(pl.multiple_of(r * 32, 32), 32)
        hat = xhat[at, :]
        inv = rstd[at, :][:, 0:1]
        dn = dnorm[0, at, :] + dn_recv[at, :]
        dhat = dn * krows[9:10, :]
        mean = jnp.mean(dhat, axis=-1, keepdims=True)
        cross = jnp.mean(dhat * hat, axis=-1, keepdims=True)
        dd = (inv * (dhat - mean - hat * cross)).reshape(2, 16, 256)
        zpad[pl.ds(r * 2 + 2, 2)] = dd
        fresh = []
        for i in range(3):
            for j in range(3):
                v = (dd * shifted[j][pl.ds(r * 2 + i, 2)]).reshape(4, 8, 256)
                fresh.append(sums[3 * i + j] + ((v[0] + v[1]) + (v[2] + v[3])))
        v = (dn * hat).reshape(4, 8, 256)
        fresh.append(sums[9] + ((v[0] + v[1]) + (v[2] + v[3])))
        return tuple(fresh)

    sums = lax.fori_loop(0, 8, norm_rows, tuple(jnp.zeros((8, 256), F32) for _ in range(10)))

    lanes16 = lax.broadcasted_iota(jnp.int32, (2, 16, 256), 1)

    def back_rows(r, carry):
        parts = []
        for j in range(3):
            acc = jnp.zeros((2, 16, 256), F32)
            for i in range(3):
                acc = acc + krows[3 * i + j : 3 * i + j + 1, :] * zpad[pl.ds(r * 2 + 2 - i, 2)]
            parts.append(acc)
        to = pl.ds(r * 2, 2)
        left = jnp.where(lanes16 < 15, pltpu.roll(parts[0], 15, 1), 0.0)
        right = jnp.where(lanes16 > 0, pltpu.roll(parts[2], 1, 1), 0.0)
        centre[to] = parts[1] + (left + right)
        wcol[to] = parts[0][:, 0:1, :]
        ecol[to] = parts[2][:, 15:16, :]
        return carry

    lax.fori_loop(0, 9, back_rows, 0)
    for k, (edge, line) in enumerate(((0, 0), (1, 17))):
        first, last = wcol[line], ecol[line]
        bns_send[k, 0:1, :] = mixed(flips[edge], first, last)
        bns_send[k, 17:18, :] = mixed(flips[edge], last, first)
        for i in range(16):
            bns_send[k, 1 + i : 2 + i, :] = mixed(
                flips[edge], centre[line, i : i + 1, :], centre[line, 15 - i : 16 - i, :]
            )
    bns = rim_copies(bns_send, bns_recv, R_HALO, 8, 0, 1, inner_n, inner_s)
    for each in bns:
        each.start()

    grad_rows = [jnp.sum(sums[k], axis=0, keepdims=True) for k in range(10)]
    grouped = jnp.concatenate([jnp.where(owner, jnp.broadcast_to(v, (64, 256)), 0.0) for v in grad_rows], axis=0)
    first, second = split(grouped)
    fold = lax.dot_general(first, spread4, NT, preferred_element_type=F32) + lax.dot_general(
        second, spread4, NT, preferred_element_type=F32
    )
    folded = jnp.zeros((64, 128), F32)
    for k in range(10):
        folded = folded + jnp.where(lane % 32 == k, fold[64 * k : 64 * k + 64], 0.0)
    kgr_own[...] = folded.reshape(8, 8, 128)
    kgs = []
    for k in range(1, NY):
        yy = (y + k) % NY
        each = copy(kgr_own.at[yy], kgr_y.at[k], R_KY + k, device(x, h, yy, l, c))
        each.start()
        kgs.append(each)

    for k, offset in enumerate(FAR):
        yy = (y + offset) % NY
        for dx in (1, 3, 2):
            arrived(x_recv.at[k, dx - 1], R_X + 3 * k + dx - 1)
        g[yy, x] = (g[yy, x] + x_recv[k, 0]) + (x_recv[k, 1] + x_recv[k, 2])
        if offset:
            each = copy(g.at[yy, x], y_recv.at[offset], R_Y + offset, device(x, h, yy, l, c))
            each.start()
            reduces.append(each)

    arrived(br_recv, R_BR + 1)

    def new_rows(r, carry):
        at = pl.ds(pl.multiple_of(r * 64, 64), 64)
        value = branch[0, at, :] + br_recv[at, :]
        to = pl.ds(r * 4, 4)
        out_new[to] = state[to] + value.reshape(4, 16, 256)
        return carry

    lax.fori_loop(0, 4, new_rows, 0)

    for k, line in enumerate((1, 16)):
        arrived(bns_recv.at[k], R_HALO + k)
        wcol[line] = wcol[line] + bns_recv[k, 0:1, :]
        centre[line] = centre[line] + bns_recv[k, 1:17, :]
        ecol[line] = ecol[line] + bns_recv[k, 17:18, :]
    for i in range(16):
        bwe_send[0, i : i + 1, :] = mixed(flips[2], wcol[1 + i], wcol[16 - i])
        bwe_send[1, i : i + 1, :] = mixed(flips[3], ecol[1 + i], ecol[16 - i])
    bwe = rim_copies(bwe_send, bwe_recv, R_HALO + 2, 1, 2, 3, inner_w, inner_e)
    for each in bwe:
        each.start()

    for k in range(1, NY):
        arrived(kgr_y.at[k], R_KY + k)
    total = kgr_own[y]
    for k in range(1, NY):
        total = total + kgr_y[k]
    kgr_x[x] = total
    for k in range(1, NX):
        each = copy(kgr_x.at[x], kgr_x.at[x], R_KX + k, device((x + k) % NX, h, y, l, c))
        each.start()
        kgs.append(each)

    for k in range(1, NY):
        arrived(y_recv.at[k], R_Y + k)
    total = g[y, x]
    for k in range(1, NY):
        total = total + y_recv[k]
    z_recv[z] = total

    def z_sends(whole):
        sends = []
        for k in range(1, 8):
            dh, dl = k // 4, k % 4
            full = whole if dh == 0 else not whole
            ref = z_recv.at[z, 2:8] if full else z_recv.at[z, 0:2]
            sends.append(copy(ref, ref, R_Z + k, device(x, (h + dh) % NH, y, (l + dl) % NL, c)))
        return sends

    def z_start(whole):
        for each in z_sends(whole):
            each.start()

    both(z_start)

    for k in range(1, NX):
        arrived(kgr_x.at[(x - k + NX) % NX], R_KX + k)
    total = kgr_x[0]
    for k in range(1, NX):
        total = total + kgr_x[k]
    zc = z * 2 + c
    kgr_z[zc] = total
    for k in range(1, 16):
        to = device(x, (h + k // 8) % 2, y, (l + (k // 2) % 4) % 4, (c + k % 2) % 2)
        each = copy(kgr_z.at[zc], kgr_z.at[zc], R_KZ + k, to)
        each.start()
        kgs.append(each)

    for k in range(2):
        arrived(bwe_recv.at[k], R_HALO + 2 + k)
    for i in range(16):
        centre[1 + i, 0:1, :] = centre[1 + i, 0:1, :] + bwe_recv[0, i : i + 1, :]
        centre[1 + i, 15:16, :] = centre[1 + i, 15:16, :] + bwe_recv[1, i : i + 1, :]
        out_field[i] = centre[1 + i] + cot[i]

    def fin_sends(whole):
        sends = [copy(fin_up.at[c], fin_up.at[c], R_F, sibling)]
        if whole:
            sends.append(copy(fin_down, fin_down, R_F + 1, sibling))
        return sends

    def z_end(whole):
        for k in range(1, 8):
            zz = ((h + k // 4) % NH) * 4 + (l - k % 4 + NL) % NL
            arrived(z_recv.at[zz, 2:8] if whole else z_recv.at[zz, 0:2], R_Z + k)
        span = slice(2, 8) if whole else slice(0, 2)
        total = z_recv[0, span]
        for zz in range(1, 8):
            total = total + z_recv[zz, span]
        fin_up[c] = total[0:2]
        if whole:
            fin_down[...] = total[2:6]
        for each in fin_sends(whole):
            each.start()
        arrived(fin_up.at[1 - c], R_F)
        if not whole:
            arrived(fin_down, R_F + 1)

    both(z_end)
    for cc in range(2):
        for e in range(2):
            v = fin_up[cc, e]
            for bb in range(2):
                first = 128 * (2 * (2 * e + bb) + cc)
                out_up[:, first : first + 128] = v[4 * bb : 4 * bb + 4]
    for rh in range(2):
        for q in range(2):
            out_down[8 * rh : 8 * rh + 8, 128 * q : 128 * q + 128] = fin_down[2 * rh + q]

    for k in range(1, 16):
        hh, ll, cc = (h + k // 8) % 2, (l - (k // 2) % 4 + 4) % 4, (c + k % 2) % 2
        arrived(kgr_z.at[(hh * 4 + ll) * 2 + cc], R_KZ + k)
    total = kgr_z[0]
    for k in range(1, 16):
        total = total + kgr_z[k]
    out_kg[...] = jnp.sum(jnp.where(sub8 == xh, total, 0.0), axis=0, keepdims=True)

    def all_sent(whole):
        sends = y_sends(whole) + z_sends(whole) + fin_sends(whole)
        for k in range(NY):
            for other in (False, True):
                sends += x_sends(k, other, whole)
        for each in sends:
            each.wait_send()

        @pl.when(ends == 0)
        def _():
            for each in cross_sends(whole):
                each.wait_send()

    both(all_sent)
    for each in [*we, *kg1, *ns, *kg2, cot_copy, norm_copy, *swaps, *reduces, *bns, *kgs, *bwe]:
        each.wait_send()


def results(new, field, up, down, kg, out_new, out_field, out_up, out_down, out_kt, out_gn):
    out_new[...] = new[...]
    out_field[...] = field[...]
    out_up[...] = up[...]
    out_down[...] = down[...]
    for i in range(4):
        moved = kg[...] if i == 0 else pltpu.roll(kg[...], 128 - 32 * i, 1)
        out_kt[i : i + 1, :] = moved[:, 0:9]
        out_gn[0:1, i : i + 1] = moved[:, 9:10]


def shards(state_field, out_grad, depth_kernel, norm_gain, up_weight, down_weight, seam_code):
    vmem = pl.BlockSpec(memory_space=pltpu.VMEM)

    def buf(*shape, dtype=F32):
        return pltpu.VMEM(shape, dtype)

    def half(*shape):
        return pltpu.VMEM(shape, BF16)

    found = pl.pallas_call(
        kernel,
        out_shape=(
            jax.ShapeDtypeStruct((16, 16, 256), F32),
            jax.ShapeDtypeStruct((16, 16, 256), F32),
            jax.ShapeDtypeStruct((4, 1024), F32),
            jax.ShapeDtypeStruct((16, 256), F32),
            jax.ShapeDtypeStruct((1, 128), F32),
        ),
        in_specs=[vmem] * 6 + [pl.BlockSpec(memory_space=pltpu.SMEM)],
        out_specs=(vmem,) * 5,
        scratch_shapes=[
            buf(8, 4, 8, 8, 128), buf(8, 4, 8, 8, 128),
            buf(18, 16, 256), buf(18, 16, 256), buf(18, 16, 256),
            buf(20, 16, 256), buf(18, 16, 256), buf(18, 1, 256), buf(18, 1, 256),
            buf(2, 18, 256), buf(2, 18, 256), buf(2, 16, 256), buf(2, 16, 256),
            buf(2, 18, 256), buf(2, 18, 256), buf(2, 16, 256), buf(2, 16, 256),
            buf(8, 128), buf(8, 128), buf(8, 8, 128), buf(8, 8, 128),
            buf(8, 8, 128), buf(8, 8, 128), buf(4, 8, 128), buf(16, 8, 128),
            half(2, 256, 256), half(2, 256, 256), half(2, 256, 256), half(2, 256, 256),
            buf(256, 256), buf(256, 128), buf(256, 256), buf(256, 256), buf(16, 16, 256),
            half(2, 256, 256), half(2, 256, 256), half(2, 2, 256, 128), half(2, 2, 256, 128),
            half(2, 256, 256), half(2, 256, 256),
            buf(2, 256, 256), buf(2, 256, 256), buf(256, 256), buf(256, 256),
            buf(2, 256, 256), buf(2, 256, 256), buf(16, 256),
            buf(8, 3, 8, 8, 128), buf(8, 8, 8, 128), buf(8, 8, 8, 128),
            buf(2, 2, 8, 128), buf(4, 8, 128),
            pltpu.SemaphoreType.DMA((N_SLOTS,)),
            pltpu.SemaphoreType.DMA((N_SLOTS,)),
        ],
        compiler_params=pltpu.CompilerParams(
            collective_id=0, has_side_effects=True, vmem_limit_bytes=48 * 1024 * 1024
        ),
        name="block",
    )(
        state_field[0, 0], out_grad[0, 0], up_weight, down_weight,
        depth_kernel.T, norm_gain.reshape(1, 4), seam_code[0],
    )
    new, field, up, down, kt, gn = pl.pallas_call(
        results,
        out_shape=(
            jax.ShapeDtypeStruct((16, 16, 256), F32),
            jax.ShapeDtypeStruct((16, 16, 256), F32),
            jax.ShapeDtypeStruct((4, 1024), F32),
            jax.ShapeDtypeStruct((16, 256), F32),
            jax.ShapeDtypeStruct((4, 9), F32),
            jax.ShapeDtypeStruct((1, 4), F32),
        ),
        in_specs=[vmem] * 5,
        out_specs=(vmem,) * 6,
        name="results",
    )(*found)
    return (new[None, None], field[None, None], kt.T, gn.reshape(4), up, down)


def solution(mesh):
    placed = (
        P("face", "tile", None, None, None),
        P("face", "tile", None, None, None),
        P(None, "tile"),
        P("tile"),
        P("tile", None),
        P("tile", None),
        P("face", "tile", None),
    )
    return jax.shard_map(
        shards,
        mesh=mesh,
        in_specs=placed,
        out_specs=(
            P("face", "tile", None, None, None),
            P("face", "tile", None, None, None),
            P(None, "tile"),
            P("tile"),
            P("tile", None),
            P("tile", None),
        ),
        check_vma=False,
    )
```

```python
import functools
import math

import jax
import jax.numpy as jnp
from jax import lax
from jax.experimental import pallas as pl
from jax.experimental.pallas import tpu as pltpu
from jax.sharding import PartitionSpec as P

EPSILON = 1e-06
NX, NH, NY, NL, NC = 4, 2, 8, 4, 2
MESH = pl.DeviceIdType.MESH
F32, BF16 = jnp.float32, jnp.bfloat16
ROOT = math.sqrt(2.0 / math.pi)
NN = (((1,), (0,)), ((), ()))
NT = (((1,), (1,)), ((), ()))


class Slots:
    def __init__(self):
        self.used = 0

    def take(self, count):
        first = self.used
        self.used += count
        return first


SLOTS = Slots()
S_Y = SLOTS.take(8)
S_C = SLOTS.take(16)
S_X = SLOTS.take(24)
S_BX = SLOTS.take(8)
S_BY = SLOTS.take(8)
S_IN = SLOTS.take(6)
S_OUT = SLOTS.take(5)
S_COT = SLOTS.take(1)
S_NORM = SLOTS.take(1)
S_KG1 = SLOTS.take(8)
S_KG2 = SLOTS.take(8)
S_HALO = SLOTS.take(4)
R_X = SLOTS.take(24)
R_XU = SLOTS.take(24)
R_BY = SLOTS.take(8)
R_BX = SLOTS.take(4)
R_Y = SLOTS.take(8)
R_Z = SLOTS.take(8)
R_F = SLOTS.take(2)
R_BR = SLOTS.take(2)
R_KY = SLOTS.take(8)
R_KX = SLOTS.take(4)
R_KZ = SLOTS.take(16)
R_HALO = SLOTS.take(4)
N_SLOTS = SLOTS.used

NEAR = (1, 7, 2, 6, 3, 5, 4)
FAR = (4, 3, 5, 2, 6, 1, 7, 0)


def split(value):
    high = value.astype(BF16)
    return high, (value - high.astype(F32)).astype(BF16)


def dot3(a, b, dims):
    def one(p, q):
        return lax.dot_general(p, q, dims, preferred_element_type=F32)

    return one(a[0], b[0]) + (one(a[0], b[1]) + one(a[1], b[0]))


def device(x, h, y, l, c):
    return (l * NC + c, (x * NH + h) * NY + y)


def kernel(
    state_in, cot_in, up_in, down_in, kt_in, gn_in, code,
    new_out, field_out, up_out, down_out, kg_out,
    state, cot, up, down, kt, gn, out_new, out_field, out_up, out_down, out_kg,
    w, g, west, middle, east, zpad, centre, wcol, ecol,
    ns_send, ns_recv, we_send, we_recv, bns_send, bns_recv, bwe_send, bwe_recv,
    kg_row, kg_own, kg_xh, kg_all, kgr_own, kgr_y, kgr_x, kgr_z,
    u_hi, u_lo, d_hi, d_lo, xhat, rstd, norm_own, norm_sib, cot_sib,
    n_hi, n_lo, nt_hi, nt_lo, g_hi, g_lo, h_hi, h_lo, p_hi, p_lo, branch, dnorm, br_recv, dn_recv, ugrad, dgrad, krows,
    x_recv, xu_recv, y_recv, by_recv, bx_recv, z_recv, fin_up, fin_down,
    ssem, rsem,
):
    face, tile = lax.axis_index("face"), lax.axis_index("tile")
    l, c = face // 2, face % 2
    x, h, y = tile // 16, (tile // 8) % 2, tile % 8
    xh = x * 2 + h
    z = h * 4 + l
    same = (h + c) % 2
    ends = (l % 3 + 1) // 2

    def copy(src, dst, slot, to, send_slot=None):
        return pltpu.make_async_remote_copy(
            src_ref=src, dst_ref=dst,
            send_sem=ssem.at[slot if send_slot is None else send_slot], recv_sem=rsem.at[slot],
            device_id=to, device_id_type=MESH,
        )

    sibling = device(x, h, y, l, 1 - c)

    def arrived(dst, slot):
        copy(dst, dst, slot, sibling).wait_recv()

    def both(fn):
        pl.when(same == 0)(functools.partial(fn, True))
        pl.when(same == 1)(functools.partial(fn, False))

    barrier = pltpu.get_barrier_semaphore()
    peers = []
    for k in range(1, 16):
        peers.append(device(x, (h + k // 8) % 2, y, (l + (k // 2) % 4) % 4, (c + k % 2) % 2))
    for k in range(1, NY):
        peers.append(device(x, h, (y + k) % NY, l, c))
    for dx in range(1, NX):
        for dh in range(NH):
            peers.append(device((x + dx) % NX, (h + dh) % NH, y, l, c))
    loads = [
        pltpu.make_async_copy(src, dst, ssem.at[S_IN + k])
        for k, (src, dst) in enumerate(
            ((state_in, state), (kt_in, kt), (gn_in, gn), (up_in, up), (down_in, down), (cot_in, cot))
        )
    ]
    for each in loads:
        each.start()

    def greet(peer):
        pl.semaphore_signal(barrier, inc=1, device_id=peer, device_id_type=MESH)

    for peer in peers:
        greet(peer)
    source = 3 * (1 - l // 2)

    def greet_sources(whole):
        if whole:
            for k in range(NX):
                greet(device((x + k) % NX, 1 - h, y, source, c))
        else:
            for k in range(NY):
                greet(device(x, 1 - h, (y + k) % NY, source, c))

    both(greet_sources)
    for each in loads:
        each.wait()

    def own_up(core, first):
        for e in range(2):
            low, high = (128 * (2 * (2 * e + bb) + core) for bb in range(2))
            w[y, x, first + e] = jnp.concatenate([up[:, low : low + 128], up[:, high : high + 128]], axis=0)

    def own_down():
        for rh in range(2):
            for q in range(2):
                w[y, x, 4 + 2 * rh + q] = down[8 * rh : 8 * rh + 8, 128 * q : 128 * q + 128]

    for core in range(2):
        for kind in range(2):

            def own(core=core, kind=kind):
                own_up(core, 2 if kind == 0 else 0)
                if kind == 0:
                    own_down()

            pl.when((c * 2 + same) == (core * 2 + kind))(own)

    sub8 = lax.broadcasted_iota(jnp.int32, (8, 128), 0)
    kg_row[...] = jnp.zeros_like(kg_row)
    for i in range(4):
        kg_row[i : i + 1, 0:9] = kt[i : i + 1, :]
        kg_row[i : i + 1, 9:10] = gn[0:1, i : i + 1]
    packed = kg_row[0:1, :]
    for i in range(1, 4):
        packed = packed + pltpu.roll(kg_row[i : i + 1, :], 32 * i, 1)
    kg_tile = jnp.where(sub8 == xh, jnp.broadcast_to(packed, (8, 128)), 0.0)
    kg_own[...] = kg_tile
    kg_xh[0] = kg_tile

    flips = [code[0, e].astype(F32) for e in range(4)]

    def mixed(flip, a, b):
        return a * (1.0 - flip) + b * flip

    for i in range(16):
        we_send[0, i : i + 1, :] = mixed(flips[2], state[i, 0:1, :], state[15 - i, 0:1, :])
        we_send[1, i : i + 1, :] = mixed(flips[3], state[i, 15:16, :], state[15 - i, 15:16, :])

    row, col = xh, y
    inner_n, inner_s = (row + 7) // 8, (14 - row) // 8
    inner_w, inner_e = (col + 7) // 8, (14 - col) // 8
    across = (
        (face + 4) % 8,
        7 - face,
        (face + 7 + 2 * (face % 2)) % 8,
        face + 1 - 2 * (face % 2),
    )

    def rim_copies(send, recv, base, stride, low_edge, high_edge, inner_low, inner_high):
        low_to = (
            inner_low * face + (1 - inner_low) * across[low_edge],
            tile - stride * inner_low,
        )
        high_to = (
            inner_high * face + (1 - inner_high) * across[high_edge],
            tile + stride * inner_high,
        )
        low = pltpu.make_async_remote_copy(
            src_ref=send.at[0], dst_ref=recv.at[inner_low], send_sem=ssem.at[base],
            recv_sem=rsem.at[base + inner_low], device_id=low_to, device_id_type=MESH,
        )
        high = pltpu.make_async_remote_copy(
            src_ref=send.at[1], dst_ref=recv.at[1 - inner_high], send_sem=ssem.at[base + 1],
            recv_sem=rsem.at[base + 1 - inner_high], device_id=high_to, device_id_type=MESH,
        )
        return low, high

    def prepare(r, carry):
        rows = state[pl.ds(r * 4, 4)]
        at = pl.ds(1 + r * 4, 4)
        middle[at] = rows
        west[at] = pltpu.roll(rows, 1, 1)
        east[at] = pltpu.roll(rows, 15, 1)
        high, low = split(cot[pl.ds(r * 4, 4)].reshape(64, 256))
        to = pl.ds(pl.multiple_of(r * 64, 64), 64)
        g_hi[0, to, :] = high
        g_lo[0, to, :] = low
        return carry

    lax.fori_loop(0, 4, prepare, 0)

    pl.semaphore_wait(barrier, len(peers) + (1 - ends) * (16 - 8 * same))

    we = rim_copies(we_send, we_recv, S_HALO, 1, 2, 3, inner_w, inner_e)
    for each in we:
        each.start()

    def big(yy, xx):
        return w.at[yy, xx, 2:8]

    def small(yy, xx):
        return w.at[yy, xx, 0:2]

    def own_sends(whole):
        mine = big(y, x) if whole else small(y, x)
        if whole:
            return [copy(mine, mine, S_Y + k, device(x, h, (y + k) % NY, l, c)) for k in NEAR]
        return [copy(mine, mine, S_BX + k, device((x + k) % NX, h, y, l, c)) for k in (1, 3, 2)]

    def cross_sends(whole):
        mine = big(y, x) if whole else small(y, x)
        sends = []
        for k in (0, *NEAR) if whole else (0, 1, 3, 2):
            for m in range(2):
                ll = (3 - m) * (1 - l // 3) + m * (l // 3)
                if whole:
                    to, slot = device(x, 1 - h, (y + k) % NY, ll, c), S_Y + k
                else:
                    to, slot = device((x + k) % NX, 1 - h, y, ll, c), S_BX + k
                sends.append(
                    pltpu.make_async_remote_copy(
                        src_ref=mine, dst_ref=mine, send_sem=ssem.at[S_C + 2 * k + m], recv_sem=rsem.at[slot],
                        device_id=to, device_id_type=MESH,
                    )
                )
        return sends

    def x_sends(k):
        ref = big((y - k + NY) % NY, x)
        return [copy(ref, ref, S_X + 3 * k + dx - 1, device((x + dx) % NX, h, y, l, c)) for dx in (2, 1, 3)]

    def forward(k, whole):
        if k or not whole:
            arrived(big((y - k + NY) % NY, x), S_Y + k)
        for each in x_sends(k):
            each.start()

    def small_sends():
        ref = w.at[y, :, 0:2]
        return [copy(ref, ref, S_BY + k, device(x, h, (y + k) % NY, l, c)) for k in (4, 3, 5, 2, 6, 1, 7)]

    def forward_small(whole):
        for k in range(NX):
            if k or whole:
                arrived(small(y, (x - k + NX) % NX), S_BX + k)
        for each in small_sends():
            each.start()

    def first_leg(whole):
        for each in own_sends(whole):
            each.start()

        @pl.when(ends == 0)
        def _():
            for each in cross_sends(whole):
                each.start()

        if whole:
            forward(0, whole)

    both(first_leg)
    cot_copy = copy(cot, cot_sib, S_COT, sibling)
    cot_copy.start()
    kg1 = []
    for k in range(1, 8):
        dx, dh = k // 2, k % 2
        each = copy(kg_own, kg_xh.at[k], S_KG1 + k, device((x + dx) % NX, (h + dh) % NH, y, l, c))
        each.start()
        kg1.append(each)

    def second_leg(whole):
        if whole:
            forward(1, whole)
            forward(7, whole)
        else:
            forward(0, whole)

    both(second_leg)

    for k in range(2):
        arrived(we_recv.at[k], S_HALO + k)
    for i in range(16):
        west[1 + i, 0:1, :] = we_recv[0, i : i + 1, :]
        east[1 + i, 15:16, :] = we_recv[1, i : i + 1, :]
    for k, (edge, line) in enumerate(((0, 0), (1, 15))):
        first, last = we_recv[0, line : line + 1, :], we_recv[1, line : line + 1, :]
        ns_send[k, 0:1, :] = mixed(flips[edge], first, last)
        ns_send[k, 17:18, :] = mixed(flips[edge], last, first)
        for i in range(16):
            ns_send[k, 1 + i : 2 + i, :] = mixed(
                flips[edge], state[line, i : i + 1, :], state[line, 15 - i : 16 - i, :]
            )
    ns = rim_copies(ns_send, ns_recv, S_HALO + 2, 8, 0, 1, inner_n, inner_s)
    for each in ns:
        each.start()

    def third_leg(whole):
        for k in (2, 6) if whole else (1, 7):
            forward(k, whole)
        forward_small(whole)
        for k in (3, 5) if whole else (2, 6):
            forward(k, whole)

    both(third_leg)

    for k in range(1, 8):
        arrived(kg_xh.at[k], S_KG1 + k)
    total = kg_xh[0]
    for k in range(1, 8):
        total = total + kg_xh[k]
    kg_all[y] = total
    kg2 = []
    for k in range(1, NY):
        mine = kg_all.at[y]
        each = copy(mine, mine, S_KG2 + k, device(x, h, (y + k) % NY, l, c))
        each.start()
        kg2.append(each)

    def fourth_leg(whole):
        for k in (4,) if whole else (3, 5, 4):
            forward(k, whole)

    both(fourth_leg)

    for k in range(1, NY):
        arrived(kg_all.at[(y - k + NY) % NY], S_KG2 + k)
    rows64 = lax.broadcasted_iota(jnp.int32, (64, 256), 0)
    chan = lax.broadcasted_iota(jnp.int32, (64, 256), 1)
    owner = (chan // 4) == ((rows64 % 8) * 8 + rows64 // 8)
    lane = lax.broadcasted_iota(jnp.int32, (64, 128), 1)
    same4 = (
        lax.broadcasted_iota(jnp.int32, (128, 256), 0) // 32
        == lax.broadcasted_iota(jnp.int32, (128, 256), 1) % 4
    )
    spread4 = jnp.where(same4, 1.0, 0.0).astype(BF16)
    tiles = kg_all[...].reshape(64, 128)
    grouped = jnp.concatenate([jnp.where(lane % 32 == k, tiles, 0.0) for k in range(10)], axis=0)
    first, second = split(grouped)
    spread_rows = lax.dot_general(first, spread4, NN, preferred_element_type=F32) + lax.dot_general(
        second, spread4, NN, preferred_element_type=F32
    )
    for k in range(10):
        krows[k : k + 1, :] = jnp.sum(
            jnp.where(owner, spread_rows[64 * k : 64 * k + 64], 0.0), axis=0, keepdims=True
        )

    for k in range(2):
        arrived(ns_recv.at[k], S_HALO + 2 + k)
        line = 17 * k
        west[line] = ns_recv[k, 0:16, :]
        middle[line] = ns_recv[k, 1:17, :]
        east[line] = ns_recv[k, 2:18, :]

    shifted = (west, middle, east)
    taps = [krows[k : k + 1, :] for k in range(9)]
    gain = krows[9:10, :]

    def conv_rows(r, carry):
        acc = jnp.zeros((4, 16, 256), F32)
        for i in range(3):
            for j in range(3):
                acc = acc + krows[3 * i + j : 3 * i + j + 1, :] * shifted[j][pl.ds(r * 4 + i, 4)]
        acc = acc.reshape(64, 256)
        mean = jnp.mean(acc, axis=-1, keepdims=True)
        centred = acc - mean
        var = jnp.mean(centred * centred, axis=-1, keepdims=True)
        inv = lax.rsqrt(var + EPSILON)
        hat = centred * inv
        at = pl.ds(pl.multiple_of(r * 64, 64), 64)
        xhat[at, :] = hat
        rstd[at, :] = jnp.broadcast_to(inv, (64, 128))
        normed = hat * krows[9:10, :]
        norm_own[at, :] = normed
        return carry

    lax.fori_loop(0, 4, conv_rows, 0)
    norm_copy = copy(norm_own, norm_sib, S_NORM, sibling)
    norm_copy.start()

    def prepare_tokens(m, source):
        def halves(r, carry):
            at = pl.ds(pl.multiple_of(r * 128, 128), 128)
            value = source[at, :]
            high, low = split(value)
            n_hi[m, at, :] = high
            n_lo[m, at, :] = low
            high, low = split(jnp.transpose(value))
            nt_hi[m, r] = high
            nt_lo[m, r] = low
            return carry

        lax.fori_loop(0, 2, halves, 0)

    prepare_tokens(0, norm_own)

    for k in NEAR:
        arrived(w.at[(y - k + NY) % NY, :, 0:2], S_BY + k)
    for k in (0, *NEAR):
        for dx in (1, 3, 2):
            arrived(big((y - k + NY) % NY, (x - dx + NX) % NX), S_X + 3 * k + dx - 1)

    lows = lax.broadcasted_iota(jnp.int32, (4, 8, 128), 1) < 4

    def unpack(xs, carry):
        for r in range(2):
            hs = r * c + (1 - r) * (1 - c)
            at = pl.ds(pl.multiple_of(xs * 64 + hs * 32, 32), 32)
            for e in range(2):
                v = w[:, xs, 2 * r + e].reshape(4, 2, 8, 128)
                a, b = v[:, 0], v[:, 1]
                for bb, value in (
                    (0, jnp.where(lows, a, pltpu.roll(b, 4, 1))),
                    (1, jnp.where(lows, pltpu.roll(a, 4, 1), b)),
                ):
                    high, low = split(value.reshape(32, 128))
                    u_hi[e, at, 128 * bb : 128 * bb + 128] = high
                    u_lo[e, at, 128 * bb : 128 * bb + 128] = low
        at = pl.ds(pl.multiple_of((xs % 2) * 128, 128), 128)
        for q in range(2):
            value = jnp.concatenate([w[:, xs, 4 + q], w[:, xs, 6 + q]], axis=1).reshape(128, 128)
            high, low = split(value)
            d_hi[xs // 2, at, 128 * q : 128 * q + 128] = high
            d_lo[xs // 2, at, 128 * q : 128 * q + 128] = low
        return carry

    lax.fori_loop(0, NX, unpack, 0)

    arrived(cot_sib, S_COT)

    def prepare_cot(r, carry):
        high, low = split(cot_sib[pl.ds(r * 4, 4)].reshape(64, 256))
        to = pl.ds(pl.multiple_of(r * 64, 64), 64)
        g_hi[1, to, :] = high
        g_lo[1, to, :] = low
        return carry

    lax.fori_loop(0, 4, prepare_cot, 0)
    arrived(norm_sib, S_NORM)
    prepare_tokens(1, norm_sib)

    def first_products(e, carry):
        downs = (d_hi[e], d_lo[e])
        ups = (u_hi[e], u_lo[e])
        total = jnp.zeros((256, 256), F32)
        for m in range(2):
            grads = (g_hi[m], g_lo[m])
            pre = dot3((n_hi[m], n_lo[m]), ups, NN)
            back = dot3(grads, downs, NT)
            square = pre * pre
            t = jnp.tanh(ROOT * (pre + 0.044715 * (square * pre)))
            half = 0.5 * (1.0 + t)
            hidden = pre * half
            slope = half + 0.5 * pre * (1.0 - t * t) * (ROOT * (1.0 + 3 * 0.044715 * square))
            high, low = split(back * slope)
            p_hi[m, e] = high
            p_lo[m, e] = low
            high, low = split(hidden)
            h_hi[m, e] = high
            h_lo[m, e] = low
            total = total + dot3(split(jnp.transpose(hidden)), grads, NN)
        for bb in range(2):
            for q in range(2):
                v = total[128 * bb : 128 * bb + 128, 128 * q : 128 * q + 128].reshape(8, 2, 8, 128)
                for rh in range(2):
                    g[:, 2 * e + bb, 4 + 2 * rh + q] = v[:, rh]
        return carry

    lax.fori_loop(0, 2, first_products, 0)

    reduces = []
    for k, offset in enumerate(FAR):
        yy = (y + offset) % NY
        for dx in (2, 1, 3):
            to = (x + dx) % NX
            each = copy(
                g.at[yy, to, 4:8], x_recv.at[k, dx - 1], R_X + 3 * k + dx - 1, device(to, h, y, l, c)
            )
            each.start()
            reduces.append(each)

    def second_products(e, carry):
        ugrad[e] = sum(
            dot3((nt_hi[m, r], nt_lo[m, r]), (p_hi[m, e, 128 * r : 128 * r + 128], p_lo[m, e, 128 * r : 128 * r + 128]), NN)
            for m in range(2)
            for r in range(2)
        )
        return carry

    lax.fori_loop(0, 2, second_products, 0)

    def pack(xs, carry):
        for r in range(2):
            hs = r * c + (1 - r) * (1 - c)
            at = pl.ds(pl.multiple_of(xs * 64 + hs * 32, 32), 32)
            for e in range(2):
                v0 = ugrad[e, at, 0:128].reshape(4, 8, 128)
                v1 = ugrad[e, at, 128:256].reshape(4, 8, 128)
                even = jnp.where(lows, v0, pltpu.roll(v1, 4, 1))
                odd = jnp.where(lows, pltpu.roll(v0, 4, 1), v1)
                g[:, xs, 2 * r + e] = jnp.concatenate([even[:, None], odd[:, None]], axis=1).reshape(8, 8, 128)
        return carry

    lax.fori_loop(0, NX, pack, 0)
    for k in (4, 3, 5, 2, 6, 1, 7):
        yy = (y + k) % NY
        each = copy(g.at[yy, :, 0:2], by_recv.at[k], R_BY + k, device(x, h, yy, l, c))
        each.start()
        reduces.append(each)
    for k, offset in enumerate(FAR):
        yy = (y + offset) % NY
        for dx in (2, 1, 3):
            to = (x + dx) % NX
            each = copy(
                g.at[yy, to, 2:4], xu_recv.at[k, dx - 1], R_XU + 3 * k + dx - 1, device(to, h, y, l, c)
            )
            each.start()
            reduces.append(each)

    swaps = [copy(dnorm.at[1], dn_recv, R_BR, sibling), copy(branch.at[1], br_recv, R_BR + 1, sibling)]
    for m in (1, 0):
        dnorm[m] = sum(dot3((p_hi[m, e], p_lo[m, e]), (u_hi[e], u_lo[e]), NT) for e in range(2))
        if m:
            swaps[0].start()
    for m in (1, 0):
        branch[m] = sum(dot3((h_hi[m, e], h_lo[m, e]), (d_hi[e], d_lo[e]), NN) for e in range(2))
        if m:
            swaps[1].start()

    zpad[0:2] = jnp.zeros((2, 16, 256), F32)
    zpad[18:20] = jnp.zeros((2, 16, 256), F32)
    arrived(dn_recv, R_BR)

    def norm_rows(r, sums):
        at = pl.ds(pl.multiple_of(r * 32, 32), 32)
        hat = xhat[at, :]
        inv = rstd[at, :][:, 0:1]
        dn = dnorm[0, at, :] + dn_recv[at, :]
        dhat = dn * krows[9:10, :]
        mean = jnp.mean(dhat, axis=-1, keepdims=True)
        cross = jnp.mean(dhat * hat, axis=-1, keepdims=True)
        dd = (inv * (dhat - mean - hat * cross)).reshape(2, 16, 256)
        zpad[pl.ds(r * 2 + 2, 2)] = dd
        fresh = []
        for i in range(3):
            for j in range(3):
                v = (dd * shifted[j][pl.ds(r * 2 + i, 2)]).reshape(4, 8, 256)
                fresh.append(sums[3 * i + j] + ((v[0] + v[1]) + (v[2] + v[3])))
        v = (dn * hat).reshape(4, 8, 256)
        fresh.append(sums[9] + ((v[0] + v[1]) + (v[2] + v[3])))
        return tuple(fresh)

    sums = lax.fori_loop(0, 8, norm_rows, tuple(jnp.zeros((8, 256), F32) for _ in range(10)))

    lanes16 = lax.broadcasted_iota(jnp.int32, (2, 16, 256), 1)

    def back_rows(r, carry):
        parts = []
        for j in range(3):
            acc = jnp.zeros((2, 16, 256), F32)
            for i in range(3):
                acc = acc + krows[3 * i + j : 3 * i + j + 1, :] * zpad[pl.ds(r * 2 + 2 - i, 2)]
            parts.append(acc)
        to = pl.ds(r * 2, 2)
        left = jnp.where(lanes16 < 15, pltpu.roll(parts[0], 15, 1), 0.0)
        right = jnp.where(lanes16 > 0, pltpu.roll(parts[2], 1, 1), 0.0)
        centre[to] = parts[1] + (left + right)
        wcol[to] = parts[0][:, 0:1, :]
        ecol[to] = parts[2][:, 15:16, :]
        return carry

    lax.fori_loop(0, 9, back_rows, 0)
    for k, (edge, line) in enumerate(((0, 0), (1, 17))):
        first, last = wcol[line], ecol[line]
        bns_send[k, 0:1, :] = mixed(flips[edge], first, last)
        bns_send[k, 17:18, :] = mixed(flips[edge], last, first)
        for i in range(16):
            bns_send[k, 1 + i : 2 + i, :] = mixed(
                flips[edge], centre[line, i : i + 1, :], centre[line, 15 - i : 16 - i, :]
            )
    bns = rim_copies(bns_send, bns_recv, R_HALO, 8, 0, 1, inner_n, inner_s)
    for each in bns:
        each.start()

    grad_rows = [jnp.sum(sums[k], axis=0, keepdims=True) for k in range(10)]
    grouped = jnp.concatenate([jnp.where(owner, jnp.broadcast_to(v, (64, 256)), 0.0) for v in grad_rows], axis=0)
    first, second = split(grouped)
    fold = lax.dot_general(first, spread4, NT, preferred_element_type=F32) + lax.dot_general(
        second, spread4, NT, preferred_element_type=F32
    )
    folded = jnp.zeros((64, 128), F32)
    for k in range(10):
        folded = folded + jnp.where(lane % 32 == k, fold[64 * k : 64 * k + 64], 0.0)
    kgr_own[...] = folded.reshape(8, 8, 128)
    kgs = []
    for k in range(1, NY):
        yy = (y + k) % NY
        each = copy(kgr_own.at[yy], kgr_y.at[k], R_KY + k, device(x, h, yy, l, c))
        each.start()
        kgs.append(each)

    for k in range(1, NY):
        arrived(by_recv.at[k], R_BY + k)
    total = g[y, :, 0:2]
    for k in range(1, NY):
        total = total + by_recv[k]
    g[y, :, 0:2] = total
    for dx in (2, 1, 3):
        to = (x + dx) % NX
        each = copy(g.at[y, to, 0:2], bx_recv.at[dx], R_BX + dx, device(to, h, y, l, c))
        each.start()
        reduces.append(each)

    for k, offset in enumerate(FAR):
        yy = (y + offset) % NY
        for dx in (1, 3, 2):
            arrived(x_recv.at[k, dx - 1], R_X + 3 * k + dx - 1)
            arrived(xu_recv.at[k, dx - 1], R_XU + 3 * k + dx - 1)
        g[yy, x, 4:8] = (g[yy, x, 4:8] + x_recv[k, 0]) + (x_recv[k, 1] + x_recv[k, 2])
        g[yy, x, 2:4] = (g[yy, x, 2:4] + xu_recv[k, 0]) + (xu_recv[k, 1] + xu_recv[k, 2])
        if offset:
            each = copy(g.at[yy, x, 2:8], y_recv.at[offset], R_Y + offset, device(x, h, yy, l, c))
            each.start()
            reduces.append(each)

    arrived(br_recv, R_BR + 1)

    def new_rows(r, carry):
        at = pl.ds(pl.multiple_of(r * 64, 64), 64)
        value = branch[0, at, :] + br_recv[at, :]
        to = pl.ds(r * 4, 4)
        out_new[to] = state[to] + value.reshape(4, 16, 256)
        return carry

    lax.fori_loop(0, 4, new_rows, 0)
    stores = [pltpu.make_async_copy(out_new, new_out, rsem.at[S_OUT])]
    stores[0].start()

    for k, line in enumerate((1, 16)):
        arrived(bns_recv.at[k], R_HALO + k)
        wcol[line] = wcol[line] + bns_recv[k, 0:1, :]
        centre[line] = centre[line] + bns_recv[k, 1:17, :]
        ecol[line] = ecol[line] + bns_recv[k, 17:18, :]
    for i in range(16):
        bwe_send[0, i : i + 1, :] = mixed(flips[2], wcol[1 + i], wcol[16 - i])
        bwe_send[1, i : i + 1, :] = mixed(flips[3], ecol[1 + i], ecol[16 - i])
    bwe = rim_copies(bwe_send, bwe_recv, R_HALO + 2, 1, 2, 3, inner_w, inner_e)
    for each in bwe:
        each.start()

    for k in range(1, NY):
        arrived(kgr_y.at[k], R_KY + k)
    total = kgr_own[y]
    for k in range(1, NY):
        total = total + kgr_y[k]
    kgr_x[x] = total
    for k in range(1, NX):
        each = copy(kgr_x.at[x], kgr_x.at[x], R_KX + k, device((x + k) % NX, h, y, l, c))
        each.start()
        kgs.append(each)

    for k in range(1, NY):
        arrived(y_recv.at[k], R_Y + k)
    total = g[y, x, 2:8]
    for k in range(1, NY):
        total = total + y_recv[k]
    z_recv[z, 2:8] = total
    for dx in range(1, NX):
        arrived(bx_recv.at[dx], R_BX + dx)
    z_recv[z, 0:2] = (g[y, x, 0:2] + bx_recv[1]) + (bx_recv[2] + bx_recv[3])

    def z_sends(whole):
        sends = []
        for k in range(1, 8):
            dh, dl = k // 4, k % 4
            full = whole if dh == 0 else not whole
            ref = z_recv.at[z, 2:8] if full else z_recv.at[z, 0:2]
            sends.append(copy(ref, ref, R_Z + k, device(x, (h + dh) % NH, y, (l + dl) % NL, c)))
        return sends

    def z_start(whole):
        for each in z_sends(whole):
            each.start()

    both(z_start)

    for k in range(1, NX):
        arrived(kgr_x.at[(x - k + NX) % NX], R_KX + k)
    total = kgr_x[0]
    for k in range(1, NX):
        total = total + kgr_x[k]
    zc = z * 2 + c
    kgr_z[zc] = total
    for k in range(1, 16):
        to = device(x, (h + k // 8) % 2, y, (l + (k // 2) % 4) % 4, (c + k % 2) % 2)
        each = copy(kgr_z.at[zc], kgr_z.at[zc], R_KZ + k, to)
        each.start()
        kgs.append(each)

    for k in range(2):
        arrived(bwe_recv.at[k], R_HALO + 2 + k)
    for i in range(16):
        centre[1 + i, 0:1, :] = centre[1 + i, 0:1, :] + bwe_recv[0, i : i + 1, :]
        centre[1 + i, 15:16, :] = centre[1 + i, 15:16, :] + bwe_recv[1, i : i + 1, :]
        out_field[i] = centre[1 + i] + cot[i]
    stores.append(pltpu.make_async_copy(out_field, field_out, rsem.at[S_OUT + 1]))
    stores[1].start()

    def fin_sends(whole):
        sends = [copy(fin_up.at[c], fin_up.at[c], R_F, sibling)]
        if whole:
            sends.append(copy(fin_down, fin_down, R_F + 1, sibling))
        return sends

    def z_end(whole):
        for k in range(1, 8):
            zz = ((h + k // 4) % NH) * 4 + (l - k % 4 + NL) % NL
            arrived(z_recv.at[zz, 2:8] if whole else z_recv.at[zz, 0:2], R_Z + k)
        span = slice(2, 8) if whole else slice(0, 2)
        total = z_recv[0, span]
        for zz in range(1, 8):
            total = total + z_recv[zz, span]
        fin_up[c] = total[0:2]
        if whole:
            fin_down[...] = total[2:6]
        for each in fin_sends(whole):
            each.start()
        arrived(fin_up.at[1 - c], R_F)
        if not whole:
            arrived(fin_down, R_F + 1)

    both(z_end)
    for cc in range(2):
        for e in range(2):
            v = fin_up[cc, e]
            for bb in range(2):
                first = 128 * (2 * (2 * e + bb) + cc)
                out_up[:, first : first + 128] = v[4 * bb : 4 * bb + 4]
    for rh in range(2):
        for q in range(2):
            out_down[8 * rh : 8 * rh + 8, 128 * q : 128 * q + 128] = fin_down[2 * rh + q]
    stores.append(pltpu.make_async_copy(out_up, up_out, rsem.at[S_OUT + 2]))
    stores.append(pltpu.make_async_copy(out_down, down_out, rsem.at[S_OUT + 3]))
    stores[2].start()
    stores[3].start()

    for k in range(1, 16):
        hh, ll, cc = (h + k // 8) % 2, (l - (k // 2) % 4 + 4) % 4, (c + k % 2) % 2
        arrived(kgr_z.at[(hh * 4 + ll) * 2 + cc], R_KZ + k)
    total = kgr_z[0]
    for k in range(1, 16):
        total = total + kgr_z[k]
    out_kg[...] = jnp.sum(jnp.where(sub8 == xh, total, 0.0), axis=0, keepdims=True)
    stores.append(pltpu.make_async_copy(out_kg, kg_out, rsem.at[S_OUT + 4]))
    stores[4].start()

    def all_sent(whole):
        for each in own_sends(whole) + z_sends(whole) + fin_sends(whole):
            each.wait_send()

        @pl.when(ends == 0)
        def _():
            for each in cross_sends(whole):
                each.wait_send()

    both(all_sent)
    for k in range(NY):
        for each in x_sends(k):
            each.wait_send()
    for each in [
        *small_sends(), *we, *kg1, *ns, *kg2, cot_copy, norm_copy, *swaps, *reduces, *bns, *kgs, *bwe
    ]:
        each.wait_send()
    for each in stores:
        each.wait()


def results(
    new, field, up, down, kg, out_new, out_field, out_up, out_down, out_kt, out_gn,
    v_new, v_field, v_up, v_down, v_kg, v_kt, v_gn, sem,
):
    held = (v_kg, v_new, v_field, v_up, v_down)
    reads = [pltpu.make_async_copy(src, dst, sem.at[k]) for k, (src, dst) in enumerate(zip((kg, new, field, up, down), held))]
    writes = [
        pltpu.make_async_copy(src, dst, sem.at[5 + k])
        for k, (src, dst) in enumerate(
            ((v_new, out_new), (v_field, out_field), (v_up, out_up), (v_down, out_down), (v_kt, out_kt), (v_gn, out_gn))
        )
    ]
    for each in reads:
        each.start()
    reads[0].wait()
    for i in range(4):
        moved = v_kg[...] if i == 0 else pltpu.roll(v_kg[...], 128 - 32 * i, 1)
        v_kt[i : i + 1, :] = moved[:, 0:9]
        v_gn[0:1, i : i + 1] = moved[:, 9:10]
    writes[4].start()
    writes[5].start()
    for k in range(4):
        reads[1 + k].wait()
        writes[k].start()
    for each in writes:
        each.wait()


def shards(state_field, out_grad, depth_kernel, norm_gain, up_weight, down_weight, seam_code):
    anywhere = pl.BlockSpec(memory_space=pl.ANY)

    def buf(*shape, dtype=F32):
        return pltpu.VMEM(shape, dtype)

    def half(*shape):
        return pltpu.VMEM(shape, BF16)

    found = pl.pallas_call(
        kernel,
        out_shape=(
            jax.ShapeDtypeStruct((16, 16, 256), F32),
            jax.ShapeDtypeStruct((16, 16, 256), F32),
            jax.ShapeDtypeStruct((4, 1024), F32),
            jax.ShapeDtypeStruct((16, 256), F32),
            jax.ShapeDtypeStruct((1, 128), F32),
        ),
        in_specs=[anywhere] * 6 + [pl.BlockSpec(memory_space=pltpu.SMEM)],
        out_specs=(anywhere,) * 5,
        scratch_shapes=[
            buf(16, 16, 256), buf(16, 16, 256), buf(4, 1024), buf(16, 256), buf(4, 9), buf(1, 4),
            buf(16, 16, 256), buf(16, 16, 256), buf(4, 1024), buf(16, 256), buf(1, 128),
            buf(8, 4, 8, 8, 128), buf(8, 4, 8, 8, 128),
            buf(18, 16, 256), buf(18, 16, 256), buf(18, 16, 256),
            buf(20, 16, 256), buf(18, 16, 256), buf(18, 1, 256), buf(18, 1, 256),
            buf(2, 18, 256), buf(2, 18, 256), buf(2, 16, 256), buf(2, 16, 256),
            buf(2, 18, 256), buf(2, 18, 256), buf(2, 16, 256), buf(2, 16, 256),
            buf(8, 128), buf(8, 128), buf(8, 8, 128), buf(8, 8, 128),
            buf(8, 8, 128), buf(8, 8, 128), buf(4, 8, 128), buf(16, 8, 128),
            half(2, 256, 256), half(2, 256, 256), half(2, 256, 256), half(2, 256, 256),
            buf(256, 256), buf(256, 128), buf(256, 256), buf(256, 256), buf(16, 16, 256),
            half(2, 256, 256), half(2, 256, 256), half(2, 2, 256, 128), half(2, 2, 256, 128),
            half(2, 256, 256), half(2, 256, 256),
            half(2, 2, 256, 256), half(2, 2, 256, 256), half(2, 2, 256, 256), half(2, 2, 256, 256),
            buf(2, 256, 256), buf(2, 256, 256), buf(256, 256), buf(256, 256),
            buf(2, 256, 256), buf(2, 256, 256), buf(16, 256),
            buf(8, 3, 4, 8, 128), buf(8, 3, 2, 8, 128), buf(8, 6, 8, 128),
            buf(8, 4, 2, 8, 128), buf(4, 2, 8, 128), buf(8, 8, 8, 128),
            buf(2, 2, 8, 128), buf(4, 8, 128),
            pltpu.SemaphoreType.DMA((N_SLOTS,)),
            pltpu.SemaphoreType.DMA((N_SLOTS,)),
        ],
        compiler_params=pltpu.CompilerParams(
            collective_id=0, has_side_effects=True, vmem_limit_bytes=60 * 1024 * 1024
        ),
        name="block",
    )(
        state_field[0, 0], out_grad[0, 0], up_weight, down_weight,
        depth_kernel.T, norm_gain.reshape(1, 4), seam_code[0],
    )
    new, field, up, down, kt, gn = pl.pallas_call(
        results,
        out_shape=(
            jax.ShapeDtypeStruct((16, 16, 256), F32),
            jax.ShapeDtypeStruct((16, 16, 256), F32),
            jax.ShapeDtypeStruct((4, 1024), F32),
            jax.ShapeDtypeStruct((16, 256), F32),
            jax.ShapeDtypeStruct((4, 9), F32),
            jax.ShapeDtypeStruct((1, 4), F32),
        ),
        in_specs=[anywhere] * 5,
        out_specs=(anywhere,) * 6,
        scratch_shapes=[
            buf(16, 16, 256), buf(16, 16, 256), buf(4, 1024), buf(16, 256), buf(1, 128), buf(4, 9), buf(1, 4),
            pltpu.SemaphoreType.DMA((11,)),
        ],
        compiler_params=pltpu.CompilerParams(vmem_limit_bytes=60 * 1024 * 1024),
        name="results",
    )(*found)
    return (new[None, None], field[None, None], kt.T, gn.reshape(4), up, down)


def solution(mesh):
    placed = (
        P("face", "tile", None, None, None),
        P("face", "tile", None, None, None),
        P(None, "tile"),
        P("tile"),
        P("tile", None),
        P("tile", None),
        P("face", "tile", None),
    )
    return jax.shard_map(
        shards,
        mesh=mesh,
        in_specs=placed,
        out_specs=(
            P("face", "tile", None, None, None),
            P("face", "tile", None, None, None),
            P(None, "tile"),
            P("tile"),
            P("tile", None),
            P("tile", None),
        ),
        check_vma=False,
    )
```

```python
import functools
import math

import jax
import jax.numpy as jnp
from jax import lax
from jax.experimental import pallas as pl
from jax.experimental.pallas import tpu as pltpu
from jax.sharding import PartitionSpec as P

EPSILON = 1e-06
NX, NH, NY, NL, NC = 4, 2, 8, 4, 2
MESH = pl.DeviceIdType.MESH
F32, BF16 = jnp.float32, jnp.bfloat16
ROOT = math.sqrt(2.0 / math.pi)
NN = (((1,), (0,)), ((), ()))
NT = (((1,), (1,)), ((), ()))


class Slots:
    def __init__(self):
        self.used = 0

    def take(self, count):
        first = self.used
        self.used += count
        return first


SLOTS = Slots()
S_Y = SLOTS.take(8)
S_C = SLOTS.take(16)
S_X = SLOTS.take(24)
S_BX = SLOTS.take(8)
S_BY = SLOTS.take(8)
S_IN = SLOTS.take(6)
S_OUT = SLOTS.take(5)
S_COT = SLOTS.take(1)
S_NORM = SLOTS.take(4)
S_KG1 = SLOTS.take(8)
S_KG2 = SLOTS.take(8)
S_HALO = SLOTS.take(4)
R_X = SLOTS.take(6)
R_XU = SLOTS.take(6)
R_BY = SLOTS.take(8)
R_BX = SLOTS.take(4)
R_Y = SLOTS.take(8)
R_Z = SLOTS.take(8)
R_F = SLOTS.take(2)
R_BR = SLOTS.take(2)
R_KY = SLOTS.take(8)
R_KX = SLOTS.take(4)
R_KZ = SLOTS.take(16)
R_HALO = SLOTS.take(4)
N_SLOTS = SLOTS.used

NEAR = (1, 7, 2, 6, 3, 5, 4)


def split(value):
    high = value.astype(BF16)
    return high, (value - high.astype(F32)).astype(BF16)


def dot3(a, b, dims):
    def one(p, q):
        return lax.dot_general(p, q, dims, preferred_element_type=F32)

    return one(a[0], b[0]) + (one(a[0], b[1]) + one(a[1], b[0]))


def kernel(
    state_in, cot_in, up_in, down_in, kt_in, gn_in, code,
    new_out, field_out, up_out, down_out, kg_out,
    state, cot, up, down, kt, gn, out_new, out_field, out_up, out_down, out_kg,
    w, g, west, middle, east, zpad, centre, wcol, ecol,
    ns_send, ns_recv, we_send, we_recv, bns_send, bns_recv, bwe_send, bwe_recv,
    kg_row, kg_own, kg_xh, kg_all, kgr_own, kgr_y, kgr_x, kgr_z,
    u_hi, u_lo, d_hi, d_lo, xhat, rstd, norm_own, norm_sib, cot_sib,
    n_hi, n_lo, nt_hi, nt_lo, g_hi, g_lo, h_hi, h_lo, p_hi, p_lo, branch, dnorm, br_recv, dn_recv, ugrad, dgrad, krows,
    x_recv, xu_recv, y_recv, by_recv, bx_recv, z_recv, fin_up, fin_down,
    ssem, rsem,
):
    face, tile = lax.axis_index("face"), lax.axis_index("tile")
    l, c = face // 2, face % 2
    x, h, y = tile // 16, (tile // 8) % 2, tile % 8
    xs_at = [x] + [(x + k) % NX for k in range(1, NX)]
    ys_at = [y] + [(y + k) % NY for k in range(1, NY)]
    hs_at = [h, 1 - h]
    ls_at = [l] + [(l + k) % NL for k in range(1, NL)]
    cs_at = [c, 1 - c]
    cross_l = [(3 - m) * (1 - l // 3) + m * (l // 3) for m in range(2)]
    source = 3 * (1 - l // 2)
    known = {}

    def device(x, h, y, l, c):
        key = (id(x), id(h), id(y), id(l), id(c))
        return known[key] if key in known else (l * NC + c, (x * NH + h) * NY + y)

    def remember(*place):
        known[tuple(id(v) for v in place)] = device(*place)

    for k in range(NY):
        remember(x, h, ys_at[k], l, c)
        for ll in (*cross_l, source):
            remember(x, hs_at[1], ys_at[k], ll, c)
    for k in range(NX):
        for hh in hs_at:
            remember(xs_at[k], hh, y, l, c)
        for ll in (*cross_l, source):
            remember(xs_at[k], hs_at[1], y, ll, c)
    for hh in hs_at:
        for ll in ls_at:
            for cc in cs_at:
                remember(x, hh, y, ll, cc)
    xh = x * 2 + h
    z = h * 4 + l
    same = (h + c) % 2
    ends = (l % 3 + 1) // 2

    def copy(src, dst, slot, to, send_slot=None):
        return pltpu.make_async_remote_copy(
            src_ref=src, dst_ref=dst,
            send_sem=ssem.at[slot if send_slot is None else send_slot], recv_sem=rsem.at[slot],
            device_id=to, device_id_type=MESH,
        )

    sibling = device(x, h, y, l, cs_at[1])

    def arrived(dst, slot):
        copy(dst, dst, slot, sibling).wait_recv()

    def both(fn):
        pl.when(same == 0)(functools.partial(fn, True))
        pl.when(same == 1)(functools.partial(fn, False))

    barrier = pltpu.get_barrier_semaphore()
    peers = []
    for k in range(1, 16):
        peers.append(device(x, hs_at[k // 8], y, ls_at[(k // 2) % 4], cs_at[k % 2]))
    for k in range(1, NY):
        peers.append(device(x, h, ys_at[k], l, c))
    for dx in range(1, NX):
        for dh in range(NH):
            peers.append(device(xs_at[dx], hs_at[dh], y, l, c))
    loads = [
        pltpu.make_async_copy(src, dst, ssem.at[S_IN + k])
        for k, (src, dst) in enumerate(
            ((state_in, state), (kt_in, kt), (gn_in, gn), (up_in, up), (down_in, down), (cot_in, cot))
        )
    ]
    for each in loads:
        each.start()

    def greet(peer):
        pl.semaphore_signal(barrier, inc=1, device_id=peer, device_id_type=MESH)

    for peer in peers:
        greet(peer)
    def greet_sources(whole):
        if whole:
            for k in range(NX):
                greet(device(xs_at[k], hs_at[1], y, source, c))
        else:
            for k in range(NY):
                greet(device(x, hs_at[1], ys_at[k], source, c))

    both(greet_sources)
    for each in loads:
        each.wait()

    def own_up(core, first):
        for e in range(2):
            low, high = (128 * (2 * (2 * e + bb) + core) for bb in range(2))
            w[y, x, first + e] = jnp.concatenate([up[:, low : low + 128], up[:, high : high + 128]], axis=0)

    def own_down():
        for rh in range(2):
            for q in range(2):
                w[y, x, 4 + 2 * rh + q] = down[8 * rh : 8 * rh + 8, 128 * q : 128 * q + 128]

    for core in range(2):
        for kind in range(2):

            def own(core=core, kind=kind):
                own_up(core, 2 if kind == 0 else 0)
                if kind == 0:
                    own_down()

            pl.when((c * 2 + same) == (core * 2 + kind))(own)

    sub8 = lax.broadcasted_iota(jnp.int32, (8, 128), 0)
    kg_row[...] = jnp.zeros_like(kg_row)
    for i in range(4):
        kg_row[i : i + 1, 0:9] = kt[i : i + 1, :]
        kg_row[i : i + 1, 9:10] = gn[0:1, i : i + 1]
    packed = kg_row[0:1, :]
    for i in range(1, 4):
        packed = packed + pltpu.roll(kg_row[i : i + 1, :], 32 * i, 1)
    kg_tile = jnp.where(sub8 == xh, jnp.broadcast_to(packed, (8, 128)), 0.0)
    kg_own[...] = kg_tile
    kg_xh[0] = kg_tile

    flips = [code[0, e].astype(F32) for e in range(4)]

    def mixed(flip, a, b):
        return a * (1.0 - flip) + b * flip

    for i in range(16):
        we_send[0, i : i + 1, :] = mixed(flips[2], state[i, 0:1, :], state[15 - i, 0:1, :])
        we_send[1, i : i + 1, :] = mixed(flips[3], state[i, 15:16, :], state[15 - i, 15:16, :])

    row, col = xh, y
    inner_n, inner_s = (row + 7) // 8, (14 - row) // 8
    inner_w, inner_e = (col + 7) // 8, (14 - col) // 8
    across = (
        (face + 4) % 8,
        7 - face,
        (face + 7 + 2 * (face % 2)) % 8,
        face + 1 - 2 * (face % 2),
    )

    def rim_copies(send, recv, base, stride, low_edge, high_edge, inner_low, inner_high):
        low_to = (
            inner_low * face + (1 - inner_low) * across[low_edge],
            tile - stride * inner_low,
        )
        high_to = (
            inner_high * face + (1 - inner_high) * across[high_edge],
            tile + stride * inner_high,
        )
        low = pltpu.make_async_remote_copy(
            src_ref=send.at[0], dst_ref=recv.at[inner_low], send_sem=ssem.at[base],
            recv_sem=rsem.at[base + inner_low], device_id=low_to, device_id_type=MESH,
        )
        high = pltpu.make_async_remote_copy(
            src_ref=send.at[1], dst_ref=recv.at[1 - inner_high], send_sem=ssem.at[base + 1],
            recv_sem=rsem.at[base + 1 - inner_high], device_id=high_to, device_id_type=MESH,
        )
        return low, high

    def prepare(r, carry):
        rows = state[pl.ds(r * 4, 4)]
        at = pl.ds(1 + r * 4, 4)
        middle[at] = rows
        west[at] = pltpu.roll(rows, 1, 1)
        east[at] = pltpu.roll(rows, 15, 1)
        high, low = split(cot[pl.ds(r * 4, 4)].reshape(64, 256))
        to = pl.ds(pl.multiple_of(r * 64, 64), 64)
        g_hi[0, to, :] = high
        g_lo[0, to, :] = low
        return carry

    lax.fori_loop(0, 4, prepare, 0)

    pl.semaphore_wait(barrier, len(peers) + (1 - ends) * (16 - 8 * same))

    we = rim_copies(we_send, we_recv, S_HALO, 1, 2, 3, inner_w, inner_e)
    for each in we:
        each.start()

    def big(yy, xx):
        return w.at[yy, xx, 2:8]

    def small(yy, xx):
        return w.at[yy, xx, 0:2]

    def own_sends(whole):
        mine = big(y, x) if whole else small(y, x)
        if whole:
            return [copy(mine, mine, S_Y + k, device(x, h, ys_at[k], l, c)) for k in NEAR]
        return [copy(mine, mine, S_BX + k, device(xs_at[k], h, y, l, c)) for k in (1, 3, 2)]

    def cross_sends(whole):
        mine = big(y, x) if whole else small(y, x)
        sends = []
        for k in (0, *NEAR) if whole else (0, 1, 3, 2):
            for m in range(2):
                ll = cross_l[m]
                if whole:
                    to, slot = device(x, hs_at[1], ys_at[k], ll, c), S_Y + k
                else:
                    to, slot = device(xs_at[k], hs_at[1], y, ll, c), S_BX + k
                sends.append(
                    pltpu.make_async_remote_copy(
                        src_ref=mine, dst_ref=mine, send_sem=ssem.at[S_C + 2 * k + m], recv_sem=rsem.at[slot],
                        device_id=to, device_id_type=MESH,
                    )
                )
        return sends

    def x_sends(k):
        ref = big(ys_at[-k % NY], x)
        return [copy(ref, ref, S_X + 3 * k + dx - 1, device(xs_at[dx], h, y, l, c)) for dx in (2, 1, 3)]

    def forward(k, whole):
        if k or not whole:
            arrived(big(ys_at[-k % NY], x), S_Y + k)
        for each in x_sends(k):
            each.start()

    def small_sends():
        ref = w.at[y, :, 0:2]
        return [copy(ref, ref, S_BY + k, device(x, h, ys_at[k], l, c)) for k in (4, 3, 5, 2, 6, 1, 7)]

    def forward_small(whole):
        for k in range(NX):
            if k or whole:
                arrived(small(y, xs_at[-k % NX]), S_BX + k)
        for each in small_sends():
            each.start()

    def first_leg(whole):
        for each in own_sends(whole):
            each.start()

        @pl.when(ends == 0)
        def _():
            for each in cross_sends(whole):
                each.start()

        if whole:
            forward(0, whole)

    both(first_leg)
    cot_copy = copy(cot, cot_sib, S_COT, sibling)
    cot_copy.start()
    kg1 = []
    for k in range(1, 8):
        dx, dh = k // 2, k % 2
        each = copy(kg_own, kg_xh.at[k], S_KG1 + k, device(xs_at[dx], hs_at[dh], y, l, c))
        each.start()
        kg1.append(each)

    def second_leg(whole):
        if whole:
            forward(1, whole)
            forward(7, whole)
        else:
            forward(0, whole)

    both(second_leg)

    for k in range(2):
        arrived(we_recv.at[k], S_HALO + k)
    for i in range(16):
        west[1 + i, 0:1, :] = we_recv[0, i : i + 1, :]
        east[1 + i, 15:16, :] = we_recv[1, i : i + 1, :]
    for k, (edge, line) in enumerate(((0, 0), (1, 15))):
        first, last = we_recv[0, line : line + 1, :], we_recv[1, line : line + 1, :]
        ns_send[k, 0:1, :] = mixed(flips[edge], first, last)
        ns_send[k, 17:18, :] = mixed(flips[edge], last, first)
        for i in range(16):
            ns_send[k, 1 + i : 2 + i, :] = mixed(
                flips[edge], state[line, i : i + 1, :], state[line, 15 - i : 16 - i, :]
            )
    ns = rim_copies(ns_send, ns_recv, S_HALO + 2, 8, 0, 1, inner_n, inner_s)
    for each in ns:
        each.start()

    def third_leg(whole):
        for k in (2, 6) if whole else (1, 7):
            forward(k, whole)
        forward_small(whole)

    both(third_leg)

    for k in range(1, 8):
        arrived(kg_xh.at[k], S_KG1 + k)
    total = kg_xh[0]
    for k in range(1, 8):
        total = total + kg_xh[k]
    kg_all[y] = total
    kg2 = []
    for k in range(1, NY):
        mine = kg_all.at[y]
        each = copy(mine, mine, S_KG2 + k, device(x, h, ys_at[k], l, c))
        each.start()
        kg2.append(each)

    def fourth_leg(whole):
        for k in (3, 5, 4) if whole else (2, 6, 3, 5, 4):
            forward(k, whole)

    both(fourth_leg)

    for k in range(1, NY):
        arrived(kg_all.at[ys_at[-k % NY]], S_KG2 + k)
    rows64 = lax.broadcasted_iota(jnp.int32, (64, 256), 0)
    chan = lax.broadcasted_iota(jnp.int32, (64, 256), 1)
    owner = (chan // 4) == ((rows64 % 8) * 8 + rows64 // 8)
    lane = lax.broadcasted_iota(jnp.int32, (64, 128), 1)
    same4 = (
        lax.broadcasted_iota(jnp.int32, (128, 256), 0) // 32
        == lax.broadcasted_iota(jnp.int32, (128, 256), 1) % 4
    )
    spread4 = jnp.where(same4, 1.0, 0.0).astype(BF16)
    tiles = kg_all[...].reshape(64, 128)
    grouped = jnp.concatenate([jnp.where(lane % 32 == k, tiles, 0.0) for k in range(10)], axis=0)
    first, second = split(grouped)
    spread_rows = lax.dot_general(first, spread4, NN, preferred_element_type=F32) + lax.dot_general(
        second, spread4, NN, preferred_element_type=F32
    )
    for k in range(10):
        krows[k : k + 1, :] = jnp.sum(
            jnp.where(owner, spread_rows[64 * k : 64 * k + 64], 0.0), axis=0, keepdims=True
        )

    for k in range(2):
        arrived(ns_recv.at[k], S_HALO + 2 + k)
        line = 17 * k
        west[line] = ns_recv[k, 0:16, :]
        middle[line] = ns_recv[k, 1:17, :]
        east[line] = ns_recv[k, 2:18, :]

    shifted = (west, middle, east)
    taps = [krows[k : k + 1, :] for k in range(9)]
    gain = krows[9:10, :]

    def conv_rows(r, carry):
        acc = jnp.zeros((4, 16, 256), F32)
        for i in range(3):
            for j in range(3):
                acc = acc + krows[3 * i + j : 3 * i + j + 1, :] * shifted[j][pl.ds(r * 4 + i, 4)]
        acc = acc.reshape(64, 256)
        mean = jnp.mean(acc, axis=-1, keepdims=True)
        centred = acc - mean
        var = jnp.mean(centred * centred, axis=-1, keepdims=True)
        inv = lax.rsqrt(var + EPSILON)
        hat = centred * inv
        at = pl.ds(pl.multiple_of(r * 64, 64), 64)
        xhat[at, :] = hat
        rstd[at, :] = jnp.broadcast_to(inv, (64, 128))
        normed = hat * krows[9:10, :]
        norm_own[at, :] = normed
        copy(norm_own.at[at], norm_sib.at[at], S_NORM + r, sibling).start()
        return carry

    lax.fori_loop(0, 4, conv_rows, 0)
    parts = [pl.ds(64 * r, 64) for r in range(4)]
    norm_copies = [copy(norm_own.at[at], norm_sib.at[at], S_NORM + r, sibling) for r, at in enumerate(parts)]

    def prepare_tokens(m, source):
        def halves(r, carry):
            at = pl.ds(pl.multiple_of(r * 128, 128), 128)
            value = source[at, :]
            high, low = split(value)
            n_hi[m, at, :] = high
            n_lo[m, at, :] = low
            high, low = split(jnp.transpose(value))
            nt_hi[m, r] = high
            nt_lo[m, r] = low
            return carry

        lax.fori_loop(0, 2, halves, 0)

    prepare_tokens(0, norm_own)

    for k in NEAR:
        arrived(w.at[ys_at[-k % NY], :, 0:2], S_BY + k)
    for k in (0, *NEAR):
        for dx in (1, 3, 2):
            arrived(big(ys_at[-k % NY], xs_at[-dx % NX]), S_X + 3 * k + dx - 1)

    lows = lax.broadcasted_iota(jnp.int32, (4, 8, 128), 1) < 4

    def unpack(xs, carry):
        for r in range(2):
            hs = r * c + (1 - r) * (1 - c)
            at = pl.ds(pl.multiple_of(xs * 64 + hs * 32, 32), 32)
            for e in range(2):
                v = w[:, xs, 2 * r + e].reshape(4, 2, 8, 128)
                a, b = v[:, 0], v[:, 1]
                for bb, value in (
                    (0, jnp.where(lows, a, pltpu.roll(b, 4, 1))),
                    (1, jnp.where(lows, pltpu.roll(a, 4, 1), b)),
                ):
                    high, low = split(value.reshape(32, 128))
                    u_hi[e, at, 128 * bb : 128 * bb + 128] = high
                    u_lo[e, at, 128 * bb : 128 * bb + 128] = low
        at = pl.ds(pl.multiple_of((xs % 2) * 128, 128), 128)
        for q in range(2):
            value = jnp.concatenate([w[:, xs, 4 + q], w[:, xs, 6 + q]], axis=1).reshape(128, 128)
            high, low = split(value)
            d_hi[xs // 2, at, 128 * q : 128 * q + 128] = high
            d_lo[xs // 2, at, 128 * q : 128 * q + 128] = low
        return carry

    lax.fori_loop(0, NX, unpack, 0)

    arrived(cot_sib, S_COT)

    def prepare_cot(r, carry):
        high, low = split(cot_sib[pl.ds(r * 4, 4)].reshape(64, 256))
        to = pl.ds(pl.multiple_of(r * 64, 64), 64)
        g_hi[1, to, :] = high
        g_lo[1, to, :] = low
        return carry

    lax.fori_loop(0, 4, prepare_cot, 0)
    def first_products(e, m):
        downs = (d_hi[e], d_lo[e])
        grads = (g_hi[m], g_lo[m])
        pre = dot3((n_hi[m], n_lo[m]), (u_hi[e], u_lo[e]), NN)
        back = dot3(grads, downs, NT)
        square = pre * pre
        t = jnp.tanh(ROOT * (pre + 0.044715 * (square * pre)))
        half = 0.5 * (1.0 + t)
        hidden = pre * half
        slope = half + 0.5 * pre * (1.0 - t * t) * (ROOT * (1.0 + 3 * 0.044715 * square))
        high, low = split(back * slope)
        p_hi[m, e] = high
        p_lo[m, e] = low
        high, low = split(hidden)
        h_hi[m, e] = high
        h_lo[m, e] = low
        value = dot3(split(jnp.transpose(hidden)), grads, NN)
        dgrad[...] = value if m == 0 else dgrad[...] + value

    def x_reduce(first, count, into, base):
        return [
            copy(
                g.at[pl.ds(4 * yh, 4), xs_at[dx], pl.ds(first, count)], into.at[dx - 1, pl.ds(4 * yh, 4)],
                base + 3 * yh + dx - 1, device(xs_at[dx], h, y, l, c),
            )
            for yh in range(2)
            for dx in (2, 1, 3)
        ]

    reduces = x_reduce(4, 4, x_recv, R_X)
    for e in range(2):
        first_products(e, 0)
        if e == 0:
            for r, at in enumerate(parts):
                arrived(norm_sib.at[at], S_NORM + r)
            prepare_tokens(1, norm_sib)
        first_products(e, 1)
        for bb in range(2):
            for q in range(2):
                v = dgrad[128 * bb : 128 * bb + 128, 128 * q : 128 * q + 128].reshape(8, 2, 8, 128)
                for rh in range(2):
                    g[:, 2 * e + bb, 4 + 2 * rh + q] = v[:, rh]
        for k, dx in enumerate((2, 1, 3)):

            @pl.when(xs_at[dx] // 2 == e)
            def _(k=k):
                reduces[k].start()
                reduces[3 + k].start()

    def second_products(e, carry):
        ugrad[e] = sum(
            dot3((nt_hi[m, r], nt_lo[m, r]), (p_hi[m, e, 128 * r : 128 * r + 128], p_lo[m, e, 128 * r : 128 * r + 128]), NN)
            for m in range(2)
            for r in range(2)
        )
        return carry

    lax.fori_loop(0, 2, second_products, 0)

    def pack(xs, carry):
        for r in range(2):
            hs = r * c + (1 - r) * (1 - c)
            at = pl.ds(pl.multiple_of(xs * 64 + hs * 32, 32), 32)
            for e in range(2):
                v0 = ugrad[e, at, 0:128].reshape(4, 8, 128)
                v1 = ugrad[e, at, 128:256].reshape(4, 8, 128)
                even = jnp.where(lows, v0, pltpu.roll(v1, 4, 1))
                odd = jnp.where(lows, pltpu.roll(v0, 4, 1), v1)
                g[:, xs, 2 * r + e] = jnp.concatenate([even[:, None], odd[:, None]], axis=1).reshape(8, 8, 128)
        return carry

    lax.fori_loop(0, NX, pack, 0)
    for k in (4, 3, 5, 2, 6, 1, 7):
        yy = ys_at[k]
        each = copy(g.at[yy, :, 0:2], by_recv.at[k], R_BY + k, device(x, h, yy, l, c))
        each.start()
        reduces.append(each)
    for each in x_reduce(2, 2, xu_recv, R_XU):
        each.start()
        reduces.append(each)

    swaps = [copy(dnorm.at[1], dn_recv, R_BR, sibling), copy(branch.at[1], br_recv, R_BR + 1, sibling)]
    for m in (1, 0):
        dnorm[m] = sum(dot3((p_hi[m, e], p_lo[m, e]), (u_hi[e], u_lo[e]), NT) for e in range(2))
        if m:
            swaps[0].start()
    for m in (1, 0):
        branch[m] = sum(dot3((h_hi[m, e], h_lo[m, e]), (d_hi[e], d_lo[e]), NN) for e in range(2))
        if m:
            swaps[1].start()

    zpad[0:2] = jnp.zeros((2, 16, 256), F32)
    zpad[18:20] = jnp.zeros((2, 16, 256), F32)
    arrived(dn_recv, R_BR)

    def norm_rows(r, sums):
        at = pl.ds(pl.multiple_of(r * 32, 32), 32)
        hat = xhat[at, :]
        inv = rstd[at, :][:, 0:1]
        dn = dnorm[0, at, :] + dn_recv[at, :]
        dhat = dn * krows[9:10, :]
        mean = jnp.mean(dhat, axis=-1, keepdims=True)
        cross = jnp.mean(dhat * hat, axis=-1, keepdims=True)
        dd = (inv * (dhat - mean - hat * cross)).reshape(2, 16, 256)
        zpad[pl.ds(r * 2 + 2, 2)] = dd
        fresh = []
        for i in range(3):
            for j in range(3):
                v = (dd * shifted[j][pl.ds(r * 2 + i, 2)]).reshape(4, 8, 256)
                fresh.append(sums[3 * i + j] + ((v[0] + v[1]) + (v[2] + v[3])))
        v = (dn * hat).reshape(4, 8, 256)
        fresh.append(sums[9] + ((v[0] + v[1]) + (v[2] + v[3])))
        return tuple(fresh)

    sums = lax.fori_loop(0, 8, norm_rows, tuple(jnp.zeros((8, 256), F32) for _ in range(10)))

    lanes16 = lax.broadcasted_iota(jnp.int32, (2, 16, 256), 1)

    def back_rows(r, carry):
        parts = []
        for j in range(3):
            acc = jnp.zeros((2, 16, 256), F32)
            for i in range(3):
                acc = acc + krows[3 * i + j : 3 * i + j + 1, :] * zpad[pl.ds(r * 2 + 2 - i, 2)]
            parts.append(acc)
        to = pl.ds(r * 2, 2)
        left = jnp.where(lanes16 < 15, pltpu.roll(parts[0], 15, 1), 0.0)
        right = jnp.where(lanes16 > 0, pltpu.roll(parts[2], 1, 1), 0.0)
        centre[to] = parts[1] + (left + right)
        wcol[to] = parts[0][:, 0:1, :]
        ecol[to] = parts[2][:, 15:16, :]
        return carry

    lax.fori_loop(0, 9, back_rows, 0)
    for k, (edge, line) in enumerate(((0, 0), (1, 17))):
        first, last = wcol[line], ecol[line]
        bns_send[k, 0:1, :] = mixed(flips[edge], first, last)
        bns_send[k, 17:18, :] = mixed(flips[edge], last, first)
        for i in range(16):
            bns_send[k, 1 + i : 2 + i, :] = mixed(
                flips[edge], centre[line, i : i + 1, :], centre[line, 15 - i : 16 - i, :]
            )
    bns = rim_copies(bns_send, bns_recv, R_HALO, 8, 0, 1, inner_n, inner_s)
    for each in bns:
        each.start()

    grad_rows = [jnp.sum(sums[k], axis=0, keepdims=True) for k in range(10)]
    grouped = jnp.concatenate([jnp.where(owner, jnp.broadcast_to(v, (64, 256)), 0.0) for v in grad_rows], axis=0)
    first, second = split(grouped)
    fold = lax.dot_general(first, spread4, NT, preferred_element_type=F32) + lax.dot_general(
        second, spread4, NT, preferred_element_type=F32
    )
    folded = jnp.zeros((64, 128), F32)
    for k in range(10):
        folded = folded + jnp.where(lane % 32 == k, fold[64 * k : 64 * k + 64], 0.0)
    kgr_own[...] = folded.reshape(8, 8, 128)
    kgs = []
    for k in range(1, NY):
        yy = ys_at[k]
        each = copy(kgr_own.at[yy], kgr_y.at[k], R_KY + k, device(x, h, yy, l, c))
        each.start()
        kgs.append(each)

    for k in range(1, NY):
        arrived(by_recv.at[k], R_BY + k)
    total = g[y, :, 0:2]
    for k in range(1, NY):
        total = total + by_recv[k]
    g[y, :, 0:2] = total
    for dx in (2, 1, 3):
        to = xs_at[dx]
        each = copy(g.at[y, to, 0:2], bx_recv.at[dx], R_BX + dx, device(to, h, y, l, c))
        each.start()
        reduces.append(each)

    for yh in range(2):
        half = pl.ds(4 * yh, 4)
        for dx in (1, 3, 2):
            arrived(x_recv.at[dx - 1, half], R_X + 3 * yh + dx - 1)
            arrived(xu_recv.at[dx - 1, half], R_XU + 3 * yh + dx - 1)
        g[half, x, 4:8] = (g[half, x, 4:8] + x_recv[0, half]) + (x_recv[1, half] + x_recv[2, half])
        g[half, x, 2:4] = (g[half, x, 2:4] + xu_recv[0, half]) + (xu_recv[1, half] + xu_recv[2, half])
        for k in range(1, NY):
            yy = ys_at[k]

            @pl.when(yy // 4 == yh)
            def _(k=k, yy=yy):
                copy(g.at[yy, x, 2:8], y_recv.at[k], R_Y + k, device(x, h, yy, l, c)).start()

    for k in range(1, NY):
        reduces.append(copy(g.at[ys_at[k], x, 2:8], y_recv.at[k], R_Y + k, device(x, h, ys_at[k], l, c)))

    arrived(br_recv, R_BR + 1)

    def new_rows(r, carry):
        at = pl.ds(pl.multiple_of(r * 64, 64), 64)
        value = branch[0, at, :] + br_recv[at, :]
        to = pl.ds(r * 4, 4)
        out_new[to] = state[to] + value.reshape(4, 16, 256)
        return carry

    lax.fori_loop(0, 4, new_rows, 0)
    stores = [pltpu.make_async_copy(out_new, new_out, rsem.at[S_OUT])]
    stores[0].start()

    for k, line in enumerate((1, 16)):
        arrived(bns_recv.at[k], R_HALO + k)
        wcol[line] = wcol[line] + bns_recv[k, 0:1, :]
        centre[line] = centre[line] + bns_recv[k, 1:17, :]
        ecol[line] = ecol[line] + bns_recv[k, 17:18, :]
    for i in range(16):
        bwe_send[0, i : i + 1, :] = mixed(flips[2], wcol[1 + i], wcol[16 - i])
        bwe_send[1, i : i + 1, :] = mixed(flips[3], ecol[1 + i], ecol[16 - i])
    bwe = rim_copies(bwe_send, bwe_recv, R_HALO + 2, 1, 2, 3, inner_w, inner_e)
    for each in bwe:
        each.start()

    for k in range(1, NY):
        arrived(kgr_y.at[k], R_KY + k)
    total = kgr_own[y]
    for k in range(1, NY):
        total = total + kgr_y[k]
    kgr_x[x] = total
    for k in range(1, NX):
        each = copy(kgr_x.at[x], kgr_x.at[x], R_KX + k, device(xs_at[k], h, y, l, c))
        each.start()
        kgs.append(each)

    for k in range(1, NY):
        arrived(y_recv.at[k], R_Y + k)
    total = g[y, x, 2:8]
    for k in range(1, NY):
        total = total + y_recv[k]
    z_recv[z, 2:8] = total
    for dx in range(1, NX):
        arrived(bx_recv.at[dx], R_BX + dx)
    z_recv[z, 0:2] = (g[y, x, 0:2] + bx_recv[1]) + (bx_recv[2] + bx_recv[3])

    def z_sends(whole):
        sends = []
        for k in range(1, 8):
            dh, dl = k // 4, k % 4
            full = whole if dh == 0 else not whole
            ref = z_recv.at[z, 2:8] if full else z_recv.at[z, 0:2]
            sends.append(copy(ref, ref, R_Z + k, device(x, hs_at[dh], y, ls_at[dl], c)))
        return sends

    def z_start(whole):
        for each in z_sends(whole):
            each.start()

    both(z_start)

    for k in range(1, NX):
        arrived(kgr_x.at[xs_at[-k % NX]], R_KX + k)
    total = kgr_x[0]
    for k in range(1, NX):
        total = total + kgr_x[k]
    zc = z * 2 + c
    kgr_z[zc] = total
    for k in range(1, 16):
        to = device(x, hs_at[k // 8], y, ls_at[(k // 2) % 4], cs_at[k % 2])
        each = copy(kgr_z.at[zc], kgr_z.at[zc], R_KZ + k, to)
        each.start()
        kgs.append(each)

    for k in range(2):
        arrived(bwe_recv.at[k], R_HALO + 2 + k)
    for i in range(16):
        centre[1 + i, 0:1, :] = centre[1 + i, 0:1, :] + bwe_recv[0, i : i + 1, :]
        centre[1 + i, 15:16, :] = centre[1 + i, 15:16, :] + bwe_recv[1, i : i + 1, :]
        out_field[i] = centre[1 + i] + cot[i]
    stores.append(pltpu.make_async_copy(out_field, field_out, rsem.at[S_OUT + 1]))
    stores[1].start()

    def early_sent(whole):
        for each in own_sends(whole):
            each.wait_send()

        @pl.when(ends == 0)
        def _():
            for each in cross_sends(whole):
                each.wait_send()

    both(early_sent)
    for k in range(NY):
        for each in x_sends(k):
            each.wait_send()
    for each in [*small_sends(), *we, *kg1, *ns, *kg2, cot_copy, *norm_copies, *swaps, *reduces, *bns]:
        each.wait_send()

    def fin_sends(whole):
        sends = [copy(fin_up.at[c], fin_up.at[c], R_F, sibling)]
        if whole:
            sends.append(copy(fin_down, fin_down, R_F + 1, sibling))
        return sends

    def z_end(whole):
        for k in range(1, 8):
            zz = (hs_at[k // 4]) * 4 + ls_at[-(k % 4) % NL]
            arrived(z_recv.at[zz, 2:8] if whole else z_recv.at[zz, 0:2], R_Z + k)
        span = slice(2, 8) if whole else slice(0, 2)
        total = z_recv[0, span]
        for zz in range(1, 8):
            total = total + z_recv[zz, span]
        fin_up[c] = total[0:2]
        if whole:
            fin_down[...] = total[2:6]
        for each in fin_sends(whole):
            each.start()
        arrived(fin_up.at[1 - c], R_F)
        if not whole:
            arrived(fin_down, R_F + 1)

    both(z_end)
    for cc in range(2):
        for e in range(2):
            v = fin_up[cc, e]
            for bb in range(2):
                first = 128 * (2 * (2 * e + bb) + cc)
                out_up[:, first : first + 128] = v[4 * bb : 4 * bb + 4]
    for rh in range(2):
        for q in range(2):
            out_down[8 * rh : 8 * rh + 8, 128 * q : 128 * q + 128] = fin_down[2 * rh + q]
    stores.append(pltpu.make_async_copy(out_up, up_out, rsem.at[S_OUT + 2]))
    stores.append(pltpu.make_async_copy(out_down, down_out, rsem.at[S_OUT + 3]))
    stores[2].start()
    stores[3].start()

    for k in range(1, 16):
        hh, ll, cc = hs_at[k // 8], ls_at[-(k // 2) % 4], cs_at[k % 2]
        arrived(kgr_z.at[(hh * 4 + ll) * 2 + cc], R_KZ + k)
    total = kgr_z[0]
    for k in range(1, 16):
        total = total + kgr_z[k]
    out_kg[...] = jnp.sum(jnp.where(sub8 == xh, total, 0.0), axis=0, keepdims=True)
    stores.append(pltpu.make_async_copy(out_kg, kg_out, rsem.at[S_OUT + 4]))
    stores[4].start()

    def last_sent(whole):
        for each in z_sends(whole) + fin_sends(whole):
            each.wait_send()

    both(last_sent)
    for each in [*kgs, *bwe]:
        each.wait_send()
    for each in stores:
        each.wait()


def results(
    new, field, up, down, kg, out_new, out_field, out_up, out_down, out_kt, out_gn,
    v_new, v_field, v_up, v_down, v_kg, v_kt, v_gn, sem,
):
    held = (v_kg, v_new, v_field, v_up, v_down)
    reads = [pltpu.make_async_copy(src, dst, sem.at[k]) for k, (src, dst) in enumerate(zip((kg, new, field, up, down), held))]
    writes = [
        pltpu.make_async_copy(src, dst, sem.at[5 + k])
        for k, (src, dst) in enumerate(
            ((v_new, out_new), (v_field, out_field), (v_up, out_up), (v_down, out_down), (v_kt, out_kt), (v_gn, out_gn))
        )
    ]
    for each in reads:
        each.start()
    reads[0].wait()
    for i in range(4):
        moved = v_kg[...] if i == 0 else pltpu.roll(v_kg[...], 128 - 32 * i, 1)
        v_kt[i : i + 1, :] = moved[:, 0:9]
        v_gn[0:1, i : i + 1] = moved[:, 9:10]
    writes[4].start()
    writes[5].start()
    for k in range(4):
        reads[1 + k].wait()
        writes[k].start()
    for each in writes:
        each.wait()


def shards(state_field, out_grad, depth_kernel, norm_gain, up_weight, down_weight, seam_code):
    anywhere = pl.BlockSpec(memory_space=pl.ANY)

    def buf(*shape, dtype=F32):
        return pltpu.VMEM(shape, dtype)

    def half(*shape):
        return pltpu.VMEM(shape, BF16)

    found = pl.pallas_call(
        kernel,
        out_shape=(
            jax.ShapeDtypeStruct((16, 16, 256), F32),
            jax.ShapeDtypeStruct((16, 16, 256), F32),
            jax.ShapeDtypeStruct((4, 1024), F32),
            jax.ShapeDtypeStruct((16, 256), F32),
            jax.ShapeDtypeStruct((1, 128), F32),
        ),
        in_specs=[anywhere] * 6 + [pl.BlockSpec(memory_space=pltpu.SMEM)],
        out_specs=(anywhere,) * 5,
        scratch_shapes=[
            buf(16, 16, 256), buf(16, 16, 256), buf(4, 1024), buf(16, 256), buf(4, 9), buf(1, 4),
            buf(16, 16, 256), buf(16, 16, 256), buf(4, 1024), buf(16, 256), buf(1, 128),
            buf(8, 4, 8, 8, 128), buf(8, 4, 8, 8, 128),
            buf(18, 16, 256), buf(18, 16, 256), buf(18, 16, 256),
            buf(20, 16, 256), buf(18, 16, 256), buf(18, 1, 256), buf(18, 1, 256),
            buf(2, 18, 256), buf(2, 18, 256), buf(2, 16, 256), buf(2, 16, 256),
            buf(2, 18, 256), buf(2, 18, 256), buf(2, 16, 256), buf(2, 16, 256),
            buf(8, 128), buf(8, 128), buf(8, 8, 128), buf(8, 8, 128),
            buf(8, 8, 128), buf(8, 8, 128), buf(4, 8, 128), buf(16, 8, 128),
            half(2, 256, 256), half(2, 256, 256), half(2, 256, 256), half(2, 256, 256),
            buf(256, 256), buf(256, 128), buf(256, 256), buf(256, 256), buf(16, 16, 256),
            half(2, 256, 256), half(2, 256, 256), half(2, 2, 256, 128), half(2, 2, 256, 128),
            half(2, 256, 256), half(2, 256, 256),
            half(2, 2, 256, 256), half(2, 2, 256, 256), half(2, 2, 256, 256), half(2, 2, 256, 256),
            buf(2, 256, 256), buf(2, 256, 256), buf(256, 256), buf(256, 256),
            buf(2, 256, 256), buf(256, 256), buf(16, 256),
            buf(3, 8, 4, 8, 128), buf(3, 8, 2, 8, 128), buf(8, 6, 8, 128),
            buf(8, 4, 2, 8, 128), buf(4, 2, 8, 128), buf(8, 8, 8, 128),
            buf(2, 2, 8, 128), buf(4, 8, 128),
            pltpu.SemaphoreType.DMA((N_SLOTS,)),
            pltpu.SemaphoreType.DMA((N_SLOTS,)),
        ],
        compiler_params=pltpu.CompilerParams(
            collective_id=0, has_side_effects=True, vmem_limit_bytes=60 * 1024 * 1024
        ),
        name="block",
    )(
        state_field[0, 0], out_grad[0, 0], up_weight, down_weight,
        depth_kernel.T, norm_gain.reshape(1, 4), seam_code[0],
    )
    new, field, up, down, kt, gn = pl.pallas_call(
        results,
        out_shape=(
            jax.ShapeDtypeStruct((16, 16, 256), F32),
            jax.ShapeDtypeStruct((16, 16, 256), F32),
            jax.ShapeDtypeStruct((4, 1024), F32),
            jax.ShapeDtypeStruct((16, 256), F32),
            jax.ShapeDtypeStruct((4, 9), F32),
            jax.ShapeDtypeStruct((1, 4), F32),
        ),
        in_specs=[anywhere] * 5,
        out_specs=(anywhere,) * 6,
        scratch_shapes=[
            buf(16, 16, 256), buf(16, 16, 256), buf(4, 1024), buf(16, 256), buf(1, 128), buf(4, 9), buf(1, 4),
            pltpu.SemaphoreType.DMA((11,)),
        ],
        compiler_params=pltpu.CompilerParams(vmem_limit_bytes=60 * 1024 * 1024),
        name="results",
    )(*found)
    return (new[None, None], field[None, None], kt.T, gn.reshape(4), up, down)


def solution(mesh):
    placed = (
        P("face", "tile", None, None, None),
        P("face", "tile", None, None, None),
        P(None, "tile"),
        P("tile"),
        P("tile", None),
        P("tile", None),
        P("face", "tile", None),
    )
    return jax.shard_map(
        shards,
        mesh=mesh,
        in_specs=placed,
        out_specs=(
            P("face", "tile", None, None, None),
            P("face", "tile", None, None, None),
            P(None, "tile"),
            P("tile"),
            P("tile", None),
            P("tile", None),
        ),
        check_vma=False,
    )
```

```python
import functools
import math

import jax
import jax.numpy as jnp
from jax import lax
from jax.experimental import pallas as pl
from jax.experimental.pallas import tpu as pltpu
from jax.sharding import PartitionSpec as P

EPSILON = 1e-06
NX, NH, NY, NL, NC = 4, 2, 8, 4, 2
MESH = pl.DeviceIdType.MESH
F32, BF16 = jnp.float32, jnp.bfloat16
ROOT = math.sqrt(2.0 / math.pi)
NN = (((1,), (0,)), ((), ()))
NT = (((1,), (1,)), ((), ()))


class Slots:
    def __init__(self):
        self.used = 0

    def take(self, count):
        first = self.used
        self.used += count
        return first


SLOTS = Slots()
S_Y = SLOTS.take(8)
S_C = SLOTS.take(8)
S_CK = SLOTS.take(8)
S_X = SLOTS.take(24)
S_BX = SLOTS.take(8)
S_BY = SLOTS.take(8)
S_IN = SLOTS.take(6)
S_OUT = SLOTS.take(5)
S_COT = SLOTS.take(1)
S_NORM = SLOTS.take(4)
S_KG1 = SLOTS.take(8)
S_KG2 = SLOTS.take(8)
S_HALO = SLOTS.take(4)
R_X = SLOTS.take(6)
R_XU = SLOTS.take(6)
R_BY = SLOTS.take(8)
R_BX = SLOTS.take(4)
R_Y = SLOTS.take(8)
R_Z = SLOTS.take(8)
R_F = SLOTS.take(2)
R_BR = SLOTS.take(2)
R_KY = SLOTS.take(8)
R_KX = SLOTS.take(4)
R_KZ = SLOTS.take(16)
R_HALO = SLOTS.take(4)
N_SLOTS = SLOTS.used

NEAR = (1, 7, 2, 6, 3, 5, 4)


def split(value):
    high = value.astype(BF16)
    return high, (value - high.astype(F32)).astype(BF16)


def dot3(a, b, dims):
    def one(p, q):
        return lax.dot_general(p, q, dims, preferred_element_type=F32)

    return one(a[0], b[0]) + (one(a[0], b[1]) + one(a[1], b[0]))


def kernel(
    state_in, cot_in, up_in, down_in, kt_in, gn_in, code,
    new_out, field_out, up_out, down_out, kg_out,
    state, cot, up, down, kt, gn, out_new, out_field, out_up, out_down, out_kg,
    w, g, west, middle, east, zpad, centre, wcol, ecol,
    ns_send, ns_recv, we_send, we_recv, bns_send, bns_recv, bwe_send, bwe_recv,
    kg_row, kg_own, kg_xh, kg_all, kgr_own, kgr_y, kgr_x, kgr_z,
    u_hi, u_lo, d_hi, d_lo, xhat, rstd, norm_own, norm_sib, cot_sib,
    n_hi, n_lo, nt_hi, nt_lo, g_hi, g_lo, h_hi, h_lo, p_hi, p_lo, branch, dnorm, br_recv, dn_recv, ugrad, dgrad, krows,
    x_recv, xu_recv, y_recv, by_recv, bx_recv, z_recv, fin_up, fin_down,
    ssem, rsem,
):
    face, tile = lax.axis_index("face"), lax.axis_index("tile")
    l, c = face // 2, face % 2
    x, h, y = tile // 16, (tile // 8) % 2, tile % 8
    xs_at = [x] + [(x + k) % NX for k in range(1, NX)]
    ys_at = [y] + [(y + k) % NY for k in range(1, NY)]
    hs_at = [h, 1 - h]
    ls_at = [l] + [(l + k) % NL for k in range(1, NL)]
    cs_at = [c, 1 - c]
    cross_l = [(3 - m) * (1 - l // 3) + m * (l // 3) for m in range(2)]
    source = 3 * (1 - l // 2)
    known = {}

    def device(x, h, y, l, c):
        key = (id(x), id(h), id(y), id(l), id(c))
        return known[key] if key in known else (l * NC + c, (x * NH + h) * NY + y)

    def remember(*place):
        known[tuple(id(v) for v in place)] = device(*place)

    for k in range(NY):
        remember(x, h, ys_at[k], l, c)
        for ll in (*cross_l, source):
            remember(x, hs_at[1], ys_at[k], ll, c)
    for k in range(NX):
        for hh in hs_at:
            remember(xs_at[k], hh, y, l, c)
        for ll in (*cross_l, source):
            remember(xs_at[k], hs_at[1], y, ll, c)
    for hh in hs_at:
        for ll in ls_at:
            for cc in cs_at:
                remember(x, hh, y, ll, cc)
    xh = x * 2 + h
    z = h * 4 + l
    same = (h + c) % 2
    ends = (l % 3 + 1) // 2

    def copy(src, dst, slot, to, send_slot=None):
        return pltpu.make_async_remote_copy(
            src_ref=src, dst_ref=dst,
            send_sem=ssem.at[slot if send_slot is None else send_slot], recv_sem=rsem.at[slot],
            device_id=to, device_id_type=MESH,
        )

    sibling = device(x, h, y, l, cs_at[1])

    def arrived(dst, slot):
        copy(dst, dst, slot, sibling).wait_recv()

    def both(fn):
        pl.when(same == 0)(functools.partial(fn, True))
        pl.when(same == 1)(functools.partial(fn, False))

    barrier = pltpu.get_barrier_semaphore()
    peers = []
    for k in range(1, 16):
        peers.append(device(x, hs_at[k // 8], y, ls_at[(k // 2) % 4], cs_at[k % 2]))
    for k in range(1, NY):
        peers.append(device(x, h, ys_at[k], l, c))
    for dx in range(1, NX):
        peers.append(device(xs_at[dx], h, y, l, c))
    peers.append(device((x + 2 * h + 3) % NX, hs_at[1], y, l, c))
    loads = [
        pltpu.make_async_copy(src, dst, ssem.at[S_IN + k])
        for k, (src, dst) in enumerate(
            ((state_in, state), (kt_in, kt), (gn_in, gn), (up_in, up), (down_in, down), (cot_in, cot))
        )
    ]
    for each in loads:
        each.start()

    def greet(peer):
        pl.semaphore_signal(barrier, inc=1, device_id=peer, device_id_type=MESH)

    for peer in peers:
        greet(peer)
    for k in range(NX):
        greet(device(xs_at[k], hs_at[1], y, source, c))
    for each in loads:
        each.wait()

    def own_up(core, first):
        for e in range(2):
            low, high = (128 * (2 * (2 * e + bb) + core) for bb in range(2))
            w[y, x, first + e] = jnp.concatenate([up[:, low : low + 128], up[:, high : high + 128]], axis=0)

    def own_down():
        for rh in range(2):
            for q in range(2):
                w[y, x, 4 + 2 * rh + q] = down[8 * rh : 8 * rh + 8, 128 * q : 128 * q + 128]

    for core in range(2):
        for kind in range(2):

            def own(core=core, kind=kind):
                own_up(core, 2 if kind == 0 else 0)
                if kind == 0:
                    own_down()

            pl.when((c * 2 + same) == (core * 2 + kind))(own)

    sub8 = lax.broadcasted_iota(jnp.int32, (8, 128), 0)
    kg_row[...] = jnp.zeros_like(kg_row)
    for i in range(4):
        kg_row[i : i + 1, 0:9] = kt[i : i + 1, :]
        kg_row[i : i + 1, 9:10] = gn[0:1, i : i + 1]
    packed = kg_row[0:1, :]
    for i in range(1, 4):
        packed = packed + pltpu.roll(kg_row[i : i + 1, :], 32 * i, 1)
    kg_tile = jnp.where(sub8 == xh, jnp.broadcast_to(packed, (8, 128)), 0.0)
    kg_own[...] = kg_tile
    kg_xh[0] = kg_tile

    flips = [code[0, e].astype(F32) for e in range(4)]

    def mixed(flip, a, b):
        return a * (1.0 - flip) + b * flip

    for i in range(16):
        we_send[0, i : i + 1, :] = mixed(flips[2], state[i, 0:1, :], state[15 - i, 0:1, :])
        we_send[1, i : i + 1, :] = mixed(flips[3], state[i, 15:16, :], state[15 - i, 15:16, :])

    row, col = xh, y
    inner_n, inner_s = (row + 7) // 8, (14 - row) // 8
    inner_w, inner_e = (col + 7) // 8, (14 - col) // 8
    across = (
        (face + 4) % 8,
        7 - face,
        (face + 7 + 2 * (face % 2)) % 8,
        face + 1 - 2 * (face % 2),
    )

    def rim_copies(send, recv, base, stride, low_edge, high_edge, inner_low, inner_high):
        low_to = (
            inner_low * face + (1 - inner_low) * across[low_edge],
            tile - stride * inner_low,
        )
        high_to = (
            inner_high * face + (1 - inner_high) * across[high_edge],
            tile + stride * inner_high,
        )
        low = pltpu.make_async_remote_copy(
            src_ref=send.at[0], dst_ref=recv.at[inner_low], send_sem=ssem.at[base],
            recv_sem=rsem.at[base + inner_low], device_id=low_to, device_id_type=MESH,
        )
        high = pltpu.make_async_remote_copy(
            src_ref=send.at[1], dst_ref=recv.at[1 - inner_high], send_sem=ssem.at[base + 1],
            recv_sem=rsem.at[base + 1 - inner_high], device_id=high_to, device_id_type=MESH,
        )
        return low, high

    def prepare(r, carry):
        rows = state[pl.ds(r * 4, 4)]
        at = pl.ds(1 + r * 4, 4)
        middle[at] = rows
        west[at] = pltpu.roll(rows, 1, 1)
        east[at] = pltpu.roll(rows, 15, 1)
        high, low = split(cot[pl.ds(r * 4, 4)].reshape(64, 256))
        to = pl.ds(pl.multiple_of(r * 64, 64), 64)
        g_hi[0, to, :] = high
        g_lo[0, to, :] = low
        return carry

    lax.fori_loop(0, 4, prepare, 0)

    pl.semaphore_wait(barrier, len(peers) + (1 - ends) * 8)

    we = rim_copies(we_send, we_recv, S_HALO, 1, 2, 3, inner_w, inner_e)
    for each in we:
        each.start()

    def big(yy, xx):
        return w.at[yy, xx, 2:8]

    def small(yy, xx):
        return w.at[yy, xx, 0:2]

    def own_sends(whole):
        mine = big(y, x) if whole else small(y, x)
        if whole:
            return y_sends()
        return [copy(mine, mine, S_BX + k, device(xs_at[k], h, y, l, c)) for k in (1, 3, 2)]

    def cross_sends(whole):
        mine = big(y, x) if whole else small(y, x)
        sends = []
        for k in (0,) if whole else (0, 1, 3, 2):
            for m in range(2):
                sends.append(
                    copy(
                        mine, mine, S_Y if whole else S_BX + k, device(xs_at[k], hs_at[1], y, cross_l[m], c),
                        S_C + 2 * k + m,
                    )
                )
        return sends

    def y_sends():
        ref = big(y, x)
        return [copy(ref, ref, S_Y + k, device(x, h, ys_at[k], l, c)) for k in NEAR]

    def kg_cross():
        return [
            copy(kg_own, kg_xh.at[4 + k], S_KG1 + 4 + k, device(xs_at[k], hs_at[1], y, cross_l[m], c), S_CK + 2 * k + m)
            for k in (0, 1, 3, 2)
            for m in range(2)
        ]

    def x_sends(k):
        ref = big(ys_at[-k % NY], x)
        return [copy(ref, ref, S_X + 3 * k + dx - 1, device(xs_at[dx], h, y, l, c)) for dx in (2, 1, 3)]

    def forward(k, whole):
        if k:
            arrived(big(ys_at[-k % NY], x), S_Y + k)
        for each in x_sends(k):
            each.start()

    def small_sends():
        ref = w.at[y, :, 0:2]
        return [copy(ref, ref, S_BY + k, device(x, h, ys_at[k], l, c)) for k in (4, 3, 5, 2, 6, 1, 7)]

    def forward_small(whole):
        for k in range(NX):
            if k or whole:
                arrived(small(y, xs_at[-k % NX]), S_BX + k)
        for each in small_sends():
            each.start()

    def first_leg(whole):
        for each in own_sends(whole):
            each.start()

        @pl.when(ends == 0)
        def _():
            for each in cross_sends(whole):
                each.start()

        if whole:
            forward(0, whole)

    both(first_leg)
    cot_copy = copy(cot, cot_sib, S_COT, sibling)
    cot_copy.start()
    kg1 = [copy(kg_own, kg_xh.at[k], S_KG1 + k, device(xs_at[k], h, y, l, c)) for k in range(1, NX)]
    for each in kg1:
        each.start()

    @pl.when(ends == 0)
    def _():
        for each in kg_cross():
            each.start()

    def second_leg(whole):
        if whole:
            forward(1, whole)
            forward(7, whole)
        else:
            arrived(big(y, x), S_Y)
            for each in y_sends() + x_sends(0):
                each.start()

    both(second_leg)

    for k in range(2):
        arrived(we_recv.at[k], S_HALO + k)
    for i in range(16):
        west[1 + i, 0:1, :] = we_recv[0, i : i + 1, :]
        east[1 + i, 15:16, :] = we_recv[1, i : i + 1, :]
    for k, (edge, line) in enumerate(((0, 0), (1, 15))):
        first, last = we_recv[0, line : line + 1, :], we_recv[1, line : line + 1, :]
        ns_send[k, 0:1, :] = mixed(flips[edge], first, last)
        ns_send[k, 17:18, :] = mixed(flips[edge], last, first)
        for i in range(16):
            ns_send[k, 1 + i : 2 + i, :] = mixed(
                flips[edge], state[line, i : i + 1, :], state[line, 15 - i : 16 - i, :]
            )
    ns = rim_copies(ns_send, ns_recv, S_HALO + 2, 8, 0, 1, inner_n, inner_s)
    for each in ns:
        each.start()

    for k in range(1, 8):
        arrived(kg_xh.at[k], S_KG1 + k)
    total = kg_xh[0]
    for k in range(1, 8):
        total = total + kg_xh[k]
    kg_all[y] = total
    kg2 = []
    for k in range(1, NY):
        mine = kg_all.at[y]
        each = copy(mine, mine, S_KG2 + k, device(x, h, ys_at[k], l, c))
        each.start()
        kg2.append(each)

    def third_leg(whole):
        for k in (2, 6) if whole else ():
            forward(k, whole)
        forward_small(whole)

    both(third_leg)

    def fourth_leg(whole):
        for k in (3, 5, 4) if whole else NEAR:
            forward(k, whole)

    both(fourth_leg)

    for k in range(1, NY):
        arrived(kg_all.at[ys_at[-k % NY]], S_KG2 + k)
    rows64 = lax.broadcasted_iota(jnp.int32, (64, 256), 0)
    chan = lax.broadcasted_iota(jnp.int32, (64, 256), 1)
    owner = (chan // 4) == ((rows64 % 8) * 8 + rows64 // 8)
    lane = lax.broadcasted_iota(jnp.int32, (64, 128), 1)
    same4 = (
        lax.broadcasted_iota(jnp.int32, (128, 256), 0) // 32
        == lax.broadcasted_iota(jnp.int32, (128, 256), 1) % 4
    )
    spread4 = jnp.where(same4, 1.0, 0.0).astype(BF16)
    tiles = kg_all[...].reshape(64, 128)
    grouped = jnp.concatenate([jnp.where(lane % 32 == k, tiles, 0.0) for k in range(10)], axis=0)
    first, second = split(grouped)
    spread_rows = lax.dot_general(first, spread4, NN, preferred_element_type=F32) + lax.dot_general(
        second, spread4, NN, preferred_element_type=F32
    )
    for k in range(10):
        krows[k : k + 1, :] = jnp.sum(
            jnp.where(owner, spread_rows[64 * k : 64 * k + 64], 0.0), axis=0, keepdims=True
        )

    for k in range(2):
        arrived(ns_recv.at[k], S_HALO + 2 + k)
        line = 17 * k
        west[line] = ns_recv[k, 0:16, :]
        middle[line] = ns_recv[k, 1:17, :]
        east[line] = ns_recv[k, 2:18, :]

    shifted = (west, middle, east)
    taps = [krows[k : k + 1, :] for k in range(9)]
    gain = krows[9:10, :]

    def conv_rows(r, carry):
        acc = jnp.zeros((4, 16, 256), F32)
        for i in range(3):
            for j in range(3):
                acc = acc + krows[3 * i + j : 3 * i + j + 1, :] * shifted[j][pl.ds(r * 4 + i, 4)]
        acc = acc.reshape(64, 256)
        mean = jnp.mean(acc, axis=-1, keepdims=True)
        centred = acc - mean
        var = jnp.mean(centred * centred, axis=-1, keepdims=True)
        inv = lax.rsqrt(var + EPSILON)
        hat = centred * inv
        at = pl.ds(pl.multiple_of(r * 64, 64), 64)
        xhat[at, :] = hat
        rstd[at, :] = jnp.broadcast_to(inv, (64, 128))
        normed = hat * krows[9:10, :]
        norm_own[at, :] = normed
        copy(norm_own.at[at], norm_sib.at[at], S_NORM + r, sibling).start()
        return carry

    lax.fori_loop(0, 4, conv_rows, 0)
    parts = [pl.ds(64 * r, 64) for r in range(4)]
    norm_copies = [copy(norm_own.at[at], norm_sib.at[at], S_NORM + r, sibling) for r, at in enumerate(parts)]

    def prepare_tokens(m, source):
        def halves(r, carry):
            at = pl.ds(pl.multiple_of(r * 128, 128), 128)
            value = source[at, :]
            high, low = split(value)
            n_hi[m, at, :] = high
            n_lo[m, at, :] = low
            high, low = split(jnp.transpose(value))
            nt_hi[m, r] = high
            nt_lo[m, r] = low
            return carry

        lax.fori_loop(0, 2, halves, 0)

    prepare_tokens(0, norm_own)

    for k in NEAR:
        arrived(w.at[ys_at[-k % NY], :, 0:2], S_BY + k)
    for k in (0, *NEAR):
        for dx in (1, 3, 2):
            arrived(big(ys_at[-k % NY], xs_at[-dx % NX]), S_X + 3 * k + dx - 1)

    lows = lax.broadcasted_iota(jnp.int32, (4, 8, 128), 1) < 4

    def unpack(xs, carry):
        for r in range(2):
            hs = r * c + (1 - r) * (1 - c)
            at = pl.ds(pl.multiple_of(xs * 64 + hs * 32, 32), 32)
            for e in range(2):
                v = w[:, xs, 2 * r + e].reshape(4, 2, 8, 128)
                a, b = v[:, 0], v[:, 1]
                for bb, value in (
                    (0, jnp.where(lows, a, pltpu.roll(b, 4, 1))),
                    (1, jnp.where(lows, pltpu.roll(a, 4, 1), b)),
                ):
                    high, low = split(value.reshape(32, 128))
                    u_hi[e, at, 128 * bb : 128 * bb + 128] = high
                    u_lo[e, at, 128 * bb : 128 * bb + 128] = low
        at = pl.ds(pl.multiple_of((xs % 2) * 128, 128), 128)
        for q in range(2):
            value = jnp.concatenate([w[:, xs, 4 + q], w[:, xs, 6 + q]], axis=1).reshape(128, 128)
            high, low = split(value)
            d_hi[xs // 2, at, 128 * q : 128 * q + 128] = high
            d_lo[xs // 2, at, 128 * q : 128 * q + 128] = low
        return carry

    lax.fori_loop(0, NX, unpack, 0)

    arrived(cot_sib, S_COT)

    def prepare_cot(r, carry):
        high, low = split(cot_sib[pl.ds(r * 4, 4)].reshape(64, 256))
        to = pl.ds(pl.multiple_of(r * 64, 64), 64)
        g_hi[1, to, :] = high
        g_lo[1, to, :] = low
        return carry

    lax.fori_loop(0, 4, prepare_cot, 0)
    def first_products(e, m):
        downs = (d_hi[e], d_lo[e])
        grads = (g_hi[m], g_lo[m])
        pre = dot3((n_hi[m], n_lo[m]), (u_hi[e], u_lo[e]), NN)
        back = dot3(grads, downs, NT)
        square = pre * pre
        t = jnp.tanh(ROOT * (pre + 0.044715 * (square * pre)))
        half = 0.5 * (1.0 + t)
        hidden = pre * half
        slope = half + 0.5 * pre * (1.0 - t * t) * (ROOT * (1.0 + 3 * 0.044715 * square))
        high, low = split(back * slope)
        p_hi[m, e] = high
        p_lo[m, e] = low
        high, low = split(hidden)
        h_hi[m, e] = high
        h_lo[m, e] = low
        value = dot3(split(jnp.transpose(hidden)), grads, NN)
        dgrad[...] = value if m == 0 else dgrad[...] + value

    def x_reduce(first, count, into, base):
        return [
            copy(
                g.at[pl.ds(4 * yh, 4), xs_at[dx], pl.ds(first, count)], into.at[dx - 1, pl.ds(4 * yh, 4)],
                base + 3 * yh + dx - 1, device(xs_at[dx], h, y, l, c),
            )
            for yh in range(2)
            for dx in (2, 1, 3)
        ]

    reduces = x_reduce(4, 4, x_recv, R_X)
    for e in range(2):
        first_products(e, 0)
        if e == 0:
            for r, at in enumerate(parts):
                arrived(norm_sib.at[at], S_NORM + r)
            prepare_tokens(1, norm_sib)
        first_products(e, 1)
        for bb in range(2):
            for q in range(2):
                v = dgrad[128 * bb : 128 * bb + 128, 128 * q : 128 * q + 128].reshape(8, 2, 8, 128)
                for rh in range(2):
                    g[:, 2 * e + bb, 4 + 2 * rh + q] = v[:, rh]
        for k, dx in enumerate((2, 1, 3)):

            @pl.when(xs_at[dx] // 2 == e)
            def _(k=k):
                reduces[k].start()
                reduces[3 + k].start()

    def second_products(e, carry):
        ugrad[e] = sum(
            dot3((nt_hi[m, r], nt_lo[m, r]), (p_hi[m, e, 128 * r : 128 * r + 128], p_lo[m, e, 128 * r : 128 * r + 128]), NN)
            for m in range(2)
            for r in range(2)
        )
        return carry

    lax.fori_loop(0, 2, second_products, 0)

    def pack(xs, carry):
        for r in range(2):
            hs = r * c + (1 - r) * (1 - c)
            at = pl.ds(pl.multiple_of(xs * 64 + hs * 32, 32), 32)
            for e in range(2):
                v0 = ugrad[e, at, 0:128].reshape(4, 8, 128)
                v1 = ugrad[e, at, 128:256].reshape(4, 8, 128)
                even = jnp.where(lows, v0, pltpu.roll(v1, 4, 1))
                odd = jnp.where(lows, pltpu.roll(v0, 4, 1), v1)
                g[:, xs, 2 * r + e] = jnp.concatenate([even[:, None], odd[:, None]], axis=1).reshape(8, 8, 128)
        return carry

    lax.fori_loop(0, NX, pack, 0)
    for k in (4, 3, 5, 2, 6, 1, 7):
        yy = ys_at[k]
        each = copy(g.at[yy, :, 0:2], by_recv.at[k], R_BY + k, device(x, h, yy, l, c))
        each.start()
        reduces.append(each)
    for each in x_reduce(2, 2, xu_recv, R_XU):
        each.start()
        reduces.append(each)

    swaps = [copy(dnorm.at[1], dn_recv, R_BR, sibling), copy(branch.at[1], br_recv, R_BR + 1, sibling)]
    for m in (1, 0):
        dnorm[m] = sum(dot3((p_hi[m, e], p_lo[m, e]), (u_hi[e], u_lo[e]), NT) for e in range(2))
        if m:
            swaps[0].start()
    for m in (1, 0):
        branch[m] = sum(dot3((h_hi[m, e], h_lo[m, e]), (d_hi[e], d_lo[e]), NN) for e in range(2))
        if m:
            swaps[1].start()

    zpad[0:2] = jnp.zeros((2, 16, 256), F32)
    zpad[18:20] = jnp.zeros((2, 16, 256), F32)
    arrived(dn_recv, R_BR)

    def norm_rows(r, sums):
        at = pl.ds(pl.multiple_of(r * 32, 32), 32)
        hat = xhat[at, :]
        inv = rstd[at, :][:, 0:1]
        dn = dnorm[0, at, :] + dn_recv[at, :]
        dhat = dn * krows[9:10, :]
        mean = jnp.mean(dhat, axis=-1, keepdims=True)
        cross = jnp.mean(dhat * hat, axis=-1, keepdims=True)
        dd = (inv * (dhat - mean - hat * cross)).reshape(2, 16, 256)
        zpad[pl.ds(r * 2 + 2, 2)] = dd
        fresh = []
        for i in range(3):
            for j in range(3):
                v = (dd * shifted[j][pl.ds(r * 2 + i, 2)]).reshape(4, 8, 256)
                fresh.append(sums[3 * i + j] + ((v[0] + v[1]) + (v[2] + v[3])))
        v = (dn * hat).reshape(4, 8, 256)
        fresh.append(sums[9] + ((v[0] + v[1]) + (v[2] + v[3])))
        return tuple(fresh)

    sums = lax.fori_loop(0, 8, norm_rows, tuple(jnp.zeros((8, 256), F32) for _ in range(10)))

    lanes16 = lax.broadcasted_iota(jnp.int32, (2, 16, 256), 1)

    def back_rows(r, carry):
        parts = []
        for j in range(3):
            acc = jnp.zeros((2, 16, 256), F32)
            for i in range(3):
                acc = acc + krows[3 * i + j : 3 * i + j + 1, :] * zpad[pl.ds(r * 2 + 2 - i, 2)]
            parts.append(acc)
        to = pl.ds(r * 2, 2)
        left = jnp.where(lanes16 < 15, pltpu.roll(parts[0], 15, 1), 0.0)
        right = jnp.where(lanes16 > 0, pltpu.roll(parts[2], 1, 1), 0.0)
        centre[to] = parts[1] + (left + right)
        wcol[to] = parts[0][:, 0:1, :]
        ecol[to] = parts[2][:, 15:16, :]
        return carry

    lax.fori_loop(0, 9, back_rows, 0)
    for k, (edge, line) in enumerate(((0, 0), (1, 17))):
        first, last = wcol[line], ecol[line]
        bns_send[k, 0:1, :] = mixed(flips[edge], first, last)
        bns_send[k, 17:18, :] = mixed(flips[edge], last, first)
        for i in range(16):
            bns_send[k, 1 + i : 2 + i, :] = mixed(
                flips[edge], centre[line, i : i + 1, :], centre[line, 15 - i : 16 - i, :]
            )
    bns = rim_copies(bns_send, bns_recv, R_HALO, 8, 0, 1, inner_n, inner_s)
    for each in bns:
        each.start()

    grad_rows = [jnp.sum(sums[k], axis=0, keepdims=True) for k in range(10)]
    grouped = jnp.concatenate([jnp.where(owner, jnp.broadcast_to(v, (64, 256)), 0.0) for v in grad_rows], axis=0)
    first, second = split(grouped)
    fold = lax.dot_general(first, spread4, NT, preferred_element_type=F32) + lax.dot_general(
        second, spread4, NT, preferred_element_type=F32
    )
    folded = jnp.zeros((64, 128), F32)
    for k in range(10):
        folded = folded + jnp.where(lane % 32 == k, fold[64 * k : 64 * k + 64], 0.0)
    kgr_own[...] = folded.reshape(8, 8, 128)
    kgs = []
    for k in range(1, NY):
        yy = ys_at[k]
        each = copy(kgr_own.at[yy], kgr_y.at[k], R_KY + k, device(x, h, yy, l, c))
        each.start()
        kgs.append(each)

    for k in range(1, NY):
        arrived(by_recv.at[k], R_BY + k)
    total = g[y, :, 0:2]
    for k in range(1, NY):
        total = total + by_recv[k]
    g[y, :, 0:2] = total
    for dx in (2, 1, 3):
        to = xs_at[dx]
        each = copy(g.at[y, to, 0:2], bx_recv.at[dx], R_BX + dx, device(to, h, y, l, c))
        each.start()
        reduces.append(each)

    for yh in range(2):
        half = pl.ds(4 * yh, 4)
        for dx in (1, 3, 2):
            arrived(x_recv.at[dx - 1, half], R_X + 3 * yh + dx - 1)
            arrived(xu_recv.at[dx - 1, half], R_XU + 3 * yh + dx - 1)
        g[half, x, 4:8] = (g[half, x, 4:8] + x_recv[0, half]) + (x_recv[1, half] + x_recv[2, half])
        g[half, x, 2:4] = (g[half, x, 2:4] + xu_recv[0, half]) + (xu_recv[1, half] + xu_recv[2, half])
        for k in range(1, NY):
            yy = ys_at[k]

            @pl.when(yy // 4 == yh)
            def _(k=k, yy=yy):
                copy(g.at[yy, x, 2:8], y_recv.at[k], R_Y + k, device(x, h, yy, l, c)).start()

    for k in range(1, NY):
        reduces.append(copy(g.at[ys_at[k], x, 2:8], y_recv.at[k], R_Y + k, device(x, h, ys_at[k], l, c)))

    arrived(br_recv, R_BR + 1)

    def new_rows(r, carry):
        at = pl.ds(pl.multiple_of(r * 64, 64), 64)
        value = branch[0, at, :] + br_recv[at, :]
        to = pl.ds(r * 4, 4)
        out_new[to] = state[to] + value.reshape(4, 16, 256)
        return carry

    lax.fori_loop(0, 4, new_rows, 0)
    stores = [pltpu.make_async_copy(out_new, new_out, rsem.at[S_OUT])]
    stores[0].start()

    for k, line in enumerate((1, 16)):
        arrived(bns_recv.at[k], R_HALO + k)
        wcol[line] = wcol[line] + bns_recv[k, 0:1, :]
        centre[line] = centre[line] + bns_recv[k, 1:17, :]
        ecol[line] = ecol[line] + bns_recv[k, 17:18, :]
    for i in range(16):
        bwe_send[0, i : i + 1, :] = mixed(flips[2], wcol[1 + i], wcol[16 - i])
        bwe_send[1, i : i + 1, :] = mixed(flips[3], ecol[1 + i], ecol[16 - i])
    bwe = rim_copies(bwe_send, bwe_recv, R_HALO + 2, 1, 2, 3, inner_w, inner_e)
    for each in bwe:
        each.start()

    for k in range(1, NY):
        arrived(kgr_y.at[k], R_KY + k)
    total = kgr_own[y]
    for k in range(1, NY):
        total = total + kgr_y[k]
    kgr_x[x] = total
    for k in range(1, NX):
        each = copy(kgr_x.at[x], kgr_x.at[x], R_KX + k, device(xs_at[k], h, y, l, c))
        each.start()
        kgs.append(each)

    for k in range(1, NY):
        arrived(y_recv.at[k], R_Y + k)
    total = g[y, x, 2:8]
    for k in range(1, NY):
        total = total + y_recv[k]
    z_recv[z, 2:8] = total
    for dx in range(1, NX):
        arrived(bx_recv.at[dx], R_BX + dx)
    z_recv[z, 0:2] = (g[y, x, 0:2] + bx_recv[1]) + (bx_recv[2] + bx_recv[3])

    def z_sends(whole):
        sends = []
        for k in range(1, 8):
            dh, dl = k // 4, k % 4
            full = whole if dh == 0 else not whole
            ref = z_recv.at[z, 2:8] if full else z_recv.at[z, 0:2]
            sends.append(copy(ref, ref, R_Z + k, device(x, hs_at[dh], y, ls_at[dl], c)))
        return sends

    def z_start(whole):
        for each in z_sends(whole):
            each.start()

    both(z_start)

    for k in range(1, NX):
        arrived(kgr_x.at[xs_at[-k % NX]], R_KX + k)
    total = kgr_x[0]
    for k in range(1, NX):
        total = total + kgr_x[k]
    zc = z * 2 + c
    kgr_z[zc] = total
    for k in range(1, 16):
        to = device(x, hs_at[k // 8], y, ls_at[(k // 2) % 4], cs_at[k % 2])
        each = copy(kgr_z.at[zc], kgr_z.at[zc], R_KZ + k, to)
        each.start()
        kgs.append(each)

    for k in range(2):
        arrived(bwe_recv.at[k], R_HALO + 2 + k)
    for i in range(16):
        centre[1 + i, 0:1, :] = centre[1 + i, 0:1, :] + bwe_recv[0, i : i + 1, :]
        centre[1 + i, 15:16, :] = centre[1 + i, 15:16, :] + bwe_recv[1, i : i + 1, :]
        out_field[i] = centre[1 + i] + cot[i]
    stores.append(pltpu.make_async_copy(out_field, field_out, rsem.at[S_OUT + 1]))
    stores[1].start()

    def early_sent(whole):
        for each in own_sends(whole) + ([] if whole else y_sends()):
            each.wait_send()

        @pl.when(ends == 0)
        def _():
            for each in cross_sends(whole) + kg_cross():
                each.wait_send()

    both(early_sent)
    for k in range(NY):
        for each in x_sends(k):
            each.wait_send()
    for each in [*small_sends(), *we, *kg1, *ns, *kg2, cot_copy, *norm_copies, *swaps, *reduces, *bns]:
        each.wait_send()

    def fin_sends(whole):
        sends = [copy(fin_up.at[c], fin_up.at[c], R_F, sibling)]
        if whole:
            sends.append(copy(fin_down, fin_down, R_F + 1, sibling))
        return sends

    def z_end(whole):
        for k in range(1, 8):
            zz = (hs_at[k // 4]) * 4 + ls_at[-(k % 4) % NL]
            arrived(z_recv.at[zz, 2:8] if whole else z_recv.at[zz, 0:2], R_Z + k)
        span = slice(2, 8) if whole else slice(0, 2)
        total = z_recv[0, span]
        for zz in range(1, 8):
            total = total + z_recv[zz, span]
        fin_up[c] = total[0:2]
        if whole:
            fin_down[...] = total[2:6]
        for each in fin_sends(whole):
            each.start()
        arrived(fin_up.at[1 - c], R_F)
        if not whole:
            arrived(fin_down, R_F + 1)

    both(z_end)
    for cc in range(2):
        for e in range(2):
            v = fin_up[cc, e]
            for bb in range(2):
                first = 128 * (2 * (2 * e + bb) + cc)
                out_up[:, first : first + 128] = v[4 * bb : 4 * bb + 4]
    for rh in range(2):
        for q in range(2):
            out_down[8 * rh : 8 * rh + 8, 128 * q : 128 * q + 128] = fin_down[2 * rh + q]
    stores.append(pltpu.make_async_copy(out_up, up_out, rsem.at[S_OUT + 2]))
    stores.append(pltpu.make_async_copy(out_down, down_out, rsem.at[S_OUT + 3]))
    stores[2].start()
    stores[3].start()

    for k in range(1, 16):
        hh, ll, cc = hs_at[k // 8], ls_at[-(k // 2) % 4], cs_at[k % 2]
        arrived(kgr_z.at[(hh * 4 + ll) * 2 + cc], R_KZ + k)
    total = kgr_z[0]
    for k in range(1, 16):
        total = total + kgr_z[k]
    out_kg[...] = jnp.sum(jnp.where(sub8 == xh, total, 0.0), axis=0, keepdims=True)
    stores.append(pltpu.make_async_copy(out_kg, kg_out, rsem.at[S_OUT + 4]))
    stores[4].start()

    def last_sent(whole):
        for each in z_sends(whole) + fin_sends(whole):
            each.wait_send()

    both(last_sent)
    for each in [*kgs, *bwe]:
        each.wait_send()
    for each in stores:
        each.wait()


def results(
    new, field, up, down, kg, out_new, out_field, out_up, out_down, out_kt, out_gn,
    v_new, v_field, v_up, v_down, v_kg, v_kt, v_gn, sem,
):
    held = (v_kg, v_new, v_field, v_up, v_down)
    reads = [pltpu.make_async_copy(src, dst, sem.at[k]) for k, (src, dst) in enumerate(zip((kg, new, field, up, down), held))]
    writes = [
        pltpu.make_async_copy(src, dst, sem.at[5 + k])
        for k, (src, dst) in enumerate(
            ((v_new, out_new), (v_field, out_field), (v_up, out_up), (v_down, out_down), (v_kt, out_kt), (v_gn, out_gn))
        )
    ]
    for each in reads:
        each.start()
    reads[0].wait()
    for i in range(4):
        moved = v_kg[...] if i == 0 else pltpu.roll(v_kg[...], 128 - 32 * i, 1)
        v_kt[i : i + 1, :] = moved[:, 0:9]
        v_gn[0:1, i : i + 1] = moved[:, 9:10]
    writes[4].start()
    writes[5].start()
    for k in range(4):
        reads[1 + k].wait()
        writes[k].start()
    for each in writes:
        each.wait()


def shards(state_field, out_grad, depth_kernel, norm_gain, up_weight, down_weight, seam_code):
    anywhere = pl.BlockSpec(memory_space=pl.ANY)

    def buf(*shape, dtype=F32):
        return pltpu.VMEM(shape, dtype)

    def half(*shape):
        return pltpu.VMEM(shape, BF16)

    found = pl.pallas_call(
        kernel,
        out_shape=(
            jax.ShapeDtypeStruct((16, 16, 256), F32),
            jax.ShapeDtypeStruct((16, 16, 256), F32),
            jax.ShapeDtypeStruct((4, 1024), F32),
            jax.ShapeDtypeStruct((16, 256), F32),
            jax.ShapeDtypeStruct((1, 128), F32),
        ),
        in_specs=[anywhere] * 6 + [pl.BlockSpec(memory_space=pltpu.SMEM)],
        out_specs=(anywhere,) * 5,
        scratch_shapes=[
            buf(16, 16, 256), buf(16, 16, 256), buf(4, 1024), buf(16, 256), buf(4, 9), buf(1, 4),
            buf(16, 16, 256), buf(16, 16, 256), buf(4, 1024), buf(16, 256), buf(1, 128),
            buf(8, 4, 8, 8, 128), buf(8, 4, 8, 8, 128),
            buf(18, 16, 256), buf(18, 16, 256), buf(18, 16, 256),
            buf(20, 16, 256), buf(18, 16, 256), buf(18, 1, 256), buf(18, 1, 256),
            buf(2, 18, 256), buf(2, 18, 256), buf(2, 16, 256), buf(2, 16, 256),
            buf(2, 18, 256), buf(2, 18, 256), buf(2, 16, 256), buf(2, 16, 256),
            buf(8, 128), buf(8, 128), buf(8, 8, 128), buf(8, 8, 128),
            buf(8, 8, 128), buf(8, 8, 128), buf(4, 8, 128), buf(16, 8, 128),
            half(2, 256, 256), half(2, 256, 256), half(2, 256, 256), half(2, 256, 256),
            buf(256, 256), buf(256, 128), buf(256, 256), buf(256, 256), buf(16, 16, 256),
            half(2, 256, 256), half(2, 256, 256), half(2, 2, 256, 128), half(2, 2, 256, 128),
            half(2, 256, 256), half(2, 256, 256),
            half(2, 2, 256, 256), half(2, 2, 256, 256), half(2, 2, 256, 256), half(2, 2, 256, 256),
            buf(2, 256, 256), buf(2, 256, 256), buf(256, 256), buf(256, 256),
            buf(2, 256, 256), buf(256, 256), buf(16, 256),
            buf(3, 8, 4, 8, 128), buf(3, 8, 2, 8, 128), buf(8, 6, 8, 128),
            buf(8, 4, 2, 8, 128), buf(4, 2, 8, 128), buf(8, 8, 8, 128),
            buf(2, 2, 8, 128), buf(4, 8, 128),
            pltpu.SemaphoreType.DMA((N_SLOTS,)),
            pltpu.SemaphoreType.DMA((N_SLOTS,)),
        ],
        compiler_params=pltpu.CompilerParams(
            collective_id=0, has_side_effects=True, vmem_limit_bytes=60 * 1024 * 1024
        ),
        name="block",
    )(
        state_field[0, 0], out_grad[0, 0], up_weight, down_weight,
        depth_kernel.T, norm_gain.reshape(1, 4), seam_code[0],
    )
    new, field, up, down, kt, gn = pl.pallas_call(
        results,
        out_shape=(
            jax.ShapeDtypeStruct((16, 16, 256), F32),
            jax.ShapeDtypeStruct((16, 16, 256), F32),
            jax.ShapeDtypeStruct((4, 1024), F32),
            jax.ShapeDtypeStruct((16, 256), F32),
            jax.ShapeDtypeStruct((4, 9), F32),
            jax.ShapeDtypeStruct((1, 4), F32),
        ),
        in_specs=[anywhere] * 5,
        out_specs=(anywhere,) * 6,
        scratch_shapes=[
            buf(16, 16, 256), buf(16, 16, 256), buf(4, 1024), buf(16, 256), buf(1, 128), buf(4, 9), buf(1, 4),
            pltpu.SemaphoreType.DMA((11,)),
        ],
        compiler_params=pltpu.CompilerParams(vmem_limit_bytes=60 * 1024 * 1024),
        name="results",
    )(*found)
    return (new[None, None], field[None, None], kt.T, gn.reshape(4), up, down)


def solution(mesh):
    placed = (
        P("face", "tile", None, None, None),
        P("face", "tile", None, None, None),
        P(None, "tile"),
        P("tile"),
        P("tile", None),
        P("tile", None),
        P("face", "tile", None),
    )
    return jax.shard_map(
        shards,
        mesh=mesh,
        in_specs=placed,
        out_specs=(
            P("face", "tile", None, None, None),
            P("face", "tile", None, None, None),
            P(None, "tile"),
            P("tile"),
            P("tile", None),
            P("tile", None),
        ),
        check_vma=False,
    )
```

```python
import functools
import math

import jax
import jax.numpy as jnp
from jax import lax
from jax.experimental import pallas as pl
from jax.experimental.pallas import tpu as pltpu
from jax.sharding import PartitionSpec as P

EPSILON = 1e-06
NX, NH, NY, NL, NC = 4, 2, 8, 4, 2
MESH = pl.DeviceIdType.MESH
F32, BF16 = jnp.float32, jnp.bfloat16
ROOT = math.sqrt(2.0 / math.pi)
NN = (((1,), (0,)), ((), ()))
NT = (((1,), (1,)), ((), ()))


class Slots:
    def __init__(self):
        self.used = 0

    def take(self, count):
        first = self.used
        self.used += count
        return first


SLOTS = Slots()
S_Y = SLOTS.take(8)
S_C = SLOTS.take(8)
S_CK = SLOTS.take(8)
S_X = SLOTS.take(24)
S_BX = SLOTS.take(8)
S_BY = SLOTS.take(8)
S_IN = SLOTS.take(6)
S_OUT = SLOTS.take(5)
S_COT = SLOTS.take(1)
S_NORM = SLOTS.take(4)
S_KG1 = SLOTS.take(8)
S_KG2 = SLOTS.take(8)
S_HALO = SLOTS.take(4)
R_X = SLOTS.take(6)
R_XU = SLOTS.take(6)
R_BY = SLOTS.take(8)
R_BX = SLOTS.take(4)
R_Y = SLOTS.take(8)
R_Z = SLOTS.take(8)
R_F = SLOTS.take(2)
R_BR = SLOTS.take(2)
R_KY = SLOTS.take(8)
R_KX = SLOTS.take(4)
R_KZ = SLOTS.take(16)
R_HALO = SLOTS.take(4)
N_SLOTS = SLOTS.used

NEAR = (1, 7, 2, 6, 3, 5, 4)


def split(value):
    high = value.astype(BF16)
    return high, (value - high.astype(F32)).astype(BF16)


def dot3(a, b, dims):
    def one(p, q):
        return lax.dot_general(p, q, dims, preferred_element_type=F32)

    return one(a[0], b[0]) + (one(a[0], b[1]) + one(a[1], b[0]))


def kernel(
    state_in, cot_in, up_in, down_in, kt_in, gn_in, code,
    new_out, field_out, up_out, down_out, kg_out,
    state, cot, up, down, kt, gn, out_new, out_field, out_up, out_down, out_kg,
    w, g, west, middle, east, zpad, centre, wcol, ecol,
    ns_send, ns_recv, we_send, we_recv, bns_send, bns_recv, bwe_send, bwe_recv,
    kg_row, kg_own, kg_xh, kg_all, kgr_own, kgr_y, kgr_x, kgr_z,
    u_hi, u_lo, d_hi, d_lo, xhat, rstd, norm_own, norm_sib, cot_sib,
    n_hi, n_lo, nt_hi, nt_lo, g_hi, g_lo, h_hi, h_lo, p_hi, p_lo, branch, dnorm, br_recv, dn_recv, ugrad, dgrad, krows,
    x_recv, xu_recv, y_recv, by_recv, bx_recv, z_recv, fin_up, fin_down,
    ssem, rsem,
):
    face, tile = lax.axis_index("face"), lax.axis_index("tile")
    l, c = face // 2, face % 2
    x, h, y = tile // 16, (tile // 8) % 2, tile % 8
    xs_at = [x] + [(x + k) % NX for k in range(1, NX)]
    ys_at = [y] + [(y + k) % NY for k in range(1, NY)]
    hs_at = [h, 1 - h]
    ls_at = [l] + [(l + k) % NL for k in range(1, NL)]
    cs_at = [c, 1 - c]
    cross_l = [(3 - m) * (1 - l // 3) + m * (l // 3) for m in range(2)]
    source = 3 * (1 - l // 2)
    known = {}

    def device(x, h, y, l, c):
        key = (id(x), id(h), id(y), id(l), id(c))
        return known[key] if key in known else (l * NC + c, (x * NH + h) * NY + y)

    def remember(*place):
        known[tuple(id(v) for v in place)] = device(*place)

    for k in range(NY):
        remember(x, h, ys_at[k], l, c)
        for ll in (*cross_l, source):
            remember(x, hs_at[1], ys_at[k], ll, c)
    for k in range(NX):
        for hh in hs_at:
            remember(xs_at[k], hh, y, l, c)
        for ll in (*cross_l, source):
            remember(xs_at[k], hs_at[1], y, ll, c)
    for hh in hs_at:
        for ll in ls_at:
            for cc in cs_at:
                remember(x, hh, y, ll, cc)
    xh = x * 2 + h
    z = h * 4 + l
    same = (h + c) % 2
    ends = (l % 3 + 1) // 2

    def copy(src, dst, slot, to, send_slot=None):
        return pltpu.make_async_remote_copy(
            src_ref=src, dst_ref=dst,
            send_sem=ssem.at[slot if send_slot is None else send_slot], recv_sem=rsem.at[slot],
            device_id=to, device_id_type=MESH,
        )

    sibling = device(x, h, y, l, cs_at[1])

    def arrived(dst, slot):
        copy(dst, dst, slot, sibling).wait_recv()

    def both(fn):
        pl.when(same == 0)(functools.partial(fn, True))
        pl.when(same == 1)(functools.partial(fn, False))

    barrier = pltpu.get_barrier_semaphore()
    peers = []
    for k in range(1, 16):
        peers.append(device(x, hs_at[k // 8], y, ls_at[(k // 2) % 4], cs_at[k % 2]))
    for k in range(1, NY):
        peers.append(device(x, h, ys_at[k], l, c))
    for dx in range(1, NX):
        peers.append(device(xs_at[dx], h, y, l, c))
    peers.append(device((x + 2 * h + 3) % NX, hs_at[1], y, l, c))
    loads = [
        pltpu.make_async_copy(src, dst, ssem.at[S_IN + k])
        for k, (src, dst) in enumerate(
            ((up_in, up), (down_in, down), (kt_in, kt), (gn_in, gn), (state_in, state), (cot_in, cot))
        )
    ]
    for each in loads:
        each.start()

    def greet(peer):
        pl.semaphore_signal(barrier, inc=1, device_id=peer, device_id_type=MESH)

    for peer in peers:
        greet(peer)
    for k in range(NX):
        greet(device(xs_at[k], hs_at[1], y, source, c))
    for each in loads[:2]:
        each.wait()

    def own_up(core, first):
        for e in range(2):
            low, high = (128 * (2 * (2 * e + bb) + core) for bb in range(2))
            w[y, x, first + e] = jnp.concatenate([up[:, low : low + 128], up[:, high : high + 128]], axis=0)

    def own_down():
        for rh in range(2):
            for q in range(2):
                w[y, x, 4 + 2 * rh + q] = down[8 * rh : 8 * rh + 8, 128 * q : 128 * q + 128]

    for core in range(2):
        for kind in range(2):

            def own(core=core, kind=kind):
                own_up(core, 2 if kind == 0 else 0)
                if kind == 0:
                    own_down()

            pl.when((c * 2 + same) == (core * 2 + kind))(own)

    for each in loads[2:4]:
        each.wait()
    sub8 = lax.broadcasted_iota(jnp.int32, (8, 128), 0)
    kg_row[...] = jnp.zeros_like(kg_row)
    for i in range(4):
        kg_row[i : i + 1, 0:9] = kt[i : i + 1, :]
        kg_row[i : i + 1, 9:10] = gn[0:1, i : i + 1]
    packed = kg_row[0:1, :]
    for i in range(1, 4):
        packed = packed + pltpu.roll(kg_row[i : i + 1, :], 32 * i, 1)
    kg_tile = jnp.where(sub8 == xh, jnp.broadcast_to(packed, (8, 128)), 0.0)
    kg_own[...] = kg_tile
    kg_xh[0] = kg_tile

    flips = [code[0, e].astype(F32) for e in range(4)]

    def mixed(flip, a, b):
        return a * (1.0 - flip) + b * flip

    loads[4].wait()
    for i in range(16):
        we_send[0, i : i + 1, :] = mixed(flips[2], state[i, 0:1, :], state[15 - i, 0:1, :])
        we_send[1, i : i + 1, :] = mixed(flips[3], state[i, 15:16, :], state[15 - i, 15:16, :])

    row, col = xh, y
    inner_n, inner_s = (row + 7) // 8, (14 - row) // 8
    inner_w, inner_e = (col + 7) // 8, (14 - col) // 8
    across = (
        (face + 4) % 8,
        7 - face,
        (face + 7 + 2 * (face % 2)) % 8,
        face + 1 - 2 * (face % 2),
    )

    def rim_copies(send, recv, base, stride, low_edge, high_edge, inner_low, inner_high):
        low_to = (
            inner_low * face + (1 - inner_low) * across[low_edge],
            tile - stride * inner_low,
        )
        high_to = (
            inner_high * face + (1 - inner_high) * across[high_edge],
            tile + stride * inner_high,
        )
        low = pltpu.make_async_remote_copy(
            src_ref=send.at[0], dst_ref=recv.at[inner_low], send_sem=ssem.at[base],
            recv_sem=rsem.at[base + inner_low], device_id=low_to, device_id_type=MESH,
        )
        high = pltpu.make_async_remote_copy(
            src_ref=send.at[1], dst_ref=recv.at[1 - inner_high], send_sem=ssem.at[base + 1],
            recv_sem=rsem.at[base + 1 - inner_high], device_id=high_to, device_id_type=MESH,
        )
        return low, high

    pl.semaphore_wait(barrier, len(peers) + (1 - ends) * 8)

    we = rim_copies(we_send, we_recv, S_HALO, 1, 2, 3, inner_w, inner_e)
    for each in we:
        each.start()

    def big(yy, xx):
        return w.at[yy, xx, 2:8]

    def small(yy, xx):
        return w.at[yy, xx, 0:2]

    def own_sends(whole):
        mine = big(y, x) if whole else small(y, x)
        if whole:
            return y_sends()
        return [copy(mine, mine, S_BX + k, device(xs_at[k], h, y, l, c)) for k in (1, 3, 2)]

    def cross_sends(whole):
        mine = big(y, x) if whole else small(y, x)
        sends = []
        for k in (0,) if whole else (0, 1, 3, 2):
            for m in range(2):
                sends.append(
                    copy(
                        mine, mine, S_Y if whole else S_BX + k, device(xs_at[k], hs_at[1], y, cross_l[m], c),
                        S_C + 2 * k + m,
                    )
                )
        return sends

    def y_sends():
        ref = big(y, x)
        return [copy(ref, ref, S_Y + k, device(x, h, ys_at[k], l, c)) for k in NEAR]

    def kg_cross():
        return [
            copy(kg_own, kg_xh.at[4 + k], S_KG1 + 4 + k, device(xs_at[k], hs_at[1], y, cross_l[m], c), S_CK + 2 * k + m)
            for k in (0, 1, 3, 2)
            for m in range(2)
        ]

    def x_sends(k):
        ref = big(ys_at[-k % NY], x)
        return [copy(ref, ref, S_X + 3 * k + dx - 1, device(xs_at[dx], h, y, l, c)) for dx in (2, 1, 3)]

    def forward(k, whole):
        if k:
            arrived(big(ys_at[-k % NY], x), S_Y + k)
        for each in x_sends(k):
            each.start()

    def small_sends():
        ref = w.at[y, :, 0:2]
        return [copy(ref, ref, S_BY + k, device(x, h, ys_at[k], l, c)) for k in (4, 3, 5, 2, 6, 1, 7)]

    def forward_small(whole):
        for k in range(NX):
            if k or whole:
                arrived(small(y, xs_at[-k % NX]), S_BX + k)
        for each in small_sends():
            each.start()

    def first_leg(whole):
        for each in own_sends(whole):
            each.start()

        @pl.when(ends == 0)
        def _():
            for each in cross_sends(whole):
                each.start()

        if whole:
            forward(0, whole)

    both(first_leg)
    kg1 = [copy(kg_own, kg_xh.at[k], S_KG1 + k, device(xs_at[k], h, y, l, c)) for k in range(1, NX)]
    for each in kg1:
        each.start()

    @pl.when(ends == 0)
    def _():
        for each in kg_cross():
            each.start()

    loads[5].wait()
    cot_copy = copy(cot, cot_sib, S_COT, sibling)
    cot_copy.start()

    def prepare(r, carry):
        rows = state[pl.ds(r * 4, 4)]
        at = pl.ds(1 + r * 4, 4)
        middle[at] = rows
        west[at] = pltpu.roll(rows, 1, 1)
        east[at] = pltpu.roll(rows, 15, 1)
        high, low = split(cot[pl.ds(r * 4, 4)].reshape(64, 256))
        to = pl.ds(pl.multiple_of(r * 64, 64), 64)
        g_hi[0, to, :] = high
        g_lo[0, to, :] = low
        return carry

    lax.fori_loop(0, 4, prepare, 0)

    def second_leg(whole):
        if whole:
            forward(1, whole)
            forward(7, whole)
        else:
            arrived(big(y, x), S_Y)
            for each in y_sends() + x_sends(0):
                each.start()

    both(second_leg)

    for k in range(2):
        arrived(we_recv.at[k], S_HALO + k)
    for i in range(16):
        west[1 + i, 0:1, :] = we_recv[0, i : i + 1, :]
        east[1 + i, 15:16, :] = we_recv[1, i : i + 1, :]
    for k, (edge, line) in enumerate(((0, 0), (1, 15))):
        first, last = we_recv[0, line : line + 1, :], we_recv[1, line : line + 1, :]
        ns_send[k, 0:1, :] = mixed(flips[edge], first, last)
        ns_send[k, 17:18, :] = mixed(flips[edge], last, first)
        for i in range(16):
            ns_send[k, 1 + i : 2 + i, :] = mixed(
                flips[edge], state[line, i : i + 1, :], state[line, 15 - i : 16 - i, :]
            )
    ns = rim_copies(ns_send, ns_recv, S_HALO + 2, 8, 0, 1, inner_n, inner_s)
    for each in ns:
        each.start()

    for k in range(1, 8):
        arrived(kg_xh.at[k], S_KG1 + k)
    total = kg_xh[0]
    for k in range(1, 8):
        total = total + kg_xh[k]
    kg_all[y] = total
    kg2 = []
    for k in range(1, NY):
        mine = kg_all.at[y]
        each = copy(mine, mine, S_KG2 + k, device(x, h, ys_at[k], l, c))
        each.start()
        kg2.append(each)

    def third_leg(whole):
        for k in (2, 6) if whole else ():
            forward(k, whole)
        forward_small(whole)

    both(third_leg)

    def fourth_leg(whole):
        for k in (3, 5, 4) if whole else NEAR:
            forward(k, whole)

    both(fourth_leg)

    for k in range(1, NY):
        arrived(kg_all.at[ys_at[-k % NY]], S_KG2 + k)
    rows64 = lax.broadcasted_iota(jnp.int32, (64, 256), 0)
    chan = lax.broadcasted_iota(jnp.int32, (64, 256), 1)
    owner = (chan // 4) == ((rows64 % 8) * 8 + rows64 // 8)
    lane = lax.broadcasted_iota(jnp.int32, (64, 128), 1)
    same4 = (
        lax.broadcasted_iota(jnp.int32, (128, 256), 0) // 32
        == lax.broadcasted_iota(jnp.int32, (128, 256), 1) % 4
    )
    spread4 = jnp.where(same4, 1.0, 0.0).astype(BF16)
    tiles = kg_all[...].reshape(64, 128)
    grouped = jnp.concatenate([jnp.where(lane % 32 == k, tiles, 0.0) for k in range(10)], axis=0)
    first, second = split(grouped)
    spread_rows = lax.dot_general(first, spread4, NN, preferred_element_type=F32) + lax.dot_general(
        second, spread4, NN, preferred_element_type=F32
    )
    for k in range(10):
        krows[k : k + 1, :] = jnp.sum(
            jnp.where(owner, spread_rows[64 * k : 64 * k + 64], 0.0), axis=0, keepdims=True
        )

    for k in range(2):
        arrived(ns_recv.at[k], S_HALO + 2 + k)
        line = 17 * k
        west[line] = ns_recv[k, 0:16, :]
        middle[line] = ns_recv[k, 1:17, :]
        east[line] = ns_recv[k, 2:18, :]

    shifted = (west, middle, east)
    taps = [krows[k : k + 1, :] for k in range(9)]
    gain = krows[9:10, :]

    def conv_rows(r, carry):
        acc = jnp.zeros((4, 16, 256), F32)
        for i in range(3):
            for j in range(3):
                acc = acc + krows[3 * i + j : 3 * i + j + 1, :] * shifted[j][pl.ds(r * 4 + i, 4)]
        acc = acc.reshape(64, 256)
        mean = jnp.mean(acc, axis=-1, keepdims=True)
        centred = acc - mean
        var = jnp.mean(centred * centred, axis=-1, keepdims=True)
        inv = lax.rsqrt(var + EPSILON)
        hat = centred * inv
        at = pl.ds(pl.multiple_of(r * 64, 64), 64)
        xhat[at, :] = hat
        rstd[at, :] = jnp.broadcast_to(inv, (64, 128))
        normed = hat * krows[9:10, :]
        norm_own[at, :] = normed
        high, low = split(normed)
        n_hi[0, at, :] = high
        n_lo[0, at, :] = low
        copy(norm_own.at[at], norm_sib.at[at], S_NORM + r, sibling).start()
        return carry

    lax.fori_loop(0, 4, conv_rows, 0)
    parts = [pl.ds(64 * r, 64) for r in range(4)]
    norm_copies = [copy(norm_own.at[at], norm_sib.at[at], S_NORM + r, sibling) for r, at in enumerate(parts)]

    for k in NEAR:
        arrived(w.at[ys_at[-k % NY], :, 0:2], S_BY + k)
    for k in (0, *NEAR):
        for dx in (1, 3, 2):
            arrived(big(ys_at[-k % NY], xs_at[-dx % NX]), S_X + 3 * k + dx - 1)

    lows = lax.broadcasted_iota(jnp.int32, (4, 8, 128), 1) < 4

    def unpack(xs, carry):
        for r in range(2):
            hs = r * c + (1 - r) * (1 - c)
            at = pl.ds(pl.multiple_of(xs * 64 + hs * 32, 32), 32)
            for e in range(2):
                v = w[:, xs, 2 * r + e].reshape(4, 2, 8, 128)
                a, b = v[:, 0], v[:, 1]
                for bb, value in (
                    (0, jnp.where(lows, a, pltpu.roll(b, 4, 1))),
                    (1, jnp.where(lows, pltpu.roll(a, 4, 1), b)),
                ):
                    high, low = split(value.reshape(32, 128))
                    u_hi[e, at, 128 * bb : 128 * bb + 128] = high
                    u_lo[e, at, 128 * bb : 128 * bb + 128] = low
        at = pl.ds(pl.multiple_of((xs % 2) * 128, 128), 128)
        for q in range(2):
            value = jnp.concatenate([w[:, xs, 4 + q], w[:, xs, 6 + q]], axis=1).reshape(128, 128)
            high, low = split(value)
            d_hi[xs // 2, at, 128 * q : 128 * q + 128] = high
            d_lo[xs // 2, at, 128 * q : 128 * q + 128] = low
        return carry

    lax.fori_loop(0, NX, unpack, 0)

    arrived(cot_sib, S_COT)

    def prepare_cot(r, carry):
        high, low = split(cot_sib[pl.ds(r * 4, 4)].reshape(64, 256))
        to = pl.ds(pl.multiple_of(r * 64, 64), 64)
        g_hi[1, to, :] = high
        g_lo[1, to, :] = low
        return carry

    lax.fori_loop(0, 4, prepare_cot, 0)
    def first_products(e, m):
        downs = (d_hi[e], d_lo[e])
        grads = (g_hi[m], g_lo[m])
        pre = dot3((n_hi[m], n_lo[m]), (u_hi[e], u_lo[e]), NN)
        back = dot3(grads, downs, NT)
        square = pre * pre
        t = jnp.tanh(ROOT * (pre + 0.044715 * (square * pre)))
        half = 0.5 * (1.0 + t)
        hidden = pre * half
        slope = half + 0.5 * pre * (1.0 - t * t) * (ROOT * (1.0 + 3 * 0.044715 * square))
        high, low = split(back * slope)
        p_hi[m, e] = high
        p_lo[m, e] = low
        high, low = split(hidden)
        h_hi[m, e] = high
        h_lo[m, e] = low
        value = dot3(split(jnp.transpose(hidden)), grads, NN)
        dgrad[...] = value if m == 0 else dgrad[...] + value

    def x_reduce(first, count, into, base):
        return [
            copy(
                g.at[pl.ds(4 * yh, 4), xs_at[dx], pl.ds(first, count)], into.at[dx - 1, pl.ds(4 * yh, 4)],
                base + 3 * yh + dx - 1, device(xs_at[dx], h, y, l, c),
            )
            for yh in range(2)
            for dx in (2, 1, 3)
        ]

    reduces = x_reduce(4, 4, x_recv, R_X)
    for e in range(2):
        first_products(e, 0)
        if e == 0:
            for r, at in enumerate(parts):
                arrived(norm_sib.at[at], S_NORM + r)
            for r in range(4):
                high, low = split(norm_sib[64 * r : 64 * r + 64, :])
                n_hi[1, 64 * r : 64 * r + 64, :] = high
                n_lo[1, 64 * r : 64 * r + 64, :] = low
        first_products(e, 1)
        for bb in range(2):
            for q in range(2):
                v = dgrad[128 * bb : 128 * bb + 128, 128 * q : 128 * q + 128].reshape(8, 2, 8, 128)
                for rh in range(2):
                    g[:, 2 * e + bb, 4 + 2 * rh + q] = v[:, rh]
        for k, dx in enumerate((2, 1, 3)):

            @pl.when(xs_at[dx] // 2 == e)
            def _(k=k):
                reduces[k].start()
                reduces[3 + k].start()

    for m, source_ref in enumerate((norm_own, norm_sib)):
        for r in range(2):
            high, low = split(jnp.transpose(source_ref[128 * r : 128 * r + 128, :]))
            nt_hi[m, r] = high
            nt_lo[m, r] = low

    def second_products(e, carry):
        ugrad[e] = sum(
            dot3((nt_hi[m, r], nt_lo[m, r]), (p_hi[m, e, 128 * r : 128 * r + 128], p_lo[m, e, 128 * r : 128 * r + 128]), NN)
            for m in range(2)
            for r in range(2)
        )
        return carry

    lax.fori_loop(0, 2, second_products, 0)

    def pack(xs, carry):
        for r in range(2):
            hs = r * c + (1 - r) * (1 - c)
            at = pl.ds(pl.multiple_of(xs * 64 + hs * 32, 32), 32)
            for e in range(2):
                v0 = ugrad[e, at, 0:128].reshape(4, 8, 128)
                v1 = ugrad[e, at, 128:256].reshape(4, 8, 128)
                even = jnp.where(lows, v0, pltpu.roll(v1, 4, 1))
                odd = jnp.where(lows, pltpu.roll(v0, 4, 1), v1)
                g[:, xs, 2 * r + e] = jnp.concatenate([even[:, None], odd[:, None]], axis=1).reshape(8, 8, 128)
        return carry

    lax.fori_loop(0, NX, pack, 0)
    for each in x_reduce(2, 2, xu_recv, R_XU):
        each.start()
        reduces.append(each)
    for k in (4, 3, 5, 2, 6, 1, 7):
        yy = ys_at[k]
        each = copy(g.at[yy, :, 0:2], by_recv.at[k], R_BY + k, device(x, h, yy, l, c))
        each.start()
        reduces.append(each)

    swaps = [copy(dnorm.at[1], dn_recv, R_BR, sibling), copy(branch.at[1], br_recv, R_BR + 1, sibling)]
    for m in (1, 0):
        dnorm[m] = sum(dot3((p_hi[m, e], p_lo[m, e]), (u_hi[e], u_lo[e]), NT) for e in range(2))
        if m:
            swaps[0].start()
    for m in (1, 0):
        branch[m] = sum(dot3((h_hi[m, e], h_lo[m, e]), (d_hi[e], d_lo[e]), NN) for e in range(2))
        if m:
            swaps[1].start()

    zpad[0:2] = jnp.zeros((2, 16, 256), F32)
    zpad[18:20] = jnp.zeros((2, 16, 256), F32)
    arrived(dn_recv, R_BR)

    def norm_rows(r, sums):
        at = pl.ds(pl.multiple_of(r * 32, 32), 32)
        hat = xhat[at, :]
        inv = rstd[at, :][:, 0:1]
        dn = dnorm[0, at, :] + dn_recv[at, :]
        dhat = dn * krows[9:10, :]
        mean = jnp.mean(dhat, axis=-1, keepdims=True)
        cross = jnp.mean(dhat * hat, axis=-1, keepdims=True)
        dd = (inv * (dhat - mean - hat * cross)).reshape(2, 16, 256)
        zpad[pl.ds(r * 2 + 2, 2)] = dd
        fresh = []
        for i in range(3):
            for j in range(3):
                v = (dd * shifted[j][pl.ds(r * 2 + i, 2)]).reshape(4, 8, 256)
                fresh.append(sums[3 * i + j] + ((v[0] + v[1]) + (v[2] + v[3])))
        v = (dn * hat).reshape(4, 8, 256)
        fresh.append(sums[9] + ((v[0] + v[1]) + (v[2] + v[3])))
        return tuple(fresh)

    sums = lax.fori_loop(0, 8, norm_rows, tuple(jnp.zeros((8, 256), F32) for _ in range(10)))

    lanes16 = lax.broadcasted_iota(jnp.int32, (2, 16, 256), 1)

    def back_rows(r, carry):
        parts = []
        for j in range(3):
            acc = jnp.zeros((2, 16, 256), F32)
            for i in range(3):
                acc = acc + krows[3 * i + j : 3 * i + j + 1, :] * zpad[pl.ds(r * 2 + 2 - i, 2)]
            parts.append(acc)
        to = pl.ds(r * 2, 2)
        left = jnp.where(lanes16 < 15, pltpu.roll(parts[0], 15, 1), 0.0)
        right = jnp.where(lanes16 > 0, pltpu.roll(parts[2], 1, 1), 0.0)
        centre[to] = parts[1] + (left + right)
        wcol[to] = parts[0][:, 0:1, :]
        ecol[to] = parts[2][:, 15:16, :]
        return carry

    lax.fori_loop(0, 9, back_rows, 0)
    for k, (edge, line) in enumerate(((0, 0), (1, 17))):
        first, last = wcol[line], ecol[line]
        bns_send[k, 0:1, :] = mixed(flips[edge], first, last)
        bns_send[k, 17:18, :] = mixed(flips[edge], last, first)
        for i in range(16):
            bns_send[k, 1 + i : 2 + i, :] = mixed(
                flips[edge], centre[line, i : i + 1, :], centre[line, 15 - i : 16 - i, :]
            )
    bns = rim_copies(bns_send, bns_recv, R_HALO, 8, 0, 1, inner_n, inner_s)
    for each in bns:
        each.start()

    grad_rows = [jnp.sum(sums[k], axis=0, keepdims=True) for k in range(10)]
    grouped = jnp.concatenate([jnp.where(owner, jnp.broadcast_to(v, (64, 256)), 0.0) for v in grad_rows], axis=0)
    first, second = split(grouped)
    fold = lax.dot_general(first, spread4, NT, preferred_element_type=F32) + lax.dot_general(
        second, spread4, NT, preferred_element_type=F32
    )
    folded = jnp.zeros((64, 128), F32)
    for k in range(10):
        folded = folded + jnp.where(lane % 32 == k, fold[64 * k : 64 * k + 64], 0.0)
    kgr_own[...] = folded.reshape(8, 8, 128)
    kgs = []
    for k in range(1, NY):
        yy = ys_at[k]
        each = copy(kgr_own.at[yy], kgr_y.at[k], R_KY + k, device(x, h, yy, l, c))
        each.start()
        kgs.append(each)

    def early_sent(whole):
        for each in own_sends(whole) + ([] if whole else y_sends()):
            each.wait_send()

        @pl.when(ends == 0)
        def _():
            for each in cross_sends(whole) + kg_cross():
                each.wait_send()

    both(early_sent)
    for k in range(NY):
        for each in x_sends(k):
            each.wait_send()
    for each in [*small_sends(), *we, *kg1, *ns, *kg2, cot_copy, *norm_copies]:
        each.wait_send()

    for yh in range(2):
        half = pl.ds(4 * yh, 4)
        for dx in (1, 3, 2):
            arrived(x_recv.at[dx - 1, half], R_X + 3 * yh + dx - 1)
            arrived(xu_recv.at[dx - 1, half], R_XU + 3 * yh + dx - 1)
        g[half, x, 4:8] = (g[half, x, 4:8] + x_recv[0, half]) + (x_recv[1, half] + x_recv[2, half])
        g[half, x, 2:4] = (g[half, x, 2:4] + xu_recv[0, half]) + (xu_recv[1, half] + xu_recv[2, half])
        for k in range(1, NY):
            yy = ys_at[k]

            @pl.when(yy // 4 == yh)
            def _(k=k, yy=yy):
                copy(g.at[yy, x, 2:8], y_recv.at[k], R_Y + k, device(x, h, yy, l, c)).start()

    for k in range(1, NY):
        reduces.append(copy(g.at[ys_at[k], x, 2:8], y_recv.at[k], R_Y + k, device(x, h, ys_at[k], l, c)))

    for k in range(1, NY):
        arrived(by_recv.at[k], R_BY + k)
    total = g[y, :, 0:2]
    for k in range(1, NY):
        total = total + by_recv[k]
    g[y, :, 0:2] = total
    for dx in (2, 1, 3):
        to = xs_at[dx]
        each = copy(g.at[y, to, 0:2], bx_recv.at[dx], R_BX + dx, device(to, h, y, l, c))
        each.start()
        reduces.append(each)

    arrived(br_recv, R_BR + 1)

    def new_rows(r, carry):
        at = pl.ds(pl.multiple_of(r * 64, 64), 64)
        value = branch[0, at, :] + br_recv[at, :]
        to = pl.ds(r * 4, 4)
        out_new[to] = state[to] + value.reshape(4, 16, 256)
        return carry

    lax.fori_loop(0, 4, new_rows, 0)
    stores = [pltpu.make_async_copy(out_new, new_out, rsem.at[S_OUT])]
    stores[0].start()

    for k, line in enumerate((1, 16)):
        arrived(bns_recv.at[k], R_HALO + k)
        wcol[line] = wcol[line] + bns_recv[k, 0:1, :]
        centre[line] = centre[line] + bns_recv[k, 1:17, :]
        ecol[line] = ecol[line] + bns_recv[k, 17:18, :]
    for i in range(16):
        bwe_send[0, i : i + 1, :] = mixed(flips[2], wcol[1 + i], wcol[16 - i])
        bwe_send[1, i : i + 1, :] = mixed(flips[3], ecol[1 + i], ecol[16 - i])
    bwe = rim_copies(bwe_send, bwe_recv, R_HALO + 2, 1, 2, 3, inner_w, inner_e)
    for each in bwe:
        each.start()

    for k in range(1, NY):
        arrived(kgr_y.at[k], R_KY + k)
    total = kgr_own[y]
    for k in range(1, NY):
        total = total + kgr_y[k]
    kgr_x[x] = total
    for k in range(1, NX):
        each = copy(kgr_x.at[x], kgr_x.at[x], R_KX + k, device(xs_at[k], h, y, l, c))
        each.start()
        kgs.append(each)

    for k in range(1, NY):
        arrived(y_recv.at[k], R_Y + k)
    total = g[y, x, 2:8]
    for k in range(1, NY):
        total = total + y_recv[k]
    z_recv[z, 2:8] = total
    for dx in range(1, NX):
        arrived(bx_recv.at[dx], R_BX + dx)
    z_recv[z, 0:2] = (g[y, x, 0:2] + bx_recv[1]) + (bx_recv[2] + bx_recv[3])

    def z_sends(whole):
        sends = []
        for k in range(1, 8):
            dh, dl = k // 4, k % 4
            full = whole if dh == 0 else not whole
            ref = z_recv.at[z, 2:8] if full else z_recv.at[z, 0:2]
            sends.append(copy(ref, ref, R_Z + k, device(x, hs_at[dh], y, ls_at[dl], c)))
        return sends

    def z_start(whole):
        for each in z_sends(whole):
            each.start()

    both(z_start)

    for k in range(1, NX):
        arrived(kgr_x.at[xs_at[-k % NX]], R_KX + k)
    total = kgr_x[0]
    for k in range(1, NX):
        total = total + kgr_x[k]
    zc = z * 2 + c
    kgr_z[zc] = total
    for k in range(1, 16):
        to = device(x, hs_at[k // 8], y, ls_at[(k // 2) % 4], cs_at[k % 2])
        each = copy(kgr_z.at[zc], kgr_z.at[zc], R_KZ + k, to)
        each.start()
        kgs.append(each)

    for k in range(2):
        arrived(bwe_recv.at[k], R_HALO + 2 + k)
    for i in range(16):
        centre[1 + i, 0:1, :] = centre[1 + i, 0:1, :] + bwe_recv[0, i : i + 1, :]
        centre[1 + i, 15:16, :] = centre[1 + i, 15:16, :] + bwe_recv[1, i : i + 1, :]
        out_field[i] = centre[1 + i] + cot[i]
    stores.append(pltpu.make_async_copy(out_field, field_out, rsem.at[S_OUT + 1]))
    stores[1].start()

    for each in [*swaps, *reduces, *bns]:
        each.wait_send()

    def fin_sends(whole):
        sends = [copy(fin_up.at[c], fin_up.at[c], R_F, sibling)]
        if whole:
            sends.append(copy(fin_down, fin_down, R_F + 1, sibling))
        return sends

    def z_end(whole):
        for k in range(1, 8):
            zz = (hs_at[k // 4]) * 4 + ls_at[-(k % 4) % NL]
            arrived(z_recv.at[zz, 2:8] if whole else z_recv.at[zz, 0:2], R_Z + k)
        span = slice(2, 8) if whole else slice(0, 2)
        total = z_recv[0, span]
        for zz in range(1, 8):
            total = total + z_recv[zz, span]
        fin_up[c] = total[0:2]
        if whole:
            fin_down[...] = total[2:6]
        for each in fin_sends(whole):
            each.start()
        arrived(fin_up.at[1 - c], R_F)
        if not whole:
            arrived(fin_down, R_F + 1)

    both(z_end)
    for cc in range(2):
        for e in range(2):
            v = fin_up[cc, e]
            for bb in range(2):
                first = 128 * (2 * (2 * e + bb) + cc)
                out_up[:, first : first + 128] = v[4 * bb : 4 * bb + 4]
    for rh in range(2):
        for q in range(2):
            out_down[8 * rh : 8 * rh + 8, 128 * q : 128 * q + 128] = fin_down[2 * rh + q]
    stores.append(pltpu.make_async_copy(out_up, up_out, rsem.at[S_OUT + 2]))
    stores.append(pltpu.make_async_copy(out_down, down_out, rsem.at[S_OUT + 3]))
    stores[2].start()
    stores[3].start()

    for k in range(1, 16):
        hh, ll, cc = hs_at[k // 8], ls_at[-(k // 2) % 4], cs_at[k % 2]
        arrived(kgr_z.at[(hh * 4 + ll) * 2 + cc], R_KZ + k)
    total = kgr_z[0]
    for k in range(1, 16):
        total = total + kgr_z[k]
    out_kg[...] = jnp.sum(jnp.where(sub8 == xh, total, 0.0), axis=0, keepdims=True)
    stores.append(pltpu.make_async_copy(out_kg, kg_out, rsem.at[S_OUT + 4]))
    stores[4].start()

    def last_sent(whole):
        for each in z_sends(whole) + fin_sends(whole):
            each.wait_send()

    both(last_sent)
    for each in [*kgs, *bwe]:
        each.wait_send()
    for each in stores:
        each.wait()


def results(
    new, field, up, down, kg, out_new, out_field, out_up, out_down, out_kt, out_gn,
    v_new, v_field, v_up, v_down, v_kg, v_kt, v_gn, sem,
):
    quarters = [(n, slice(4 * k, 4 * k + 4)) for n in range(2) for k in range(4)]
    ins = [(kg, v_kg)] + [((new, field)[n].at[at], (v_new, v_field)[n].at[at]) for n, at in quarters]
    outs = [((v_new, v_field)[n].at[at], (out_new, out_field)[n].at[at]) for n, at in quarters]
    ins += [(up, v_up), (down, v_down)]
    outs += [(v_up, out_up), (v_down, out_down), (v_kt, out_kt), (v_gn, out_gn)]
    reads = [pltpu.make_async_copy(src, dst, sem.at[k]) for k, (src, dst) in enumerate(ins)]
    writes = [pltpu.make_async_copy(src, dst, sem.at[len(ins) + k]) for k, (src, dst) in enumerate(outs)]
    for each in reads:
        each.start()
    reads[0].wait()
    for i in range(4):
        moved = v_kg[...] if i == 0 else pltpu.roll(v_kg[...], 128 - 32 * i, 1)
        v_kt[i : i + 1, :] = moved[:, 0:9]
        v_gn[0:1, i : i + 1] = moved[:, 9:10]
    writes[10].start()
    writes[11].start()
    for k in range(10):
        reads[1 + k].wait()
        writes[k].start()
    for each in writes:
        each.wait()


def shards(state_field, out_grad, depth_kernel, norm_gain, up_weight, down_weight, seam_code):
    anywhere = pl.BlockSpec(memory_space=pl.ANY)

    def buf(*shape, dtype=F32):
        return pltpu.VMEM(shape, dtype)

    def half(*shape):
        return pltpu.VMEM(shape, BF16)

    found = pl.pallas_call(
        kernel,
        out_shape=(
            jax.ShapeDtypeStruct((16, 16, 256), F32),
            jax.ShapeDtypeStruct((16, 16, 256), F32),
            jax.ShapeDtypeStruct((4, 1024), F32),
            jax.ShapeDtypeStruct((16, 256), F32),
            jax.ShapeDtypeStruct((1, 128), F32),
        ),
        in_specs=[anywhere] * 6 + [pl.BlockSpec(memory_space=pltpu.SMEM)],
        out_specs=(anywhere,) * 5,
        scratch_shapes=[
            buf(16, 16, 256), buf(16, 16, 256), buf(4, 1024), buf(16, 256), buf(4, 9), buf(1, 4),
            buf(16, 16, 256), buf(16, 16, 256), buf(4, 1024), buf(16, 256), buf(1, 128),
            buf(8, 4, 8, 8, 128), buf(8, 4, 8, 8, 128),
            buf(18, 16, 256), buf(18, 16, 256), buf(18, 16, 256),
            buf(20, 16, 256), buf(18, 16, 256), buf(18, 1, 256), buf(18, 1, 256),
            buf(2, 18, 256), buf(2, 18, 256), buf(2, 16, 256), buf(2, 16, 256),
            buf(2, 18, 256), buf(2, 18, 256), buf(2, 16, 256), buf(2, 16, 256),
            buf(8, 128), buf(8, 128), buf(8, 8, 128), buf(8, 8, 128),
            buf(8, 8, 128), buf(8, 8, 128), buf(4, 8, 128), buf(16, 8, 128),
            half(2, 256, 256), half(2, 256, 256), half(2, 256, 256), half(2, 256, 256),
            buf(256, 256), buf(256, 128), buf(256, 256), buf(256, 256), buf(16, 16, 256),
            half(2, 256, 256), half(2, 256, 256), half(2, 2, 256, 128), half(2, 2, 256, 128),
            half(2, 256, 256), half(2, 256, 256),
            half(2, 2, 256, 256), half(2, 2, 256, 256), half(2, 2, 256, 256), half(2, 2, 256, 256),
            buf(2, 256, 256), buf(2, 256, 256), buf(256, 256), buf(256, 256),
            buf(2, 256, 256), buf(256, 256), buf(16, 256),
            buf(3, 8, 4, 8, 128), buf(3, 8, 2, 8, 128), buf(8, 6, 8, 128),
            buf(8, 4, 2, 8, 128), buf(4, 2, 8, 128), buf(8, 8, 8, 128),
            buf(2, 2, 8, 128), buf(4, 8, 128),
            pltpu.SemaphoreType.DMA((N_SLOTS,)),
            pltpu.SemaphoreType.DMA((N_SLOTS,)),
        ],
        compiler_params=pltpu.CompilerParams(
            collective_id=0, has_side_effects=True, vmem_limit_bytes=60 * 1024 * 1024
        ),
        name="block",
    )(
        state_field[0, 0], out_grad[0, 0], up_weight, down_weight,
        depth_kernel.T, norm_gain.reshape(1, 4), seam_code[0],
    )
    new, field, up, down, kt, gn = pl.pallas_call(
        results,
        out_shape=(
            jax.ShapeDtypeStruct((16, 16, 256), F32),
            jax.ShapeDtypeStruct((16, 16, 256), F32),
            jax.ShapeDtypeStruct((4, 1024), F32),
            jax.ShapeDtypeStruct((16, 256), F32),
            jax.ShapeDtypeStruct((4, 9), F32),
            jax.ShapeDtypeStruct((1, 4), F32),
        ),
        in_specs=[anywhere] * 5,
        out_specs=(anywhere,) * 6,
        scratch_shapes=[
            buf(16, 16, 256), buf(16, 16, 256), buf(4, 1024), buf(16, 256), buf(1, 128), buf(4, 9), buf(1, 4),
            pltpu.SemaphoreType.DMA((23,)),
        ],
        compiler_params=pltpu.CompilerParams(vmem_limit_bytes=60 * 1024 * 1024),
        name="results",
    )(*found)
    return (new[None, None], field[None, None], kt.T, gn.reshape(4), up, down)


def solution(mesh):
    placed = (
        P("face", "tile", None, None, None),
        P("face", "tile", None, None, None),
        P(None, "tile"),
        P("tile"),
        P("tile", None),
        P("tile", None),
        P("face", "tile", None),
    )
    return jax.shard_map(
        shards,
        mesh=mesh,
        in_specs=placed,
        out_specs=(
            P("face", "tile", None, None, None),
            P("face", "tile", None, None, None),
            P(None, "tile"),
            P("tile"),
            P("tile", None),
            P("tile", None),
        ),
        check_vma=False,
    )
```

```python
import functools
import math

import jax
import jax.numpy as jnp
from jax import lax
from jax.experimental import pallas as pl
from jax.experimental.pallas import tpu as pltpu
from jax.sharding import PartitionSpec as P

EPSILON = 1e-06
NX, NH, NY, NL, NC = 4, 2, 8, 4, 2
MESH = pl.DeviceIdType.MESH
F32, BF16 = jnp.float32, jnp.bfloat16
ROOT = math.sqrt(2.0 / math.pi)
NN = (((1,), (0,)), ((), ()))
NT = (((1,), (1,)), ((), ()))


class Slots:
    def __init__(self):
        self.used = 0

    def take(self, count):
        first = self.used
        self.used += count
        return first


SLOTS = Slots()
S_Y = SLOTS.take(8)
S_C = SLOTS.take(8)
S_CK = SLOTS.take(8)
S_X = SLOTS.take(24)
S_BX = SLOTS.take(8)
S_BY = SLOTS.take(8)
S_IN = SLOTS.take(6)
S_OUT = SLOTS.take(5)
S_COT = SLOTS.take(1)
S_NORM = SLOTS.take(4)
S_KG1 = SLOTS.take(8)
S_KG2 = SLOTS.take(8)
S_HALO = SLOTS.take(4)
R_X = SLOTS.take(6)
R_XU = SLOTS.take(6)
R_BY = SLOTS.take(8)
R_BX = SLOTS.take(4)
R_Y = SLOTS.take(8)
R_Z = SLOTS.take(8)
R_F = SLOTS.take(2)
R_BR = SLOTS.take(2)
R_KY = SLOTS.take(8)
R_KX = SLOTS.take(4)
R_KZ = SLOTS.take(16)
R_HALO = SLOTS.take(4)
N_SLOTS = SLOTS.used

NEAR = (1, 7, 2, 6, 3, 5, 4)


def split(value):
    high = value.astype(BF16)
    return high, (value - high.astype(F32)).astype(BF16)


def dot3(a, b, dims):
    def one(p, q):
        return lax.dot_general(p, q, dims, preferred_element_type=F32)

    return one(a[0], b[0]) + (one(a[0], b[1]) + one(a[1], b[0]))


def kernel(
    state_in, cot_in, up_in, down_in, kt_in, gn_in, code,
    new_out, field_out, up_out, down_out, kg_out,
    state, cot, up, down, kt, gn, out_new, out_field, out_up, out_down, out_kg,
    w, g, west, middle, east, zpad, centre, wcol, ecol,
    ns_send, ns_recv, we_send, we_recv, bns_send, bns_recv, bwe_send, bwe_recv,
    kg_row, kg_own, kg_xh, kg_all, kgr_own, kgr_y, kgr_x, kgr_z,
    u_hi, u_lo, d_hi, d_lo, xhat, rstd, norm_own, norm_sib, cot_sib,
    n_hi, n_lo, nt_hi, nt_lo, g_hi, g_lo, h_hi, h_lo, p_hi, p_lo, branch, dnorm, br_recv, dn_recv, ugrad, dgrad, krows,
    x_recv, xu_recv, y_recv, by_recv, bx_recv, z_recv, fin_up, fin_down,
    ssem, rsem,
):
    face, tile = lax.axis_index("face"), lax.axis_index("tile")
    l, c = face // 2, face % 2
    x, h, y = tile // 16, (tile // 8) % 2, tile % 8
    xs_at = [x] + [(x + k) % NX for k in range(1, NX)]
    ys_at = [y] + [(y + k) % NY for k in range(1, NY)]
    hs_at = [h, 1 - h]
    ls_at = [l] + [(l + k) % NL for k in range(1, NL)]
    cs_at = [c, 1 - c]
    cross_l = [(3 - m) * (1 - l // 3) + m * (l // 3) for m in range(2)]
    source = 3 * (1 - l // 2)
    known = {}

    def device(x, h, y, l, c):
        key = (id(x), id(h), id(y), id(l), id(c))
        return known[key] if key in known else (l * NC + c, (x * NH + h) * NY + y)

    def remember(*place):
        known[tuple(id(v) for v in place)] = device(*place)

    for k in range(NY):
        remember(x, h, ys_at[k], l, c)
        for ll in (*cross_l, source):
            remember(x, hs_at[1], ys_at[k], ll, c)
    for k in range(NX):
        for hh in hs_at:
            remember(xs_at[k], hh, y, l, c)
        for ll in (*cross_l, source):
            remember(xs_at[k], hs_at[1], y, ll, c)
    for hh in hs_at:
        for ll in ls_at:
            for cc in cs_at:
                remember(x, hh, y, ll, cc)
    xh = x * 2 + h
    z = h * 4 + l
    same = (h + c) % 2
    ends = (l % 3 + 1) // 2

    def copy(src, dst, slot, to, send_slot=None):
        return pltpu.make_async_remote_copy(
            src_ref=src, dst_ref=dst,
            send_sem=ssem.at[slot if send_slot is None else send_slot], recv_sem=rsem.at[slot],
            device_id=to, device_id_type=MESH,
        )

    sibling = device(x, h, y, l, cs_at[1])

    def arrived(dst, slot):
        copy(dst, dst, slot, sibling).wait_recv()

    def both(fn):
        pl.when(same == 0)(functools.partial(fn, True))
        pl.when(same == 1)(functools.partial(fn, False))

    barrier = pltpu.get_barrier_semaphore()
    peers = []
    for k in range(1, 16):
        peers.append(device(x, hs_at[k // 8], y, ls_at[(k // 2) % 4], cs_at[k % 2]))
    for k in range(1, NY):
        peers.append(device(x, h, ys_at[k], l, c))
    for dx in range(1, NX):
        peers.append(device(xs_at[dx], h, y, l, c))
    peers.append(device((x + 2 * h + 3) % NX, hs_at[1], y, l, c))
    loads = [
        pltpu.make_async_copy(src, dst, ssem.at[S_IN + k])
        for k, (src, dst) in enumerate(
            ((up_in, up), (down_in, down), (kt_in, kt), (gn_in, gn), (state_in, state), (cot_in, cot))
        )
    ]
    for each in loads:
        each.start()

    def greet(peer):
        pl.semaphore_signal(barrier, inc=1, device_id=peer, device_id_type=MESH)

    for peer in peers:
        greet(peer)
    for k in range(NX):
        greet(device(xs_at[k], hs_at[1], y, source, c))
    for each in loads[:2]:
        each.wait()

    def own_up(core, first):
        for e in range(2):
            low, high = (128 * (2 * (2 * e + bb) + core) for bb in range(2))
            w[y, x, first + e] = jnp.concatenate([up[:, low : low + 128], up[:, high : high + 128]], axis=0)

    def own_down():
        for rh in range(2):
            for q in range(2):
                w[y, x, 4 + 2 * rh + q] = down[8 * rh : 8 * rh + 8, 128 * q : 128 * q + 128]

    for core in range(2):
        for kind in range(2):

            def own(core=core, kind=kind):
                own_up(core, 2 if kind == 0 else 0)
                if kind == 0:
                    own_down()

            pl.when((c * 2 + same) == (core * 2 + kind))(own)

    for each in loads[2:4]:
        each.wait()
    sub8 = lax.broadcasted_iota(jnp.int32, (8, 128), 0)
    kg_row[...] = jnp.zeros_like(kg_row)
    for i in range(4):
        kg_row[i : i + 1, 0:9] = kt[i : i + 1, :]
        kg_row[i : i + 1, 9:10] = gn[0:1, i : i + 1]
    packed = kg_row[0:1, :]
    for i in range(1, 4):
        packed = packed + pltpu.roll(kg_row[i : i + 1, :], 32 * i, 1)
    kg_tile = jnp.where(sub8 == xh, jnp.broadcast_to(packed, (8, 128)), 0.0)
    kg_own[...] = kg_tile
    kg_xh[0] = kg_tile

    flips = [code[0, e].astype(F32) for e in range(4)]

    def mixed(flip, a, b):
        return a * (1.0 - flip) + b * flip

    loads[4].wait()
    for i in range(16):
        we_send[0, i : i + 1, :] = mixed(flips[2], state[i, 0:1, :], state[15 - i, 0:1, :])
        we_send[1, i : i + 1, :] = mixed(flips[3], state[i, 15:16, :], state[15 - i, 15:16, :])

    row, col = xh, y
    inner_n, inner_s = (row + 7) // 8, (14 - row) // 8
    inner_w, inner_e = (col + 7) // 8, (14 - col) // 8
    across = (
        (face + 4) % 8,
        7 - face,
        (face + 7 + 2 * (face % 2)) % 8,
        face + 1 - 2 * (face % 2),
    )

    def rim_copies(send, recv, base, stride, low_edge, high_edge, inner_low, inner_high):
        low_to = (
            inner_low * face + (1 - inner_low) * across[low_edge],
            tile - stride * inner_low,
        )
        high_to = (
            inner_high * face + (1 - inner_high) * across[high_edge],
            tile + stride * inner_high,
        )
        low = pltpu.make_async_remote_copy(
            src_ref=send.at[0], dst_ref=recv.at[inner_low], send_sem=ssem.at[base],
            recv_sem=rsem.at[base + inner_low], device_id=low_to, device_id_type=MESH,
        )
        high = pltpu.make_async_remote_copy(
            src_ref=send.at[1], dst_ref=recv.at[1 - inner_high], send_sem=ssem.at[base + 1],
            recv_sem=rsem.at[base + 1 - inner_high], device_id=high_to, device_id_type=MESH,
        )
        return low, high

    pl.semaphore_wait(barrier, len(peers) + (1 - ends) * 8)

    we = rim_copies(we_send, we_recv, S_HALO, 1, 2, 3, inner_w, inner_e)
    for each in we:
        each.start()

    def big(yy, xx):
        return w.at[yy, xx, 2:8]

    def small(yy, xx):
        return w.at[yy, xx, 0:2]

    def own_sends(whole):
        mine = big(y, x) if whole else small(y, x)
        if whole:
            return y_sends()
        return [copy(mine, mine, S_BX + k, device(xs_at[k], h, y, l, c)) for k in (1, 3, 2)]

    def cross_sends(whole):
        mine = big(y, x) if whole else small(y, x)
        sends = []
        for k in (0,) if whole else (0, 1, 3, 2):
            for m in range(2):
                sends.append(
                    copy(
                        mine, mine, S_Y if whole else S_BX + k, device(xs_at[k], hs_at[1], y, cross_l[m], c),
                        S_C + 2 * k + m,
                    )
                )
        return sends

    def y_sends():
        ref = big(y, x)
        return [copy(ref, ref, S_Y + k, device(x, h, ys_at[k], l, c)) for k in NEAR]

    def kg_cross():
        return [
            copy(kg_own, kg_xh.at[4 + k], S_KG1 + 4 + k, device(xs_at[k], hs_at[1], y, cross_l[m], c), S_CK + 2 * k + m)
            for k in (0, 1, 3, 2)
            for m in range(2)
        ]

    def x_sends(k):
        ref = big(ys_at[-k % NY], x)
        return [copy(ref, ref, S_X + 3 * k + dx - 1, device(xs_at[dx], h, y, l, c)) for dx in (2, 1, 3)]

    def forward(k, whole):
        if k:
            arrived(big(ys_at[-k % NY], x), S_Y + k)
        for each in x_sends(k):
            each.start()

    def small_sends():
        ref = w.at[y, :, 0:2]
        return [copy(ref, ref, S_BY + k, device(x, h, ys_at[k], l, c)) for k in (4, 3, 5, 2, 6, 1, 7)]

    def forward_small(whole):
        for k in range(NX):
            if k or whole:
                arrived(small(y, xs_at[-k % NX]), S_BX + k)
        for each in small_sends():
            each.start()

    def first_leg(whole):
        for each in own_sends(whole):
            each.start()

        @pl.when(ends == 0)
        def _():
            for each in cross_sends(whole):
                each.start()

        if whole:
            forward(0, whole)

    both(first_leg)
    kg1 = [copy(kg_own, kg_xh.at[k], S_KG1 + k, device(xs_at[k], h, y, l, c)) for k in range(1, NX)]
    for each in kg1:
        each.start()

    @pl.when(ends == 0)
    def _():
        for each in kg_cross():
            each.start()

    loads[5].wait()
    cot_copy = copy(cot, cot_sib, S_COT, sibling)
    cot_copy.start()

    def prepare(r, carry):
        rows = state[pl.ds(r * 4, 4)]
        at = pl.ds(1 + r * 4, 4)
        middle[at] = rows
        west[at] = pltpu.roll(rows, 1, 1)
        east[at] = pltpu.roll(rows, 15, 1)
        high, low = split(cot[pl.ds(r * 4, 4)].reshape(64, 256))
        to = pl.ds(pl.multiple_of(r * 64, 64), 64)
        g_hi[0, to, :] = high
        g_lo[0, to, :] = low
        return carry

    lax.fori_loop(0, 4, prepare, 0)

    def second_leg(whole):
        if whole:
            forward(1, whole)
            forward(7, whole)
        else:
            arrived(big(y, x), S_Y)
            for each in y_sends() + x_sends(0):
                each.start()

    both(second_leg)

    for k in range(2):
        arrived(we_recv.at[k], S_HALO + k)
    for i in range(16):
        west[1 + i, 0:1, :] = we_recv[0, i : i + 1, :]
        east[1 + i, 15:16, :] = we_recv[1, i : i + 1, :]
    for k, (edge, line) in enumerate(((0, 0), (1, 15))):
        first, last = we_recv[0, line : line + 1, :], we_recv[1, line : line + 1, :]
        ns_send[k, 0:1, :] = mixed(flips[edge], first, last)
        ns_send[k, 17:18, :] = mixed(flips[edge], last, first)
        for i in range(16):
            ns_send[k, 1 + i : 2 + i, :] = mixed(
                flips[edge], state[line, i : i + 1, :], state[line, 15 - i : 16 - i, :]
            )
    ns = rim_copies(ns_send, ns_recv, S_HALO + 2, 8, 0, 1, inner_n, inner_s)
    for each in ns:
        each.start()

    for k in range(1, 8):
        arrived(kg_xh.at[k], S_KG1 + k)
    total = kg_xh[0]
    for k in range(1, 8):
        total = total + kg_xh[k]
    kg_all[y] = total
    kg2 = []
    for k in range(1, NY):
        mine = kg_all.at[y]
        each = copy(mine, mine, S_KG2 + k, device(x, h, ys_at[k], l, c))
        each.start()
        kg2.append(each)

    def third_leg(whole):
        for k in (2, 6) if whole else ():
            forward(k, whole)
        forward_small(whole)

    both(third_leg)

    def fourth_leg(whole):
        for k in (3, 5, 4) if whole else NEAR:
            forward(k, whole)

    both(fourth_leg)

    for k in range(1, NY):
        arrived(kg_all.at[ys_at[-k % NY]], S_KG2 + k)
    rows64 = lax.broadcasted_iota(jnp.int32, (64, 256), 0)
    chan = lax.broadcasted_iota(jnp.int32, (64, 256), 1)
    owner = (chan // 4) == ((rows64 % 8) * 8 + rows64 // 8)
    lane = lax.broadcasted_iota(jnp.int32, (64, 128), 1)
    same4 = (
        lax.broadcasted_iota(jnp.int32, (128, 256), 0) // 32
        == lax.broadcasted_iota(jnp.int32, (128, 256), 1) % 4
    )
    spread4 = jnp.where(same4, 1.0, 0.0).astype(BF16)
    tiles = kg_all[...].reshape(64, 128)
    grouped = jnp.concatenate([jnp.where(lane % 32 == k, tiles, 0.0) for k in range(10)], axis=0)
    first, second = split(grouped)
    spread_rows = lax.dot_general(first, spread4, NN, preferred_element_type=F32) + lax.dot_general(
        second, spread4, NN, preferred_element_type=F32
    )
    for k in range(10):
        krows[k : k + 1, :] = jnp.sum(
            jnp.where(owner, spread_rows[64 * k : 64 * k + 64], 0.0), axis=0, keepdims=True
        )

    for k in range(2):
        arrived(ns_recv.at[k], S_HALO + 2 + k)
        line = 17 * k
        west[line] = ns_recv[k, 0:16, :]
        middle[line] = ns_recv[k, 1:17, :]
        east[line] = ns_recv[k, 2:18, :]

    shifted = (west, middle, east)
    taps = [krows[k : k + 1, :] for k in range(9)]
    gain = krows[9:10, :]

    def conv_rows(r, carry):
        acc = jnp.zeros((4, 16, 256), F32)
        for i in range(3):
            for j in range(3):
                acc = acc + krows[3 * i + j : 3 * i + j + 1, :] * shifted[j][pl.ds(r * 4 + i, 4)]
        acc = acc.reshape(64, 256)
        mean = jnp.mean(acc, axis=-1, keepdims=True)
        centred = acc - mean
        var = jnp.mean(centred * centred, axis=-1, keepdims=True)
        inv = lax.rsqrt(var + EPSILON)
        hat = centred * inv
        at = pl.ds(pl.multiple_of(r * 64, 64), 64)
        xhat[at, :] = hat
        rstd[at, :] = jnp.broadcast_to(inv, (64, 128))
        normed = hat * krows[9:10, :]
        norm_own[at, :] = normed
        high, low = split(normed)
        n_hi[0, at, :] = high
        n_lo[0, at, :] = low
        copy(norm_own.at[at], norm_sib.at[at], S_NORM + r, sibling).start()
        return carry

    lax.fori_loop(0, 4, conv_rows, 0)
    parts = [pl.ds(64 * r, 64) for r in range(4)]
    norm_copies = [copy(norm_own.at[at], norm_sib.at[at], S_NORM + r, sibling) for r, at in enumerate(parts)]

    for k in NEAR:
        arrived(w.at[ys_at[-k % NY], :, 0:2], S_BY + k)
    for k in (0, *NEAR):
        for dx in (1, 3, 2):
            arrived(big(ys_at[-k % NY], xs_at[-dx % NX]), S_X + 3 * k + dx - 1)

    lows = lax.broadcasted_iota(jnp.int32, (4, 8, 128), 1) < 4

    def unpack(xs, carry):
        for r in range(2):
            hs = r * c + (1 - r) * (1 - c)
            at = pl.ds(pl.multiple_of(xs * 64 + hs * 32, 32), 32)
            for e in range(2):
                v = w[:, xs, 2 * r + e].reshape(4, 2, 8, 128)
                a, b = v[:, 0], v[:, 1]
                for bb, value in (
                    (0, jnp.where(lows, a, pltpu.roll(b, 4, 1))),
                    (1, jnp.where(lows, pltpu.roll(a, 4, 1), b)),
                ):
                    high, low = split(value.reshape(32, 128))
                    u_hi[e, at, 128 * bb : 128 * bb + 128] = high
                    u_lo[e, at, 128 * bb : 128 * bb + 128] = low
        at = pl.ds(pl.multiple_of((xs % 2) * 128, 128), 128)
        for q in range(2):
            value = jnp.concatenate([w[:, xs, 4 + q], w[:, xs, 6 + q]], axis=1).reshape(128, 128)
            high, low = split(value)
            d_hi[xs // 2, at, 128 * q : 128 * q + 128] = high
            d_lo[xs // 2, at, 128 * q : 128 * q + 128] = low
        return carry

    lax.fori_loop(0, NX, unpack, 0)

    arrived(cot_sib, S_COT)

    def prepare_cot(r, carry):
        high, low = split(cot_sib[pl.ds(r * 4, 4)].reshape(64, 256))
        to = pl.ds(pl.multiple_of(r * 64, 64), 64)
        g_hi[1, to, :] = high
        g_lo[1, to, :] = low
        return carry

    lax.fori_loop(0, 4, prepare_cot, 0)
    def first_products(e, m):
        downs = (d_hi[e], d_lo[e])
        grads = (g_hi[m], g_lo[m])
        pre = dot3((n_hi[m], n_lo[m]), (u_hi[e], u_lo[e]), NN)
        back = dot3(grads, downs, NT)
        square = pre * pre
        t = jnp.tanh(ROOT * (pre + 0.044715 * (square * pre)))
        half = 0.5 * (1.0 + t)
        hidden = pre * half
        slope = half + 0.5 * pre * (1.0 - t * t) * (ROOT * (1.0 + 3 * 0.044715 * square))
        high, low = split(back * slope)
        p_hi[m, e] = high
        p_lo[m, e] = low
        high, low = split(hidden)
        h_hi[m, e] = high
        h_lo[m, e] = low
        value = dot3(split(jnp.transpose(hidden)), grads, NN)
        dgrad[...] = value if m == 0 else dgrad[...] + value

    def x_reduce(first, count, into, base):
        return [
            copy(
                g.at[pl.ds(4 * yh, 4), xs_at[dx], pl.ds(first, count)], into.at[dx - 1, pl.ds(4 * yh, 4)],
                base + 3 * yh + dx - 1, device(xs_at[dx], h, y, l, c),
            )
            for yh in range(2)
            for dx in (2, 1, 3)
        ]

    reduces = x_reduce(4, 4, x_recv, R_X)
    for e in range(2):
        first_products(e, 0)
        if e == 0:
            for r, at in enumerate(parts):
                arrived(norm_sib.at[at], S_NORM + r)
            for r in range(4):
                high, low = split(norm_sib[64 * r : 64 * r + 64, :])
                n_hi[1, 64 * r : 64 * r + 64, :] = high
                n_lo[1, 64 * r : 64 * r + 64, :] = low
        first_products(e, 1)
        for bb in range(2):
            for q in range(2):
                v = dgrad[128 * bb : 128 * bb + 128, 128 * q : 128 * q + 128].reshape(8, 2, 8, 128)
                for rh in range(2):
                    g[:, 2 * e + bb, 4 + 2 * rh + q] = v[:, rh]
        for k, dx in enumerate((2, 1, 3)):

            @pl.when(xs_at[dx] // 2 == e)
            def _(k=k):
                reduces[k].start()
                reduces[3 + k].start()

    for m, source_ref in enumerate((norm_own, norm_sib)):
        for r in range(2):
            high, low = split(jnp.transpose(source_ref[128 * r : 128 * r + 128, :]))
            nt_hi[m, r] = high
            nt_lo[m, r] = low

    def second_products(e, carry):
        ugrad[e] = sum(
            dot3((nt_hi[m, r], nt_lo[m, r]), (p_hi[m, e, 128 * r : 128 * r + 128], p_lo[m, e, 128 * r : 128 * r + 128]), NN)
            for m in range(2)
            for r in range(2)
        )
        return carry

    lax.fori_loop(0, 2, second_products, 0)

    def pack(xs, carry):
        for r in range(2):
            hs = r * c + (1 - r) * (1 - c)
            at = pl.ds(pl.multiple_of(xs * 64 + hs * 32, 32), 32)
            for e in range(2):
                v0 = ugrad[e, at, 0:128].reshape(4, 8, 128)
                v1 = ugrad[e, at, 128:256].reshape(4, 8, 128)
                even = jnp.where(lows, v0, pltpu.roll(v1, 4, 1))
                odd = jnp.where(lows, pltpu.roll(v0, 4, 1), v1)
                g[:, xs, 2 * r + e] = jnp.concatenate([even[:, None], odd[:, None]], axis=1).reshape(8, 8, 128)
        return carry

    lax.fori_loop(0, NX, pack, 0)
    for each in x_reduce(2, 2, xu_recv, R_XU):
        each.start()
        reduces.append(each)
    for k in (4, 3, 5, 2, 6, 1, 7):
        yy = ys_at[k]
        each = copy(g.at[yy, :, 0:2], by_recv.at[k], R_BY + k, device(x, h, yy, l, c))
        each.start()
        reduces.append(each)

    swaps = [copy(dnorm.at[1], dn_recv, R_BR, sibling), copy(branch.at[1], br_recv, R_BR + 1, sibling)]
    for m in (1, 0):
        dnorm[m] = sum(dot3((p_hi[m, e], p_lo[m, e]), (u_hi[e], u_lo[e]), NT) for e in range(2))
        if m:
            swaps[0].start()
    for m in (1, 0):
        branch[m] = sum(dot3((h_hi[m, e], h_lo[m, e]), (d_hi[e], d_lo[e]), NN) for e in range(2))
        if m:
            swaps[1].start()

    zpad[0:2] = jnp.zeros((2, 16, 256), F32)
    zpad[18:20] = jnp.zeros((2, 16, 256), F32)
    arrived(dn_recv, R_BR)

    def norm_rows(r, sums):
        at = pl.ds(pl.multiple_of(r * 32, 32), 32)
        hat = xhat[at, :]
        inv = rstd[at, :][:, 0:1]
        dn = dnorm[0, at, :] + dn_recv[at, :]
        dhat = dn * krows[9:10, :]
        mean = jnp.mean(dhat, axis=-1, keepdims=True)
        cross = jnp.mean(dhat * hat, axis=-1, keepdims=True)
        dd = (inv * (dhat - mean - hat * cross)).reshape(2, 16, 256)
        zpad[pl.ds(r * 2 + 2, 2)] = dd
        fresh = []
        for i in range(3):
            for j in range(3):
                v = (dd * shifted[j][pl.ds(r * 2 + i, 2)]).reshape(4, 8, 256)
                fresh.append(sums[3 * i + j] + ((v[0] + v[1]) + (v[2] + v[3])))
        v = (dn * hat).reshape(4, 8, 256)
        fresh.append(sums[9] + ((v[0] + v[1]) + (v[2] + v[3])))
        return tuple(fresh)

    sums = lax.fori_loop(0, 8, norm_rows, tuple(jnp.zeros((8, 256), F32) for _ in range(10)))

    lanes16 = lax.broadcasted_iota(jnp.int32, (2, 16, 256), 1)

    def back_rows(r, carry):
        parts = []
        for j in range(3):
            acc = jnp.zeros((2, 16, 256), F32)
            for i in range(3):
                acc = acc + krows[3 * i + j : 3 * i + j + 1, :] * zpad[pl.ds(r * 2 + 2 - i, 2)]
            parts.append(acc)
        to = pl.ds(r * 2, 2)
        left = jnp.where(lanes16 < 15, pltpu.roll(parts[0], 15, 1), 0.0)
        right = jnp.where(lanes16 > 0, pltpu.roll(parts[2], 1, 1), 0.0)
        centre[to] = parts[1] + (left + right)
        wcol[to] = parts[0][:, 0:1, :]
        ecol[to] = parts[2][:, 15:16, :]
        return carry

    lax.fori_loop(0, 9, back_rows, 0)
    for k, (edge, line) in enumerate(((0, 0), (1, 17))):
        first, last = wcol[line], ecol[line]
        bns_send[k, 0:1, :] = mixed(flips[edge], first, last)
        bns_send[k, 17:18, :] = mixed(flips[edge], last, first)
        for i in range(16):
            bns_send[k, 1 + i : 2 + i, :] = mixed(
                flips[edge], centre[line, i : i + 1, :], centre[line, 15 - i : 16 - i, :]
            )
    bns = rim_copies(bns_send, bns_recv, R_HALO, 8, 0, 1, inner_n, inner_s)
    for each in bns:
        each.start()

    grad_rows = [jnp.sum(sums[k], axis=0, keepdims=True) for k in range(10)]
    grouped = jnp.concatenate([jnp.where(owner, jnp.broadcast_to(v, (64, 256)), 0.0) for v in grad_rows], axis=0)
    first, second = split(grouped)
    fold = lax.dot_general(first, spread4, NT, preferred_element_type=F32) + lax.dot_general(
        second, spread4, NT, preferred_element_type=F32
    )
    folded = jnp.zeros((64, 128), F32)
    for k in range(10):
        folded = folded + jnp.where(lane % 32 == k, fold[64 * k : 64 * k + 64], 0.0)
    kgr_own[...] = folded.reshape(8, 8, 128)
    kgs = []
    for k in range(1, NY):
        yy = ys_at[k]
        each = copy(kgr_own.at[yy], kgr_y.at[k], R_KY + k, device(x, h, yy, l, c))
        each.start()
        kgs.append(each)

    for yh in range(2):
        half = pl.ds(4 * yh, 4)
        for dx in (1, 3, 2):
            arrived(x_recv.at[dx - 1, half], R_X + 3 * yh + dx - 1)
            arrived(xu_recv.at[dx - 1, half], R_XU + 3 * yh + dx - 1)
        g[half, x, 4:8] = (g[half, x, 4:8] + x_recv[0, half]) + (x_recv[1, half] + x_recv[2, half])
        g[half, x, 2:4] = (g[half, x, 2:4] + xu_recv[0, half]) + (xu_recv[1, half] + xu_recv[2, half])
        for k in range(1, NY):
            yy = ys_at[k]

            @pl.when(yy // 4 == yh)
            def _(k=k, yy=yy):
                copy(g.at[yy, x, 2:8], y_recv.at[k], R_Y + k, device(x, h, yy, l, c)).start()

    for k in range(1, NY):
        reduces.append(copy(g.at[ys_at[k], x, 2:8], y_recv.at[k], R_Y + k, device(x, h, ys_at[k], l, c)))

    for k in range(1, NY):
        arrived(by_recv.at[k], R_BY + k)
    total = g[y, :, 0:2]
    for k in range(1, NY):
        total = total + by_recv[k]
    g[y, :, 0:2] = total
    for dx in (2, 1, 3):
        to = xs_at[dx]
        each = copy(g.at[y, to, 0:2], bx_recv.at[dx], R_BX + dx, device(to, h, y, l, c))
        each.start()
        reduces.append(each)

    arrived(br_recv, R_BR + 1)

    def new_rows(r, carry):
        at = pl.ds(pl.multiple_of(r * 64, 64), 64)
        value = branch[0, at, :] + br_recv[at, :]
        to = pl.ds(r * 4, 4)
        out_new[to] = state[to] + value.reshape(4, 16, 256)
        return carry

    lax.fori_loop(0, 4, new_rows, 0)
    stores = [pltpu.make_async_copy(out_new, new_out, rsem.at[S_OUT])]
    stores[0].start()

    for k, line in enumerate((1, 16)):
        arrived(bns_recv.at[k], R_HALO + k)
        wcol[line] = wcol[line] + bns_recv[k, 0:1, :]
        centre[line] = centre[line] + bns_recv[k, 1:17, :]
        ecol[line] = ecol[line] + bns_recv[k, 17:18, :]
    for i in range(16):
        bwe_send[0, i : i + 1, :] = mixed(flips[2], wcol[1 + i], wcol[16 - i])
        bwe_send[1, i : i + 1, :] = mixed(flips[3], ecol[1 + i], ecol[16 - i])
    bwe = rim_copies(bwe_send, bwe_recv, R_HALO + 2, 1, 2, 3, inner_w, inner_e)
    for each in bwe:
        each.start()

    for k in range(1, NY):
        arrived(kgr_y.at[k], R_KY + k)
    total = kgr_own[y]
    for k in range(1, NY):
        total = total + kgr_y[k]
    kgr_x[x] = total
    for k in range(1, NX):
        each = copy(kgr_x.at[x], kgr_x.at[x], R_KX + k, device(xs_at[k], h, y, l, c))
        each.start()
        kgs.append(each)

    def early_sent(whole):
        for each in own_sends(whole) + ([] if whole else y_sends()):
            each.wait_send()

        @pl.when(ends == 0)
        def _():
            for each in cross_sends(whole) + kg_cross():
                each.wait_send()

    both(early_sent)
    for k in range(NY):
        for each in x_sends(k):
            each.wait_send()
    for each in [*small_sends(), *we, *kg1, *ns, *kg2, cot_copy, *norm_copies]:
        each.wait_send()

    for k in range(1, NY):
        arrived(y_recv.at[k], R_Y + k)
    total = g[y, x, 2:8]
    for k in range(1, NY):
        total = total + y_recv[k]
    z_recv[z, 2:8] = total
    for dx in range(1, NX):
        arrived(bx_recv.at[dx], R_BX + dx)
    z_recv[z, 0:2] = (g[y, x, 0:2] + bx_recv[1]) + (bx_recv[2] + bx_recv[3])

    def z_sends(whole):
        sends = []
        for k in range(1, 8):
            dh, dl = k // 4, k % 4
            full = whole if dh == 0 else not whole
            ref = z_recv.at[z, 2:8] if full else z_recv.at[z, 0:2]
            sends.append(copy(ref, ref, R_Z + k, device(x, hs_at[dh], y, ls_at[dl], c)))
        return sends

    def z_start(whole):
        for each in z_sends(whole):
            each.start()

    both(z_start)

    for k in range(1, NX):
        arrived(kgr_x.at[xs_at[-k % NX]], R_KX + k)
    total = kgr_x[0]
    for k in range(1, NX):
        total = total + kgr_x[k]
    zc = z * 2 + c
    kgr_z[zc] = total
    for k in range(1, 16):
        to = device(x, hs_at[k // 8], y, ls_at[(k // 2) % 4], cs_at[k % 2])
        each = copy(kgr_z.at[zc], kgr_z.at[zc], R_KZ + k, to)
        each.start()
        kgs.append(each)

    for k in range(2):
        arrived(bwe_recv.at[k], R_HALO + 2 + k)
    for i in range(16):
        centre[1 + i, 0:1, :] = centre[1 + i, 0:1, :] + bwe_recv[0, i : i + 1, :]
        centre[1 + i, 15:16, :] = centre[1 + i, 15:16, :] + bwe_recv[1, i : i + 1, :]
        out_field[i] = centre[1 + i] + cot[i]
    stores.append(pltpu.make_async_copy(out_field, field_out, rsem.at[S_OUT + 1]))
    stores[1].start()

    for each in [*swaps, *reduces, *bns]:
        each.wait_send()

    def fin_sends(whole):
        sends = [copy(fin_up.at[c], fin_up.at[c], R_F, sibling)]
        if whole:
            sends.append(copy(fin_down, fin_down, R_F + 1, sibling))
        return sends

    def z_end(whole):
        for k in range(1, 8):
            zz = (hs_at[k // 4]) * 4 + ls_at[-(k % 4) % NL]
            arrived(z_recv.at[zz, 2:8] if whole else z_recv.at[zz, 0:2], R_Z + k)
        span = slice(2, 8) if whole else slice(0, 2)
        total = z_recv[0, span]
        for zz in range(1, 8):
            total = total + z_recv[zz, span]
        fin_up[c] = total[0:2]
        if whole:
            fin_down[...] = total[2:6]
        for each in fin_sends(whole):
            each.start()
        arrived(fin_up.at[1 - c], R_F)
        if not whole:
            arrived(fin_down, R_F + 1)

    both(z_end)
    for cc in range(2):
        for e in range(2):
            v = fin_up[cc, e]
            for bb in range(2):
                first = 128 * (2 * (2 * e + bb) + cc)
                out_up[:, first : first + 128] = v[4 * bb : 4 * bb + 4]
    for rh in range(2):
        for q in range(2):
            out_down[8 * rh : 8 * rh + 8, 128 * q : 128 * q + 128] = fin_down[2 * rh + q]
    stores.append(pltpu.make_async_copy(out_up, up_out, rsem.at[S_OUT + 2]))
    stores.append(pltpu.make_async_copy(out_down, down_out, rsem.at[S_OUT + 3]))
    stores[2].start()
    stores[3].start()

    for k in range(1, 16):
        hh, ll, cc = hs_at[k // 8], ls_at[-(k // 2) % 4], cs_at[k % 2]
        arrived(kgr_z.at[(hh * 4 + ll) * 2 + cc], R_KZ + k)
    total = kgr_z[0]
    for k in range(1, 16):
        total = total + kgr_z[k]
    out_kg[...] = jnp.sum(jnp.where(sub8 == xh, total, 0.0), axis=0, keepdims=True)
    stores.append(pltpu.make_async_copy(out_kg, kg_out, rsem.at[S_OUT + 4]))
    stores[4].start()

    def last_sent(whole):
        for each in z_sends(whole) + fin_sends(whole):
            each.wait_send()

    both(last_sent)
    for each in [*kgs, *bwe]:
        each.wait_send()
    for each in stores:
        each.wait()


def results(
    new, field, up, down, kg, out_new, out_field, out_up, out_down, out_kt, out_gn,
    v_new, v_field, v_up, v_down, v_kg, v_kt, v_gn, sem,
):
    quarters = [(n, slice(4 * k, 4 * k + 4)) for n in range(2) for k in range(4)]
    ins = [(kg, v_kg)] + [((new, field)[n].at[at], (v_new, v_field)[n].at[at]) for n, at in quarters]
    outs = [((v_new, v_field)[n].at[at], (out_new, out_field)[n].at[at]) for n, at in quarters]
    ins += [(up, v_up), (down, v_down)]
    outs += [(v_up, out_up), (v_down, out_down), (v_kt, out_kt), (v_gn, out_gn)]
    reads = [pltpu.make_async_copy(src, dst, sem.at[k]) for k, (src, dst) in enumerate(ins)]
    writes = [pltpu.make_async_copy(src, dst, sem.at[len(ins) + k]) for k, (src, dst) in enumerate(outs)]
    for each in reads:
        each.start()
    reads[0].wait()
    for i in range(4):
        moved = v_kg[...] if i == 0 else pltpu.roll(v_kg[...], 128 - 32 * i, 1)
        v_kt[i : i + 1, :] = moved[:, 0:9]
        v_gn[0:1, i : i + 1] = moved[:, 9:10]
    writes[10].start()
    writes[11].start()
    for k in range(10):
        reads[1 + k].wait()
        writes[k].start()
    for each in writes:
        each.wait()


def shards(state_field, out_grad, depth_kernel, norm_gain, up_weight, down_weight, seam_code):
    anywhere = pl.BlockSpec(memory_space=pl.ANY)

    def buf(*shape, dtype=F32):
        return pltpu.VMEM(shape, dtype)

    def half(*shape):
        return pltpu.VMEM(shape, BF16)

    found = pl.pallas_call(
        kernel,
        out_shape=(
            jax.ShapeDtypeStruct((16, 16, 256), F32),
            jax.ShapeDtypeStruct((16, 16, 256), F32),
            jax.ShapeDtypeStruct((4, 1024), F32),
            jax.ShapeDtypeStruct((16, 256), F32),
            jax.ShapeDtypeStruct((1, 128), F32),
        ),
        in_specs=[anywhere] * 6 + [pl.BlockSpec(memory_space=pltpu.SMEM)],
        out_specs=(anywhere,) * 5,
        scratch_shapes=[
            buf(16, 16, 256), buf(16, 16, 256), buf(4, 1024), buf(16, 256), buf(4, 9), buf(1, 4),
            buf(16, 16, 256), buf(16, 16, 256), buf(4, 1024), buf(16, 256), buf(1, 128),
            buf(8, 4, 8, 8, 128), buf(8, 4, 8, 8, 128),
            buf(18, 16, 256), buf(18, 16, 256), buf(18, 16, 256),
            buf(20, 16, 256), buf(18, 16, 256), buf(18, 1, 256), buf(18, 1, 256),
            buf(2, 18, 256), buf(2, 18, 256), buf(2, 16, 256), buf(2, 16, 256),
            buf(2, 18, 256), buf(2, 18, 256), buf(2, 16, 256), buf(2, 16, 256),
            buf(8, 128), buf(8, 128), buf(8, 8, 128), buf(8, 8, 128),
            buf(8, 8, 128), buf(8, 8, 128), buf(4, 8, 128), buf(16, 8, 128),
            half(2, 256, 256), half(2, 256, 256), half(2, 256, 256), half(2, 256, 256),
            buf(256, 256), buf(256, 128), buf(256, 256), buf(256, 256), buf(16, 16, 256),
            half(2, 256, 256), half(2, 256, 256), half(2, 2, 256, 128), half(2, 2, 256, 128),
            half(2, 256, 256), half(2, 256, 256),
            half(2, 2, 256, 256), half(2, 2, 256, 256), half(2, 2, 256, 256), half(2, 2, 256, 256),
            buf(2, 256, 256), buf(2, 256, 256), buf(256, 256), buf(256, 256),
            buf(2, 256, 256), buf(256, 256), buf(16, 256),
            buf(3, 8, 4, 8, 128), buf(3, 8, 2, 8, 128), buf(8, 6, 8, 128),
            buf(8, 4, 2, 8, 128), buf(4, 2, 8, 128), buf(8, 8, 8, 128),
            buf(2, 2, 8, 128), buf(4, 8, 128),
            pltpu.SemaphoreType.DMA((N_SLOTS,)),
            pltpu.SemaphoreType.DMA((N_SLOTS,)),
        ],
        compiler_params=pltpu.CompilerParams(
            collective_id=0, has_side_effects=True, vmem_limit_bytes=60 * 1024 * 1024
        ),
        name="block",
    )(
        state_field[0, 0], out_grad[0, 0], up_weight, down_weight,
        depth_kernel.T, norm_gain.reshape(1, 4), seam_code[0],
    )
    new, field, up, down, kt, gn = pl.pallas_call(
        results,
        out_shape=(
            jax.ShapeDtypeStruct((16, 16, 256), F32),
            jax.ShapeDtypeStruct((16, 16, 256), F32),
            jax.ShapeDtypeStruct((4, 1024), F32),
            jax.ShapeDtypeStruct((16, 256), F32),
            jax.ShapeDtypeStruct((4, 9), F32),
            jax.ShapeDtypeStruct((1, 4), F32),
        ),
        in_specs=[anywhere] * 5,
        out_specs=(anywhere,) * 6,
        scratch_shapes=[
            buf(16, 16, 256), buf(16, 16, 256), buf(4, 1024), buf(16, 256), buf(1, 128), buf(4, 9), buf(1, 4),
            pltpu.SemaphoreType.DMA((23,)),
        ],
        compiler_params=pltpu.CompilerParams(vmem_limit_bytes=60 * 1024 * 1024),
        name="results",
    )(*found)
    return (new[None, None], field[None, None], kt.T, gn.reshape(4), up, down)


def solution(mesh):
    placed = (
        P("face", "tile", None, None, None),
        P("face", "tile", None, None, None),
        P(None, "tile"),
        P("tile"),
        P("tile", None),
        P("tile", None),
        P("face", "tile", None),
    )
    return jax.shard_map(
        shards,
        mesh=mesh,
        in_specs=placed,
        out_specs=(
            P("face", "tile", None, None, None),
            P("face", "tile", None, None, None),
            P(None, "tile"),
            P("tile"),
            P("tile", None),
            P("tile", None),
        ),
        check_vma=False,
    )
```
